32 devices in a mesh: ctx: 16 (over z, y, x), tp: 2 (over core).
Axes of the slice: x: 2, y: 2, z: 4, core: 2. Of those that a mesh axis runs over, the one named last changes fastest.
Arguments:
- hidden: bfloat16 [4096, 4096], P('ctx', 'tp'), may hold values from -6 to 6
- w_query: bfloat16 [4096, 4096], P('ctx', 'tp'), may hold values from -0.09375 to 0.09375
- key_weight: bfloat16 [4096, 256], P('ctx', 'tp'), may hold values from -0.09375 to 0.09375
- value_weight: bfloat16 [4096, 256], P('ctx', 'tp'), may hold values from -0.09375 to 0.09375
- q_gain: float32 [128], replicated, may hold values from 0.5 to 2
- key_norm_gain: float32 [128], replicated, may hold values from 0.5 to 2
- earlier_keys: bfloat16 [16384, 256], P('ctx', 'tp'), may hold values from -288 to 288
- earlier_values: bfloat16 [16384, 256], P('ctx', 'tp'), may hold values from -6 to 6
- counts: int32 [8], replicated, may hold values from 1 to 16, as said below
- place: int32 [8, 16], replicated, may hold values from 0 to 15, as said below
Outputs:
- attended: bfloat16 [4096, 4096], P('ctx', 'tp')
- new_keys: bfloat16 [4096, 256], P('ctx', 'tp')
- new_values: bfloat16 [4096, 256], P('ctx', 'tp')
The draws below stay inside these ranges and needn't reach their ends.
Inputs may be any that keep to these rules, and one draw needn't show every extreme that they name: `counts`: 16 for one trajectory and 1 for another in every draw; most trajectories have few blocks. `place`: each row orders all 16 slots of the trajectory; the slots after the first counts[b] hold stale data.
All inputs are finite; a program needn't handle non-finite values.
Results may differ from the reference program's by a relative error of at most 0.007.
Values may be sent and summed in bfloat16 or wider, within the bound.
No kernel may reach another device: no remote copies, remote signals or barrier semaphores. Data moves between devices by JAX's collectives and lax.ppermute only.
A program may use at most 64 MiB of HBM per device.

```python
import math
import jax
import jax.numpy as jnp
from jax import lax

MODEL_WIDTH = 4096
QUERY_HEADS = 32
KEY_VALUE_HEADS = 2
HEAD_SIZE = 128
BLOCK_TOKENS = 128
BLOCK_SLOTS = 8
NEW_PER_PATH = 512
TRAJ = 8
NEW_TOKEN_TOTAL = 4096
MAXB = 16
N_CTX = 16


def draw_earlier_keys(key, part):
    leading_index = jax.random.fold_in(key, 0)
    start_offset = jnp.clip(jax.random.normal(leading_index, (N_CTX * BLOCK_SLOTS * BLOCK_TOKENS, KEY_VALUE_HEADS * HEAD_SIZE), jnp.float32), -6.0, 6.0)
    return start_offset.astype(jnp.bfloat16)


def draw_counts(key, part):
    leading_index, second, third = jax.random.split(jax.random.fold_in(key, 11), 3)
    early = jax.random.randint(leading_index, (TRAJ,), 1, MAXB + 1)
    later = jax.random.randint(second, (TRAJ,), 1, MAXB + 1)
    blocks = jnp.minimum(early, later)
    order = jax.random.permutation(third, TRAJ)
    blocks = blocks.at[order[0]].set(MAXB)
    blocks = blocks.at[order[1]].set(1)
    return blocks.astype(jnp.int32)


def draw_place(key, part):
    streams = jax.random.split(jax.random.fold_in(key, 23), TRAJ)
    return jax.vmap(lambda stream: jax.random.permutation(stream, MAXB))(streams).astype(jnp.int32)


def shard_levels(own_key, shape, cuts, low, high):
    loudness, own = 1.0, jax.random.fold_in(own_key, 6)
    for dim, shards_of in cuts:
        steps = jnp.exp(jax.random.uniform(jax.random.fold_in(own, dim), (shards_of,), jnp.float32, low / len(cuts), high / len(cuts)))
        loudness = loudness * jnp.repeat(steps, shape[dim] // shards_of).reshape([-1 if axis == dim else 1 for axis in range(len(shape))])
    return loudness


def scatter_about(stream_key, extent, scale, limit, shards=(), kind=jnp.bfloat16):
    entries = jax.random.normal(stream_key, extent, jnp.float32) * scale
    if len(shards) > 0:
        entries = shard_levels(stream_key, extent, shards, -0.22, 0.18) * entries
    return jnp.clip(entries, min=-limit, max=limit).astype(kind)


def setup_inputs(seed: int = 0) -> dict:
    splits = jax.random.split(jax.random.key(seed), 11)
    hidden = scatter_about(splits[0], (NEW_TOKEN_TOTAL, MODEL_WIDTH), 1.0, 6.0, ((0, 16), (1, 2)))
    w_query = scatter_about(splits[1], (MODEL_WIDTH, QUERY_HEADS * HEAD_SIZE), MODEL_WIDTH ** -0.5, 0.09375, ((0, 16), (1, 2)))
    key_weight = scatter_about(splits[2], (MODEL_WIDTH, KEY_VALUE_HEADS * HEAD_SIZE), MODEL_WIDTH ** -0.5, 0.09375, ((0, 16), (1, 2)))
    value_weight = scatter_about(splits[3], (MODEL_WIDTH, KEY_VALUE_HEADS * HEAD_SIZE), MODEL_WIDTH ** -0.5, 0.09375, ((0, 16), (1, 2)))
    q_gain = jnp.clip(jnp.exp(jax.random.uniform(splits[4], (HEAD_SIZE,), jnp.float32, math.log(0.5), math.log(2.0))), 0.5, 2.0)
    key_norm_gain = jnp.clip(jnp.exp(jax.random.uniform(splits[5], (HEAD_SIZE,), jnp.float32, math.log(0.5), math.log(2.0))), 0.5, 2.0)
    earlier_keys = draw_earlier_keys(jax.random.fold_in(splits[10], 71), 0)
    earlier_values = scatter_about(splits[7], (N_CTX * BLOCK_SLOTS * BLOCK_TOKENS, KEY_VALUE_HEADS * HEAD_SIZE), 1.0, 6.0, ((0, 16), (1, 2)))
    counts = draw_counts(jax.random.fold_in(splits[10], 71), 0)
    place = draw_place(jax.random.fold_in(splits[10], 71), 0)
    return {"hidden": hidden, "w_query": w_query, "key_weight": key_weight, "value_weight": value_weight, "q_gain": q_gain, "key_norm_gain": key_norm_gain, "earlier_keys": earlier_keys, "earlier_values": earlier_values, "counts": counts, "place": place}


def normalize_and_turn(values, gain, token_position):
    width = values.shape[-1]
    half = width // 2
    scaled = values * lax.rsqrt(lax.optimization_barrier(jnp.mean(values * values, axis=-1, keepdims=True)) + 1e-06) * gain
    freq = jnp.exp(jnp.arange(half, dtype=jnp.float32) * (-2.0 / width) * math.log(1000000.0))
    angle = token_position.astype(jnp.float32)[:, None] * freq[None, :]
    cosine = jnp.cos(angle)[:, None, :]
    sine = jnp.sin(angle)[:, None, :]
    leading_index = scaled[..., :half]
    second = scaled[..., half:]
    return jnp.concatenate([leading_index * cosine - second * sine, second * cosine + leading_index * sine], axis=-1)

def reference(hidden, w_query, key_weight, value_weight, q_gain, key_norm_gain, earlier_keys, earlier_values, counts, place):
    query = jnp.dot(hidden, w_query, preferred_element_type=jnp.float32)
    key_projected = jnp.dot(hidden, key_weight, preferred_element_type=jnp.float32)
    value_projected = jnp.dot(hidden, value_weight, preferred_element_type=jnp.float32)
    row_ids = jnp.arange(NEW_TOKEN_TOTAL, dtype=jnp.int32)
    token_position = counts[row_ids // NEW_PER_PATH] * BLOCK_TOKENS + row_ids % NEW_PER_PATH
    rotated = normalize_and_turn(query.reshape(NEW_TOKEN_TOTAL, QUERY_HEADS, HEAD_SIZE), q_gain, token_position).astype(jnp.bfloat16)
    fresh_keys = normalize_and_turn(key_projected.reshape(NEW_TOKEN_TOTAL, KEY_VALUE_HEADS, HEAD_SIZE), key_norm_gain, token_position).astype(jnp.bfloat16)
    fresh_values = value_projected.astype(jnp.bfloat16).reshape(NEW_TOKEN_TOTAL, KEY_VALUE_HEADS, HEAD_SIZE)
    query_group = QUERY_HEADS // KEY_VALUE_HEADS
    token_extent = MAXB * BLOCK_TOKENS

    def one_traj(index):
        start = (index * NEW_PER_PATH).astype(jnp.int32)
        query_slice = lax.dynamic_slice_in_dim(rotated, start, NEW_PER_PATH, 0).astype(jnp.float32)
        key_part = lax.dynamic_slice_in_dim(fresh_keys, start, NEW_PER_PATH, 0)
        value_part = lax.dynamic_slice_in_dim(fresh_values, start, NEW_PER_PATH, 0)
        start_offset = (index * token_extent).astype(jnp.int32)
        gathered_keys = lax.dynamic_slice_in_dim(earlier_keys, start_offset, token_extent, 0).reshape(token_extent, KEY_VALUE_HEADS, HEAD_SIZE)
        gathered_values = lax.dynamic_slice_in_dim(earlier_values, start_offset, token_extent, 0).reshape(token_extent, KEY_VALUE_HEADS, HEAD_SIZE)
        order = place[index]
        used = jnp.arange(MAXB, dtype=jnp.int32) < counts[index]
        live = jnp.any((order[:, None] == jnp.arange(MAXB, dtype=jnp.int32)[None, :]) & used[:, None], axis=0)
        live_tok = jnp.repeat(live, BLOCK_TOKENS)
        keys_all = jnp.concatenate([gathered_keys, key_part], axis=0).astype(jnp.float32)
        vals_all = jnp.concatenate([gathered_values, value_part], axis=0).astype(jnp.float32)
        offsets = jnp.arange(NEW_PER_PATH, dtype=jnp.int32)
        causal = offsets[None, :] <= offsets[:, None]
        allowed = jnp.concatenate([jnp.broadcast_to(live_tok[None, :], (NEW_PER_PATH, token_extent)), causal], axis=1)
        group_queries = query_slice.reshape(NEW_PER_PATH, KEY_VALUE_HEADS, query_group, HEAD_SIZE)
        score = jnp.einsum('ckgd,nkd->kgcn', group_queries, keys_all) * HEAD_SIZE ** (-0.5)
        score = jnp.where(allowed[None, None], score, -jnp.inf)
        top = lax.optimization_barrier(jnp.max(score, axis=-1, keepdims=True))
        weight = jnp.exp(score - top)
        total = lax.optimization_barrier(jnp.sum(weight, axis=-1, keepdims=True))
        rounded = weight.astype(jnp.bfloat16).astype(jnp.float32)
        mixed = jnp.einsum('kgcn,nkd->kgcd', rounded, vals_all) / total
        return jnp.transpose(mixed, (2, 0, 1, 3)).reshape(NEW_PER_PATH, QUERY_HEADS * HEAD_SIZE).astype(jnp.bfloat16)
    attended = lax.map(one_traj, jnp.arange(TRAJ, dtype=jnp.int32)).reshape(NEW_TOKEN_TOTAL, QUERY_HEADS * HEAD_SIZE)
    return (attended, fresh_keys.reshape(NEW_TOKEN_TOTAL, KEY_VALUE_HEADS * HEAD_SIZE), fresh_values.reshape(NEW_TOKEN_TOTAL, KEY_VALUE_HEADS * HEAD_SIZE))
```

```python
import functools
import math

import jax
import jax.numpy as jnp
from jax import lax
from jax.experimental import pallas as pl
from jax.experimental.pallas import tpu as pltpu
from jax.sharding import PartitionSpec as P

HEAD_SIZE = 128
BLOCK_TOKENS = 128
GROUP = 4
KEY_CHUNK = 512
VMEM_LIMIT = 48 * 1024 * 1024


def swap(value, mask):
    pairs = [(source, source ^ mask) for source in range(lax.axis_size("ctx"))]
    return lax.ppermute(value, "ctx", pairs)


def swap_core(value):
    return lax.ppermute(value, "tp", [(0, 1), (1, 0)])


def spread(own, planes):
    pieces = {0: own}
    bit = planes // 2
    while bit:
        for apart in list(pieces):
            pieces[apart ^ bit] = swap(pieces[apart], GROUP * bit)
        bit //= 2
    return [pieces[apart] for apart in range(planes)]


def rope_tables(token_position):
    half = HEAD_SIZE // 2
    freq = jnp.exp(jnp.arange(half, dtype=jnp.float32) * (-2.0 / HEAD_SIZE) * math.log(1000000.0))
    angle = token_position.astype(jnp.float32)[..., None] * freq
    cosine, sine = jnp.cos(angle), jnp.sin(angle)
    return (
        jnp.concatenate([cosine, cosine], axis=-1),
        jnp.concatenate([-sine, sine], axis=-1),
    )


def project_kernel(planes, with_kv, first, width, *refs):
    scal, refs = refs[0], refs[1:]
    xs, refs = refs[:10], refs[10:]
    own_w, refs = refs[:planes], refs[planes:]
    rest_w, refs = refs[:planes], refs[planes:]
    cosine, sine, gain = refs[:3]
    refs = refs[3:]
    if with_kv:
        q_out, kv_out, x_all, w_all, x_sem, w_sem = refs
    else:
        q_out, x_all, w_all, x_sem, w_sem = refs
    plane, pos, core = scal[0], scal[1], scal[2]
    rows = xs[0].shape[0]
    half_cols = xs[0].shape[1]
    w_rows = own_w[0].shape[0]
    group_cols = own_w[0].shape[1] - HEAD_SIZE

    w_copies = []

    def fetch(src, row, col, cols):
        copy = pltpu.make_async_copy(
            src,
            w_all.at[pl.ds(pl.multiple_of(row, 16), w_rows), pl.ds(col, cols)],
            w_sem.at[len(w_copies)],
        )
        copy.start()
        w_copies.append(copy)

    x_copies = [[] for _ in range(GROUP)]

    def fetch_x(index):
        other, part = index // 5, index % 5
        block = min(part, 3)
        begin = rows // 2 if part == 4 else 0
        size = xs[index].shape[0]
        column = pl.multiple_of((core ^ other) * half_cols, half_cols)
        copy = pltpu.make_async_copy(
            xs[index],
            x_all.at[block, pl.ds(begin, size), pl.ds(column, half_cols)],
            x_sem.at[index],
        )
        copy.start()
        x_copies[block].append(copy)

    fetch_x(0)
    fetch_x(5)
    for apart in range(planes):
        base = (plane ^ apart) * GROUP
        fetch(own_w[apart].at[:, pl.ds(first, width)], (base + pos) * w_rows, 0, width)
        for r in range(1, GROUP):
            src = rest_w[apart].at[:, pl.ds((r - 1) * width, width)]
            fetch(src, (base + (pos ^ r)) * w_rows, 0, width)
        if with_kv:
            fetch(
                own_w[apart].at[:, pl.ds(group_cols, HEAD_SIZE)],
                (base + pos) * w_rows,
                width,
                HEAD_SIZE,
            )
            fetch(
                rest_w[apart].at[:, pl.ds(3 * width, HEAD_SIZE)],
                (base + (pos ^ 2)) * w_rows,
                width,
                HEAD_SIZE,
            )
    for index in (1, 6, 2, 7, 3, 8, 4, 9):
        fetch_x(index)
    if with_kv:
        blank = jnp.zeros((w_rows, HEAD_SIZE), jnp.bfloat16)
        for apart in range(planes):
            for r in (1, 3):
                row = ((plane ^ apart) * GROUP + (pos ^ r)) * w_rows
                w_all[pl.ds(pl.multiple_of(row, 16), w_rows), pl.ds(width, HEAD_SIZE)] = blank
    for copy in w_copies:
        copy.wait()
    for block in range(GROUP):
        for copy in x_copies[block]:
            copy.wait()
        result = jnp.dot(x_all[block], w_all[...], preferred_element_type=jnp.float32)
        for head in range(width // HEAD_SIZE):
            values = result[:, head * HEAD_SIZE : (head + 1) * HEAD_SIZE]
            mean = jnp.mean(values * values, axis=-1, keepdims=True)
            scaled = values * lax.rsqrt(mean + 1e-06) * gain[...]
            turned = scaled * cosine[block] + pltpu.roll(scaled, HEAD_SIZE // 2, 1) * sine[block]
            q_out[block, :, pl.ds(head * HEAD_SIZE, HEAD_SIZE)] = turned.astype(jnp.bfloat16)
        if with_kv:
            kv_out[block] = result[:, width:]


def project(scal, xs, own_w, rest_w, cosine, sine, gain, with_kv, first, width):
    planes = len(own_w)
    rows, half_cols = xs[0].shape
    depth = 2 * half_cols
    total = width + (HEAD_SIZE if with_kv else 0)
    out_shape = [jax.ShapeDtypeStruct((GROUP, rows, width), jnp.bfloat16)]
    if with_kv:
        out_shape.append(jax.ShapeDtypeStruct((GROUP, rows, HEAD_SIZE), jnp.float32))
    anywhere = pl.BlockSpec(memory_space=pl.ANY)
    vmem = pl.BlockSpec(memory_space=pltpu.VMEM)
    copies = planes * (6 if with_kv else 4)
    return pl.pallas_call(
        functools.partial(project_kernel, planes, with_kv, first, width),
        out_shape=out_shape,
        in_specs=[pl.BlockSpec(memory_space=pltpu.SMEM)]
        + [anywhere] * (10 + 2 * planes)
        + [vmem] * 3,
        out_specs=[vmem] * len(out_shape),
        scratch_shapes=[
            pltpu.VMEM((GROUP, rows, depth), jnp.bfloat16),
            pltpu.VMEM((depth, total), jnp.bfloat16),
            pltpu.SemaphoreType.DMA((10,)),
            pltpu.SemaphoreType.DMA((copies,)),
        ],
        compiler_params=pltpu.CompilerParams(vmem_limit_bytes=VMEM_LIMIT),
        cost_estimate=pl.CostEstimate(
            flops=2 * GROUP * rows * depth * total,
            bytes_accessed=2 * depth * (GROUP * rows + total),
            transcendentals=0,
        ),
    )(scal, *xs, *own_w, *rest_w, cosine, sine, gain)


def attend_kernel(first, width, aliased, *refs):
    scal, order = refs[:2]
    qs = refs[2:6]
    keys_mine, keys_theirs, vals_mine, vals_theirs, new_mine, new_theirs = refs[6:12]
    refs = refs[12 + int(aliased) :]
    out, k_all, v_all, q_all, o_all, kv_sem, new_sem, out_sem = refs
    pos, count = scal[1], scal[3]
    side = pos % 2
    rows = qs[0].shape[0]
    heads = width // HEAD_SIZE
    slots = order.shape[0]
    half_slots = slots // 2
    scale = HEAD_SIZE ** (-0.5) * math.log2(math.e)
    span = 2 * rows

    news = []
    for other, new in enumerate((new_mine, new_theirs)):
        row = pl.multiple_of((side ^ other) * rows, rows)
        for kind, (into, cols) in enumerate(((k_all, HEAD_SIZE), (v_all, HEAD_SIZE))):
            copy = pltpu.make_async_copy(
                new.at[kind],
                into.at[pl.ds(row, rows), pl.ds(0, cols)],
                new_sem.at[2 * other + kind],
            )
            copy.start()
            news.append(copy)

    def block_copies(j):
        slot = order[j]
        src_row = pl.multiple_of((slot % half_slots) * BLOCK_TOKENS, BLOCK_TOKENS)
        dst_row = pl.multiple_of(span + j * BLOCK_TOKENS, BLOCK_TOKENS)
        near = (slot // half_slots) == side

        def pair(k_src, v_src):
            return (
                pltpu.make_async_copy(
                    k_src.at[pl.ds(src_row, BLOCK_TOKENS)],
                    k_all.at[pl.ds(dst_row, BLOCK_TOKENS)],
                    kv_sem.at[0, j],
                ),
                pltpu.make_async_copy(
                    v_src.at[pl.ds(src_row, BLOCK_TOKENS)],
                    v_all.at[pl.ds(dst_row, BLOCK_TOKENS), pl.ds(0, HEAD_SIZE)],
                    kv_sem.at[1, j],
                ),
            )

        return near, pair(keys_mine, vals_mine), pair(keys_theirs, vals_theirs)

    def start_block(j, carry):
        near, mine, theirs = block_copies(j)

        @pl.when(near)
        def _():
            for copy in mine:
                copy.start()

        @pl.when(jnp.logical_not(near))
        def _():
            for copy in theirs:
                copy.start()

        return carry

    def wait_block(j, carry):
        _, mine, _ = block_copies(j)
        for copy in mine:
            copy.wait()
        return carry

    def clear_block(j, carry):
        row = pl.multiple_of(span + j * BLOCK_TOKENS, BLOCK_TOKENS)
        blank = jnp.zeros((BLOCK_TOKENS, HEAD_SIZE), jnp.bfloat16)
        k_all[pl.ds(row, BLOCK_TOKENS), :] = blank
        v_all[pl.ds(row, BLOCK_TOKENS), pl.ds(0, HEAD_SIZE)] = blank
        return carry

    per_chunk = KEY_CHUNK // BLOCK_TOKENS
    chunks = (count + per_chunk - 1) // per_chunk
    lax.fori_loop(0, count, start_block, 0)
    lax.fori_loop(count, chunks * per_chunk, clear_block, 0)
    v_all[:, pl.ds(HEAD_SIZE, HEAD_SIZE)] = jnp.ones((v_all.shape[0], HEAD_SIZE), jnp.bfloat16)
    for r in range(GROUP):
        for head in range(heads):
            q_all[r, pl.ds(head * rows, rows), :] = qs[r][:, pl.ds(head * HEAD_SIZE, HEAD_SIZE)]
    for copy in news:
        copy.wait()
    lax.fori_loop(0, count, wait_block, 0)

    block_rows = heads * rows

    def scores(q, row, size):
        keys = k_all[pl.ds(row, size), :]
        return lax.dot_general(
            q, keys, (((1,), (1,)), ((), ())), preferred_element_type=jnp.float32
        )

    def mix(s, top, row, size):
        weight = jnp.exp2((s - top) * scale).astype(jnp.bfloat16)
        return jnp.dot(
            weight, v_all[pl.ds(row, size), :], preferred_element_type=jnp.float32
        )

    def attend_block(r, carry):
        q = q_all[r]
        s = scores(q, 0, span)
        token = lax.broadcasted_iota(jnp.int32, (block_rows, span), 0) % rows
        place = lax.broadcasted_iota(jnp.int32, (block_rows, span), 1)
        s = jnp.where(place <= token + side * rows, s, -1e30)
        top = jnp.max(s, axis=-1, keepdims=True)
        mixed = mix(s, top, 0, span)

        def step(chunk, state):
            top, mixed = state
            row = pl.multiple_of(span + chunk * KEY_CHUNK, KEY_CHUNK)
            s = scores(q, row, KEY_CHUNK)
            key = lax.broadcasted_iota(jnp.int32, (block_rows, KEY_CHUNK), 1)
            s = jnp.where(key < count * BLOCK_TOKENS - chunk * KEY_CHUNK, s, -1e30)
            new_top = jnp.maximum(top, jnp.max(s, axis=-1, keepdims=True))
            mixed = mixed * jnp.exp2((top - new_top) * scale) + mix(s, new_top, row, KEY_CHUNK)
            return new_top, mixed

        top, mixed = lax.fori_loop(0, chunks, step, (top, mixed))
        result = (mixed[:, :HEAD_SIZE] / mixed[:, HEAD_SIZE:]).astype(jnp.bfloat16)
        for head in range(heads):
            o_all[r, :, pl.ds(head * HEAD_SIZE, HEAD_SIZE)] = result[
                head * rows : (head + 1) * rows
            ]
        return carry

    lax.fori_loop(0, GROUP, attend_block, 0)
    group_cols = out.shape[1] // GROUP
    copies = []
    for r in range(GROUP):
        column = pl.multiple_of((pos ^ r) * group_cols + first, HEAD_SIZE)
        copy = pltpu.make_async_copy(
            o_all.at[r], out.at[:, pl.ds(column, width)], out_sem.at[r]
        )
        copy.start()
        copies.append(copy)
    for copy in copies:
        copy.wait()


def attend(scal, order, qs, caches, news, so_far, first, width, out_cols):
    rows = qs[0].shape[0]
    slots = order.shape[0]
    heads = width // HEAD_SIZE
    span = 2 * rows
    tokens = span + slots * BLOCK_TOKENS
    anywhere = pl.BlockSpec(memory_space=pl.ANY)
    vmem = pl.BlockSpec(memory_space=pltpu.VMEM)
    smem = pl.BlockSpec(memory_space=pltpu.SMEM)
    operands = [scal, order, *qs, *caches, *news]
    in_specs = [smem] * 2 + [vmem] * 4 + [anywhere] * 6
    aliases = {}
    if so_far is not None:
        aliases = {len(operands): 0}
        operands.append(so_far)
        in_specs.append(anywhere)
    return pl.pallas_call(
        functools.partial(attend_kernel, first, width, so_far is not None),
        out_shape=jax.ShapeDtypeStruct((rows, out_cols), jnp.bfloat16),
        in_specs=in_specs,
        out_specs=anywhere,
        input_output_aliases=aliases,
        scratch_shapes=[
            pltpu.VMEM((tokens, HEAD_SIZE), jnp.bfloat16),
            pltpu.VMEM((tokens, 2 * HEAD_SIZE), jnp.bfloat16),
            pltpu.VMEM((GROUP, heads * rows, HEAD_SIZE), jnp.bfloat16),
            pltpu.VMEM((GROUP, rows, width), jnp.bfloat16),
            pltpu.SemaphoreType.DMA((2, slots)),
            pltpu.SemaphoreType.DMA((4,)),
            pltpu.SemaphoreType.DMA((GROUP,)),
        ],
        compiler_params=pltpu.CompilerParams(vmem_limit_bytes=VMEM_LIMIT),
        cost_estimate=pl.CostEstimate(
            flops=8 * GROUP * heads * rows * tokens * HEAD_SIZE,
            bytes_accessed=8 * tokens * HEAD_SIZE,
            transcendentals=GROUP * heads * rows * tokens,
        ),
    )(*operands)


def on_device(
    hidden,
    w_query,
    key_weight,
    value_weight,
    q_gain,
    key_norm_gain,
    earlier_keys,
    earlier_values,
    counts,
    place,
):
    planes = lax.axis_size("ctx") // GROUP
    ctx = lax.axis_index("ctx")
    core = lax.axis_index("tp")
    plane = ctx // GROUP
    pos = ctx % GROUP
    rows = hidden.shape[0]
    w_rows = w_query.shape[0]
    group_cols = w_query.shape[1] // GROUP
    widths = (group_cols // 2, group_cols - group_cols // 2)
    takes_keys = pos < 2

    def columns_for(r):
        return lax.dynamic_slice(w_query, (0, group_cols * (pos ^ r)), (w_rows, group_cols))

    kind_mine = jnp.where(takes_keys, key_weight, value_weight)
    kind_theirs = jnp.where(takes_keys, value_weight, key_weight)
    own = jnp.concatenate([columns_for(0), kind_mine], axis=1)
    got_1 = swap(columns_for(1), 1)
    got_2 = swap(jnp.concatenate([columns_for(2), kind_theirs], axis=1), 2)
    got_3 = swap(columns_for(3), 3)
    own_w = spread(own, planes)

    half_rows = rows // 2
    x_1 = swap(hidden, 1)
    x_2 = swap(hidden, 2)
    x_3a = swap(x_2[:half_rows], 1)
    x_3b = swap(x_1[half_rows:], 2)
    xs = [hidden, x_1, x_2, x_3a, x_3b]
    xs = xs + [swap_core(x) for x in xs]

    rest_first = spread(
        jnp.concatenate(
            [
                got_1[:, : widths[0]],
                got_2[:, : widths[0]],
                got_3[:, : widths[0]],
                got_2[:, group_cols:],
            ],
            axis=1,
        ),
        planes,
    )
    rest_second = spread(
        jnp.concatenate(
            [
                got_1[:, widths[0] :],
                got_2[:, widths[0] : group_cols],
                got_3[:, widths[0] :],
            ],
            axis=1,
        ),
        planes,
    )
    keys_theirs = swap(earlier_keys, 1)
    vals_theirs = swap(earlier_values, 1)

    count = lax.dynamic_index_in_dim(counts, ctx // 2, 0, keepdims=False)
    order = lax.dynamic_index_in_dim(place, ctx // 2, 0, keepdims=False)
    scal = jnp.stack([plane, pos, core, count]).astype(jnp.int32)
    spots = pos ^ jnp.arange(GROUP, dtype=jnp.int32)
    spot_counts = counts[plane * 2 + spots // 2]
    token_position = (
        spot_counts[:, None] * BLOCK_TOKENS
        + (spots % 2)[:, None] * rows
        + jnp.arange(rows, dtype=jnp.int32)[None, :]
    )
    cosine, sine = rope_tables(token_position)
    gain = q_gain[None, :]

    q_first, partial = project(
        scal, xs, own_w, rest_first, cosine, sine, gain, True, 0, widths[0]
    )

    arrived = swap(partial[1::2], 1)
    summed = partial[0::2] + arrived
    mean = jnp.mean(summed * summed, axis=-1, keepdims=True)
    scaled = summed * lax.rsqrt(mean + 1e-06) * key_norm_gain
    turned = scaled * cosine[0::2] + jnp.roll(scaled, HEAD_SIZE // 2, axis=-1) * sine[0::2]
    final = jnp.where(takes_keys, turned, summed).astype(jnp.bfloat16)
    crossed = swap(final[1], 2)
    keys_mine = jnp.where(takes_keys, final[0], crossed)
    values_mine = jnp.where(takes_keys, crossed, final[0])
    new_mine = jnp.stack([keys_mine, values_mine])
    new_theirs = swap(new_mine, 1)

    caches = (earlier_keys, keys_theirs, earlier_values, vals_theirs)
    news = (new_mine, new_theirs)

    def to_owners(q):
        return [q[0]] + [swap(q[r], r) for r in range(1, GROUP)]

    out_cols = w_query.shape[1]
    attended = attend(
        scal, order, to_owners(q_first), caches, news, None, 0, widths[0], out_cols
    )
    (q_second,) = project(
        scal, xs, own_w, rest_second, cosine, sine, gain, False, widths[0], widths[1]
    )
    attended = attend(
        scal,
        order,
        to_owners(q_second),
        caches,
        news,
        attended,
        widths[0],
        widths[1],
        out_cols,
    )
    return (attended, keys_mine, values_mine)


def solution(mesh):
    placed = (
        P("ctx", "tp"),
        P("ctx", "tp"),
        P("ctx", "tp"),
        P("ctx", "tp"),
        P(),
        P(),
        P("ctx", "tp"),
        P("ctx", "tp"),
        P(),
        P(),
    )
    return jax.shard_map(
        on_device,
        mesh=mesh,
        in_specs=placed,
        out_specs=(P("ctx", "tp"), P("ctx", "tp"), P("ctx", "tp")),
        check_vma=False,
    )
```

```python
import functools
import math

import jax
import jax.numpy as jnp
from jax import lax
from jax.experimental import pallas as pl
from jax.experimental.pallas import tpu as pltpu
from jax.sharding import PartitionSpec as P

HEAD_SIZE = 128
BLOCK_TOKENS = 128
GROUP = 4
KEY_CHUNK = 512
VMEM_LIMIT = 48 * 1024 * 1024


def swap(value, mask):
    pairs = [(source, source ^ mask) for source in range(lax.axis_size("ctx"))]
    return lax.ppermute(value, "ctx", pairs)


def after(value, *others):
    return lax.optimization_barrier((value, *others))[0]


def swap_core(value):
    return lax.ppermute(value, "tp", [(0, 1), (1, 0)])


def spread(own, planes):
    pieces = {0: own}
    bit = planes // 2
    while bit:
        for apart in list(pieces):
            pieces[apart ^ bit] = swap(pieces[apart], GROUP * bit)
        bit //= 2
    return [pieces[apart] for apart in range(planes)]


def rope_tables(token_position):
    half = HEAD_SIZE // 2
    freq = jnp.exp(jnp.arange(half, dtype=jnp.float32) * (-2.0 / HEAD_SIZE) * math.log(1000000.0))
    angle = token_position.astype(jnp.float32)[..., None] * freq
    cosine, sine = jnp.cos(angle), jnp.sin(angle)
    return (
        jnp.concatenate([cosine, cosine], axis=-1),
        jnp.concatenate([-sine, sine], axis=-1),
    )


def project_kernel(planes, with_kv, first, width, *refs):
    scal, refs = refs[0], refs[1:]
    xs, refs = refs[:2], refs[2:]
    own_w, refs = refs[:planes], refs[planes:]
    rest_w, refs = refs[:planes], refs[planes:]
    cosine, sine, gain = refs[:3]
    refs = refs[3:]
    if with_kv:
        q_out, kv_out, x_all, w_all, x_sem, w_sem = refs
    else:
        q_out, x_all, w_all, x_sem, w_sem = refs
    plane, pos, core = scal[0], scal[1], scal[2]
    half_cols = xs[0].shape[2]
    w_rows = own_w[0].shape[0]
    group_cols = own_w[0].shape[1] - HEAD_SIZE

    w_copies = []

    def fetch(src, row, col, cols):
        copy = pltpu.make_async_copy(
            src,
            w_all.at[pl.ds(pl.multiple_of(row, 16), w_rows), pl.ds(col, cols)],
            w_sem.at[len(w_copies)],
        )
        copy.start()
        w_copies.append(copy)

    x_copies = []

    def fetch_x(block):
        for other in range(2):
            column = pl.multiple_of((core ^ other) * half_cols, half_cols)
            copy = pltpu.make_async_copy(
                xs[other].at[pos ^ block],
                x_all.at[block, :, pl.ds(column, half_cols)],
                x_sem.at[block, other],
            )
            copy.start()
            x_copies.append(copy)

    fetch_x(0)
    for apart in range(planes):
        base = (plane ^ apart) * GROUP
        fetch(own_w[apart].at[:, pl.ds(first, width)], (base + pos) * w_rows, 0, width)
        for r in range(1, GROUP):
            src = rest_w[apart].at[:, pl.ds((r - 1) * width, width)]
            fetch(src, (base + (pos ^ r)) * w_rows, 0, width)
        if with_kv:
            fetch(
                own_w[apart].at[:, pl.ds(group_cols, HEAD_SIZE)],
                (base + pos) * w_rows,
                width,
                HEAD_SIZE,
            )
            fetch(
                rest_w[apart].at[:, pl.ds(3 * width, HEAD_SIZE)],
                (base + (pos ^ 2)) * w_rows,
                width,
                HEAD_SIZE,
            )
    for block in range(1, GROUP):
        fetch_x(block)
    if with_kv:
        blank = jnp.zeros((w_rows, HEAD_SIZE), jnp.bfloat16)
        for apart in range(planes):
            for r in (1, 3):
                row = ((plane ^ apart) * GROUP + (pos ^ r)) * w_rows
                w_all[pl.ds(pl.multiple_of(row, 16), w_rows), pl.ds(width, HEAD_SIZE)] = blank
    for copy in w_copies:
        copy.wait()
    for block in range(GROUP):
        for copy in x_copies[2 * block : 2 * block + 2]:
            copy.wait()
        result = jnp.dot(x_all[block], w_all[...], preferred_element_type=jnp.float32)
        for head in range(width // HEAD_SIZE):
            values = result[:, head * HEAD_SIZE : (head + 1) * HEAD_SIZE]
            mean = jnp.mean(values * values, axis=-1, keepdims=True)
            scaled = values * lax.rsqrt(mean + 1e-06) * gain[...]
            turned = scaled * cosine[block] + pltpu.roll(scaled, HEAD_SIZE // 2, 1) * sine[block]
            q_out[block, :, pl.ds(head * HEAD_SIZE, HEAD_SIZE)] = turned.astype(jnp.bfloat16)
        if with_kv:
            kv_out[block] = result[:, width:]


def project(scal, xs, own_w, rest_w, cosine, sine, gain, with_kv, first, width):
    planes = len(own_w)
    _, rows, half_cols = xs[0].shape
    depth = 2 * half_cols
    total = width + (HEAD_SIZE if with_kv else 0)
    out_shape = [jax.ShapeDtypeStruct((GROUP, rows, width), jnp.bfloat16)]
    if with_kv:
        out_shape.append(jax.ShapeDtypeStruct((GROUP, rows, HEAD_SIZE), jnp.float32))
    anywhere = pl.BlockSpec(memory_space=pl.ANY)
    vmem = pl.BlockSpec(memory_space=pltpu.VMEM)
    copies = planes * (6 if with_kv else 4)
    return pl.pallas_call(
        functools.partial(project_kernel, planes, with_kv, first, width),
        out_shape=out_shape,
        in_specs=[pl.BlockSpec(memory_space=pltpu.SMEM)]
        + [anywhere] * (2 + 2 * planes)
        + [vmem] * 3,
        out_specs=[vmem] * len(out_shape),
        scratch_shapes=[
            pltpu.VMEM((GROUP, rows, depth), jnp.bfloat16),
            pltpu.VMEM((depth, total), jnp.bfloat16),
            pltpu.SemaphoreType.DMA((GROUP, 2)),
            pltpu.SemaphoreType.DMA((copies,)),
        ],
        compiler_params=pltpu.CompilerParams(vmem_limit_bytes=VMEM_LIMIT),
        cost_estimate=pl.CostEstimate(
            flops=2 * GROUP * rows * depth * total,
            bytes_accessed=2 * depth * (GROUP * rows + total),
            transcendentals=0,
        ),
    )(scal, *xs, *own_w, *rest_w, cosine, sine, gain)


def attend_kernel(first, width, aliased, *refs):
    scal, order = refs[:2]
    qs = refs[2:6]
    keys_mine, keys_theirs, vals_mine, vals_theirs, new_mine, new_theirs = refs[6:12]
    refs = refs[12 + int(aliased) :]
    out, k_all, v_all, q_all, o_all, kv_sem, new_sem, out_sem = refs
    pos, count = scal[1], scal[3]
    side = pos % 2
    rows = qs[0].shape[0]
    heads = width // HEAD_SIZE
    slots = order.shape[0]
    half_slots = slots // 2
    scale = HEAD_SIZE ** (-0.5) * math.log2(math.e)
    span = 2 * rows

    news = []
    for other, new in enumerate((new_mine, new_theirs)):
        row = pl.multiple_of((side ^ other) * rows, rows)
        for kind, (into, cols) in enumerate(((k_all, HEAD_SIZE), (v_all, HEAD_SIZE))):
            copy = pltpu.make_async_copy(
                new.at[kind],
                into.at[pl.ds(row, rows), pl.ds(0, cols)],
                new_sem.at[2 * other + kind],
            )
            copy.start()
            news.append(copy)

    def block_copies(j):
        slot = order[j]
        src_row = pl.multiple_of((slot % half_slots) * BLOCK_TOKENS, BLOCK_TOKENS)
        dst_row = pl.multiple_of(span + j * BLOCK_TOKENS, BLOCK_TOKENS)
        near = (slot // half_slots) == side

        def pair(k_src, v_src):
            return (
                pltpu.make_async_copy(
                    k_src.at[pl.ds(src_row, BLOCK_TOKENS)],
                    k_all.at[pl.ds(dst_row, BLOCK_TOKENS)],
                    kv_sem.at[0, j],
                ),
                pltpu.make_async_copy(
                    v_src.at[pl.ds(src_row, BLOCK_TOKENS)],
                    v_all.at[pl.ds(dst_row, BLOCK_TOKENS), pl.ds(0, HEAD_SIZE)],
                    kv_sem.at[1, j],
                ),
            )

        return near, pair(keys_mine, vals_mine), pair(keys_theirs, vals_theirs)

    def start_block(j, carry):
        near, mine, theirs = block_copies(j)

        @pl.when(near)
        def _():
            for copy in mine:
                copy.start()

        @pl.when(jnp.logical_not(near))
        def _():
            for copy in theirs:
                copy.start()

        return carry

    def wait_block(j, carry):
        _, mine, _ = block_copies(j)
        for copy in mine:
            copy.wait()
        return carry

    def clear_block(j, carry):
        row = pl.multiple_of(span + j * BLOCK_TOKENS, BLOCK_TOKENS)
        blank = jnp.zeros((BLOCK_TOKENS, HEAD_SIZE), jnp.bfloat16)
        k_all[pl.ds(row, BLOCK_TOKENS), :] = blank
        v_all[pl.ds(row, BLOCK_TOKENS), pl.ds(0, HEAD_SIZE)] = blank
        return carry

    per_chunk = KEY_CHUNK // BLOCK_TOKENS
    chunks = (count + per_chunk - 1) // per_chunk
    lax.fori_loop(0, count, start_block, 0)
    lax.fori_loop(count, chunks * per_chunk, clear_block, 0)
    v_all[:, pl.ds(HEAD_SIZE, HEAD_SIZE)] = jnp.ones((v_all.shape[0], HEAD_SIZE), jnp.bfloat16)
    for r in range(GROUP):
        for head in range(heads):
            q_all[r, pl.ds(head * rows, rows), :] = qs[r][:, pl.ds(head * HEAD_SIZE, HEAD_SIZE)]
    for copy in news:
        copy.wait()
    lax.fori_loop(0, count, wait_block, 0)

    block_rows = heads * rows

    def scores(q, row, size):
        keys = k_all[pl.ds(row, size), :]
        return lax.dot_general(
            q, keys, (((1,), (1,)), ((), ())), preferred_element_type=jnp.float32
        )

    def mix(s, top, row, size):
        weight = jnp.exp2((s - top) * scale).astype(jnp.bfloat16)
        return jnp.dot(
            weight, v_all[pl.ds(row, size), :], preferred_element_type=jnp.float32
        )

    def attend_block(r, carry):
        q = q_all[r]
        s = scores(q, 0, span)
        token = lax.broadcasted_iota(jnp.int32, (block_rows, span), 0) % rows
        place = lax.broadcasted_iota(jnp.int32, (block_rows, span), 1)
        s = jnp.where(place <= token + side * rows, s, -1e30)
        top = jnp.max(s, axis=-1, keepdims=True)
        mixed = mix(s, top, 0, span)

        def step(chunk, state):
            top, mixed = state
            row = pl.multiple_of(span + chunk * KEY_CHUNK, KEY_CHUNK)
            s = scores(q, row, KEY_CHUNK)
            key = lax.broadcasted_iota(jnp.int32, (block_rows, KEY_CHUNK), 1)
            s = jnp.where(key < count * BLOCK_TOKENS - chunk * KEY_CHUNK, s, -1e30)
            new_top = jnp.maximum(top, jnp.max(s, axis=-1, keepdims=True))
            mixed = mixed * jnp.exp2((top - new_top) * scale) + mix(s, new_top, row, KEY_CHUNK)
            return new_top, mixed

        top, mixed = lax.fori_loop(0, chunks, step, (top, mixed))
        result = (mixed[:, :HEAD_SIZE] / mixed[:, HEAD_SIZE:]).astype(jnp.bfloat16)
        for head in range(heads):
            o_all[r, :, pl.ds(head * HEAD_SIZE, HEAD_SIZE)] = result[
                head * rows : (head + 1) * rows
            ]
        return carry

    lax.fori_loop(0, GROUP, attend_block, 0)
    group_cols = out.shape[1] // GROUP
    copies = []
    for r in range(GROUP):
        column = pl.multiple_of((pos ^ r) * group_cols + first, HEAD_SIZE)
        copy = pltpu.make_async_copy(
            o_all.at[r], out.at[:, pl.ds(column, width)], out_sem.at[r]
        )
        copy.start()
        copies.append(copy)
    for copy in copies:
        copy.wait()


def attend(scal, order, qs, caches, news, so_far, first, width, out_cols):
    rows = qs[0].shape[0]
    slots = order.shape[0]
    heads = width // HEAD_SIZE
    span = 2 * rows
    tokens = span + slots * BLOCK_TOKENS
    anywhere = pl.BlockSpec(memory_space=pl.ANY)
    vmem = pl.BlockSpec(memory_space=pltpu.VMEM)
    smem = pl.BlockSpec(memory_space=pltpu.SMEM)
    operands = [scal, order, *qs, *caches, *news]
    in_specs = [smem] * 2 + [vmem] * 4 + [anywhere] * 6
    aliases = {}
    if so_far is not None:
        aliases = {len(operands): 0}
        operands.append(so_far)
        in_specs.append(anywhere)
    return pl.pallas_call(
        functools.partial(attend_kernel, first, width, so_far is not None),
        out_shape=jax.ShapeDtypeStruct((rows, out_cols), jnp.bfloat16),
        in_specs=in_specs,
        out_specs=anywhere,
        input_output_aliases=aliases,
        scratch_shapes=[
            pltpu.VMEM((tokens, HEAD_SIZE), jnp.bfloat16),
            pltpu.VMEM((tokens, 2 * HEAD_SIZE), jnp.bfloat16),
            pltpu.VMEM((GROUP, heads * rows, HEAD_SIZE), jnp.bfloat16),
            pltpu.VMEM((GROUP, rows, width), jnp.bfloat16),
            pltpu.SemaphoreType.DMA((2, slots)),
            pltpu.SemaphoreType.DMA((4,)),
            pltpu.SemaphoreType.DMA((GROUP,)),
        ],
        compiler_params=pltpu.CompilerParams(vmem_limit_bytes=VMEM_LIMIT),
        cost_estimate=pl.CostEstimate(
            flops=8 * GROUP * heads * rows * tokens * HEAD_SIZE,
            bytes_accessed=8 * tokens * HEAD_SIZE,
            transcendentals=GROUP * heads * rows * tokens,
        ),
    )(*operands)


def on_device(
    hidden,
    w_query,
    key_weight,
    value_weight,
    q_gain,
    key_norm_gain,
    earlier_keys,
    earlier_values,
    counts,
    place,
):
    planes = lax.axis_size("ctx") // GROUP
    ctx = lax.axis_index("ctx")
    core = lax.axis_index("tp")
    plane = ctx // GROUP
    pos = ctx % GROUP
    rows = hidden.shape[0]
    w_rows = w_query.shape[0]
    group_cols = w_query.shape[1] // GROUP
    widths = (group_cols // 2, group_cols - group_cols // 2)
    takes_keys = pos < 2

    def columns_for(r):
        return lax.dynamic_slice(w_query, (0, group_cols * (pos ^ r)), (w_rows, group_cols))

    kind_mine = jnp.where(takes_keys, key_weight, value_weight)
    kind_theirs = jnp.where(takes_keys, value_weight, key_weight)
    own = jnp.concatenate([columns_for(0), kind_mine], axis=1)
    got_1 = swap(columns_for(1), 1)
    got_2 = swap(jnp.concatenate([columns_for(2), kind_theirs], axis=1), 2)
    got_3 = swap(columns_for(3), 3)
    own_w = spread(own, planes)

    own_far = own_w[planes // 2]
    hidden = after(hidden, got_1, got_2, got_3, own_far)
    in_plane = [[GROUP * p + q for q in range(GROUP)] for p in range(planes)]
    x_mine = lax.all_gather(hidden, "ctx", axis_index_groups=in_plane)

    first_source = jnp.concatenate(
        [
            got_1[:, : widths[0]],
            got_2[:, : widths[0]],
            got_3[:, : widths[0]],
            got_2[:, group_cols:],
        ],
        axis=1,
    )
    rest_first = spread(after(first_source, own_far), planes)
    second_source = jnp.concatenate(
        [
            got_1[:, widths[0] :],
            got_2[:, widths[0] : group_cols],
            got_3[:, widths[0] :],
        ],
        axis=1,
    )
    rest_second = spread(after(second_source, rest_first[planes // 2], own_w[-1]), planes)
    xs = [x_mine, swap_core(after(x_mine, *rest_first, *own_w))]
    earlier_keys, earlier_values = lax.optimization_barrier(
        (earlier_keys, earlier_values, x_mine)
    )[:2]
    keys_theirs = swap(earlier_keys, 1)
    vals_theirs = swap(earlier_values, 1)

    count = lax.dynamic_index_in_dim(counts, ctx // 2, 0, keepdims=False)
    order = lax.dynamic_index_in_dim(place, ctx // 2, 0, keepdims=False)
    scal = jnp.stack([plane, pos, core, count]).astype(jnp.int32)
    spots = pos ^ jnp.arange(GROUP, dtype=jnp.int32)
    spot_counts = counts[plane * 2 + spots // 2]
    token_position = (
        spot_counts[:, None] * BLOCK_TOKENS
        + (spots % 2)[:, None] * rows
        + jnp.arange(rows, dtype=jnp.int32)[None, :]
    )
    cosine, sine = rope_tables(token_position)
    gain = q_gain[None, :]

    q_first, partial = project(
        scal, xs, own_w, rest_first, cosine, sine, gain, True, 0, widths[0]
    )

    arrived = swap(partial[1::2], 1)
    summed = partial[0::2] + arrived
    mean = jnp.mean(summed * summed, axis=-1, keepdims=True)
    scaled = summed * lax.rsqrt(mean + 1e-06) * key_norm_gain
    turned = scaled * cosine[0::2] + jnp.roll(scaled, HEAD_SIZE // 2, axis=-1) * sine[0::2]
    final = jnp.where(takes_keys, turned, summed).astype(jnp.bfloat16)
    crossed = swap(final[1], 2)
    keys_mine = jnp.where(takes_keys, final[0], crossed)
    values_mine = jnp.where(takes_keys, crossed, final[0])
    new_mine = jnp.stack([keys_mine, values_mine])
    new_theirs = swap(new_mine, 1)

    caches = (earlier_keys, keys_theirs, earlier_values, vals_theirs)
    news = (new_mine, new_theirs)

    def to_owners(q):
        return [q[0]] + [swap(q[r], r) for r in range(1, GROUP)]

    out_cols = w_query.shape[1]
    attended = attend(
        scal, order, to_owners(q_first), caches, news, None, 0, widths[0], out_cols
    )
    (q_second,) = project(
        scal, xs, own_w, rest_second, cosine, sine, gain, False, widths[0], widths[1]
    )
    attended = attend(
        scal,
        order,
        to_owners(q_second),
        caches,
        news,
        attended,
        widths[0],
        widths[1],
        out_cols,
    )
    return (attended, keys_mine, values_mine)


def solution(mesh):
    placed = (
        P("ctx", "tp"),
        P("ctx", "tp"),
        P("ctx", "tp"),
        P("ctx", "tp"),
        P(),
        P(),
        P("ctx", "tp"),
        P("ctx", "tp"),
        P(),
        P(),
    )
    return jax.shard_map(
        on_device,
        mesh=mesh,
        in_specs=placed,
        out_specs=(P("ctx", "tp"), P("ctx", "tp"), P("ctx", "tp")),
        check_vma=False,
    )
```

```python
import functools
import math

import jax
import jax.numpy as jnp
from jax import lax
from jax.experimental import pallas as pl
from jax.experimental.pallas import tpu as pltpu
from jax.sharding import PartitionSpec as P

HEAD_SIZE = 128
BLOCK_TOKENS = 128
GROUP = 4
RING = (0, 1, 3, 2)
KEY_CHUNK = 512
VMEM_LIMIT = 48 * 1024 * 1024


def swap(value, mask):
    pairs = [(source, source ^ mask) for source in range(lax.axis_size("ctx"))]
    return lax.ppermute(value, "ctx", pairs)


def after(value, *others):
    return lax.optimization_barrier((value, *others))[0]


def spread(own, planes):
    pieces = {0: own}
    bit = planes // 2
    while bit:
        for apart in list(pieces):
            pieces[apart ^ bit] = swap(pieces[apart], GROUP * bit)
        bit //= 2
    return [pieces[apart] for apart in range(planes)]


def rope_tables(token_position):
    half = HEAD_SIZE // 2
    freq = jnp.exp(jnp.arange(half, dtype=jnp.float32) * (-2.0 / HEAD_SIZE) * math.log(1000000.0))
    angle = token_position.astype(jnp.float32)[..., None] * freq
    cosine, sine = jnp.cos(angle), jnp.sin(angle)
    return (
        jnp.concatenate([cosine, cosine], axis=-1),
        jnp.concatenate([-sine, sine], axis=-1),
    )


def ring_members(planes):
    groups = []
    for plane in range(planes):
        members = []
        for rank, spot in enumerate(RING):
            for side in range(2):
                members.append((plane * GROUP + spot) * 2 + (side ^ (rank & 1)))
        groups.append(members)
    return groups


def fetch_features(x_ref, x_chunk, sem, half, column, pos):
    rows = x_ref.shape[1]
    copies = []
    for rank, spot in enumerate(RING):
        member = 2 * rank + (half ^ (rank & 1))
        copy = pltpu.make_async_copy(
            x_ref.at[member, :, pl.ds(column, x_chunk.shape[1])],
            x_chunk.at[pl.ds(pl.multiple_of((pos ^ spot) * rows, rows), rows)],
            sem.at[rank],
        )
        copy.start()
        copies.append(copy)
    return copies


def project_kernel(planes, first, width, *refs):
    scal, x_ref = refs[:2]
    own_w, rest_w = refs[2 : 2 + planes], refs[2 + planes : 2 + 2 * planes]
    cosine, sine, gain, q_out, x_all, w_all, x_sem, w_sem = refs[2 + 2 * planes :]
    plane, pos = scal[0], scal[1]
    rows = x_ref.shape[1]
    w_rows = own_w[0].shape[0]
    depth = GROUP * w_rows

    copies = []
    for apart in range(planes):
        there = plane ^ apart
        half = there // (planes // 2)
        column = pl.multiple_of((there % (planes // 2)) * depth, depth)
        started = []
        for r in range(GROUP):
            if r == 0:
                src = own_w[apart].at[:, pl.ds(first, width)]
            else:
                src = rest_w[apart].at[:, pl.ds((r - 1) * width, width)]
            copy = pltpu.make_async_copy(
                src,
                w_all.at[apart, pl.ds(pl.multiple_of((pos ^ r) * w_rows, w_rows), w_rows)],
                w_sem.at[apart, r],
            )
            copy.start()
            started.append(copy)
        started += fetch_features(
            x_ref, x_all.at[apart], x_sem.at[apart], half, column, pos
        )
        copies.append(started)

    result = None
    for apart in range(planes):
        for copy in copies[apart]:
            copy.wait()
        term = jnp.dot(x_all[apart], w_all[apart], preferred_element_type=jnp.float32)
        result = term if result is None else result + term
    for head in range(width // HEAD_SIZE):
        values = result[:, head * HEAD_SIZE : (head + 1) * HEAD_SIZE]
        mean = jnp.mean(values * values, axis=-1, keepdims=True)
        scaled = values * lax.rsqrt(mean + 1e-06) * gain[...]
        turned = scaled * cosine[...] + pltpu.roll(scaled, HEAD_SIZE // 2, 1) * sine[...]
        for block in range(GROUP):
            q_out[block, :, pl.ds(head * HEAD_SIZE, HEAD_SIZE)] = turned[
                block * rows : (block + 1) * rows
            ].astype(jnp.bfloat16)


def project(scal, x, own_w, rest_w, cosine, sine, gain, first, width):
    planes = len(own_w)
    rows, half_cols = x.shape[1:]
    w_rows = own_w[0].shape[0]
    depth = 2 * half_cols
    anywhere = pl.BlockSpec(memory_space=pl.ANY)
    vmem = pl.BlockSpec(memory_space=pltpu.VMEM)
    return pl.pallas_call(
        functools.partial(project_kernel, planes, first, width),
        out_shape=jax.ShapeDtypeStruct((GROUP, rows, width), jnp.bfloat16),
        in_specs=[pl.BlockSpec(memory_space=pltpu.SMEM)]
        + [anywhere] * (1 + 2 * planes)
        + [vmem] * 3,
        out_specs=vmem,
        scratch_shapes=[
            pltpu.VMEM((planes, GROUP * rows, GROUP * w_rows), jnp.bfloat16),
            pltpu.VMEM((planes, GROUP * w_rows, width), jnp.bfloat16),
            pltpu.SemaphoreType.DMA((planes, GROUP)),
            pltpu.SemaphoreType.DMA((planes, GROUP)),
        ],
        compiler_params=pltpu.CompilerParams(vmem_limit_bytes=VMEM_LIMIT),
        cost_estimate=pl.CostEstimate(
            flops=2 * GROUP * rows * depth * width,
            bytes_accessed=2 * depth * (GROUP * rows + width),
            transcendentals=0,
        ),
    )(scal, x, *own_w, *rest_w, cosine, sine, gain)


def project_kv_kernel(planes, skip, *refs):
    scal, x_ref = refs[:2]
    own_w = refs[2 : 2 + planes]
    kv_out, x_all, w_all, x_sem, w_sem = refs[2 + planes :]
    plane, pos = scal[0], scal[1]
    w_rows = own_w[0].shape[0]
    depth = x_all.shape[2]
    width = w_all.shape[2]
    offset = pos * w_rows if depth == w_rows else 0

    copies = []
    for apart in range(planes):
        there = plane ^ apart
        half = there // (planes // 2)
        column = pl.multiple_of(
            (there % (planes // 2)) * GROUP * w_rows + offset, HEAD_SIZE
        )
        row = 0
        if depth > w_rows:
            w_all[apart] = jnp.zeros((depth, width), jnp.bfloat16)
            row = pl.multiple_of(pos * w_rows, w_rows)
        copy = pltpu.make_async_copy(
            own_w[apart].at[:, pl.ds(skip, width)],
            w_all.at[apart, pl.ds(row, w_rows)],
            w_sem.at[apart],
        )
        copy.start()
        copies.append(
            [copy]
            + fetch_features(x_ref, x_all.at[apart], x_sem.at[apart], half, column, pos)
        )
    result = None
    for apart in range(planes):
        for copy in copies[apart]:
            copy.wait()
        term = jnp.dot(x_all[apart], w_all[apart], preferred_element_type=jnp.float32)
        result = term if result is None else result + term
    rows = x_ref.shape[1]
    for block in range(GROUP):
        kv_out[block] = result[block * rows : (block + 1) * rows]


def project_kv(scal, x, own_w, skip):
    planes = len(own_w)
    rows = x.shape[1]
    w_rows = own_w[0].shape[0]
    width = own_w[0].shape[1] - skip
    depth = w_rows if w_rows % HEAD_SIZE == 0 else GROUP * w_rows
    anywhere = pl.BlockSpec(memory_space=pl.ANY)
    return pl.pallas_call(
        functools.partial(project_kv_kernel, planes, skip),
        out_shape=jax.ShapeDtypeStruct((GROUP, rows, width), jnp.float32),
        in_specs=[pl.BlockSpec(memory_space=pltpu.SMEM)] + [anywhere] * (1 + planes),
        out_specs=pl.BlockSpec(memory_space=pltpu.VMEM),
        scratch_shapes=[
            pltpu.VMEM((planes, GROUP * rows, depth), jnp.bfloat16),
            pltpu.VMEM((planes, depth, width), jnp.bfloat16),
            pltpu.SemaphoreType.DMA((planes, GROUP)),
            pltpu.SemaphoreType.DMA((planes,)),
        ],
        compiler_params=pltpu.CompilerParams(vmem_limit_bytes=VMEM_LIMIT),
        cost_estimate=pl.CostEstimate(
            flops=2 * GROUP * rows * depth * planes * width,
            bytes_accessed=2 * depth * planes * (GROUP * rows + width),
            transcendentals=0,
        ),
    )(scal, x, *own_w)


def attend_kernel(first, width, aliased, *refs):
    scal, order = refs[:2]
    qs = refs[2:6]
    keys_mine, keys_theirs, vals_mine, vals_theirs, new_mine, new_theirs = refs[6:12]
    refs = refs[12 + int(aliased) :]
    out, k_all, v_all, vt_all, q_all, o_all, tops, totals, sums = refs[:9]
    kv_sem, new_sem, out_sem = refs[9:]
    pos, count = scal[1], scal[2]
    side = pos % 2
    rows = qs[0].shape[0]
    heads = width // HEAD_SIZE
    slots = order.shape[0]
    half_slots = slots // 2
    scale = HEAD_SIZE ** (-0.5) * math.log2(math.e)
    lanes = heads * rows

    def new_copy(new, kind, row, index):
        into = v_all if kind else k_all
        return pltpu.make_async_copy(
            new.at[kind], into.at[pl.ds(row, rows)], new_sem.at[index]
        )

    for kind in range(2):
        new_copy(new_mine, kind, 0, kind).start()

    @pl.when(side == 1)
    def _():
        for kind in range(2):
            new_copy(new_theirs, kind, rows, 2 + kind).start()

    lead = rows + side * rows

    def block_copies(j):
        slot = order[j]
        src_row = pl.multiple_of((slot % half_slots) * BLOCK_TOKENS, BLOCK_TOKENS)
        dst_row = pl.multiple_of(lead + j * BLOCK_TOKENS, BLOCK_TOKENS)
        near = (slot // half_slots) == side

        def pair(k_src, v_src):
            return (
                pltpu.make_async_copy(
                    k_src.at[pl.ds(src_row, BLOCK_TOKENS)],
                    k_all.at[pl.ds(dst_row, BLOCK_TOKENS)],
                    kv_sem.at[0, j],
                ),
                pltpu.make_async_copy(
                    v_src.at[pl.ds(src_row, BLOCK_TOKENS)],
                    v_all.at[pl.ds(dst_row, BLOCK_TOKENS)],
                    kv_sem.at[1, j],
                ),
            )

        return near, pair(keys_mine, vals_mine), pair(keys_theirs, vals_theirs)

    def start_block(j, carry):
        near, mine, theirs = block_copies(j)

        @pl.when(near)
        def _():
            for copy in mine:
                copy.start()

        @pl.when(jnp.logical_not(near))
        def _():
            for copy in theirs:
                copy.start()

        return carry

    def wait_block(j, carry):
        _, mine, _ = block_copies(j)
        for copy in mine:
            copy.wait()
        return carry

    def clear_block(j, carry):
        row = pl.multiple_of(rows + j * BLOCK_TOKENS, BLOCK_TOKENS)
        blank = jnp.zeros((BLOCK_TOKENS, HEAD_SIZE), jnp.bfloat16)
        k_all[pl.ds(row, BLOCK_TOKENS), :] = blank
        v_all[pl.ds(row, BLOCK_TOKENS), :] = blank
        return carry

    per_chunk = KEY_CHUNK // BLOCK_TOKENS
    blocks = count + side * (rows // BLOCK_TOKENS)
    full = blocks // per_chunk
    chunks = (blocks + per_chunk - 1) // per_chunk
    lax.fori_loop(0, count, start_block, 0)
    lax.fori_loop(blocks, chunks * per_chunk, clear_block, 0)
    for r in range(GROUP):
        for head in range(heads):
            q_all[r, pl.ds(head * rows, rows), :] = qs[r][:, pl.ds(head * HEAD_SIZE, HEAD_SIZE)]

    def turn_values(row, size):
        values = v_all[pl.ds(row, size), :].astype(jnp.float32)
        vt_all[:, pl.ds(row, size)] = values.T.astype(jnp.bfloat16)

    def fold(values, combine):
        parts = values.reshape(values.shape[0] // 8, 8, lanes)
        return combine(parts, axis=0)

    def absorb(row, size, allowed, fresh):
        keys = k_all[pl.ds(row, size), :]
        values = vt_all[:, pl.ds(row, size)]
        for r in range(GROUP):
            s = lax.dot_general(
                keys, q_all[r], (((1,), (1,)), ((), ())), preferred_element_type=jnp.float32
            )
            if allowed is not None:
                s = jnp.where(allowed, s, -1e30)
            top = jnp.max(fold(s, jnp.max), axis=0, keepdims=True)
            if not fresh:
                before = tops[r]
                top = jnp.maximum(before, top)
            weight = jnp.exp2((s - top) * scale)
            total = fold(weight, jnp.sum)
            mixed = jnp.dot(
                values, weight.astype(jnp.bfloat16), preferred_element_type=jnp.float32
            )
            if not fresh:
                shrink = jnp.exp2((before - top) * scale)
                total = total + totals[r] * shrink
                mixed = mixed + sums[r] * shrink
            tops[r] = top
            totals[r] = total
            sums[r] = mixed

    for kind in range(2):
        new_copy(new_mine, kind, 0, kind).wait()
    turn_values(0, rows)
    key = lax.broadcasted_iota(jnp.int32, (rows, lanes), 0)
    token = lax.broadcasted_iota(jnp.int32, (rows, lanes), 1) % rows
    absorb(0, rows, key <= token, True)

    @pl.when(side == 1)
    def _():
        for kind in range(2):
            new_copy(new_theirs, kind, rows, 2 + kind).wait()

    lax.fori_loop(0, count, wait_block, 0)

    def chunk_row(chunk):
        return pl.multiple_of(rows + chunk * KEY_CHUNK, BLOCK_TOKENS)

    def step(chunk, carry):
        turn_values(chunk_row(chunk), KEY_CHUNK)
        absorb(chunk_row(chunk), KEY_CHUNK, None, False)
        return carry

    lax.fori_loop(0, full, step, 0)

    @pl.when(chunks > full)
    def _():
        turn_values(chunk_row(full), KEY_CHUNK)
        key = lax.broadcasted_iota(jnp.int32, (KEY_CHUNK, lanes), 0)
        allowed = key < (blocks - full * per_chunk) * BLOCK_TOKENS
        absorb(chunk_row(full), KEY_CHUNK, allowed, False)

    group_cols = out.shape[1] // GROUP
    copies = []
    for r in range(GROUP):
        total = jnp.sum(totals[r], axis=0, keepdims=True)
        result = (sums[r] / total).T.astype(jnp.bfloat16)
        for head in range(heads):
            o_all[r, :, pl.ds(head * HEAD_SIZE, HEAD_SIZE)] = result[
                head * rows : (head + 1) * rows
            ]
        column = pl.multiple_of((pos ^ r) * group_cols + first, HEAD_SIZE)
        copy = pltpu.make_async_copy(
            o_all.at[r], out.at[:, pl.ds(column, width)], out_sem.at[r]
        )
        copy.start()
        copies.append(copy)
    for copy in copies:
        copy.wait()


def attend(scal, order, qs, caches, news, so_far, first, width, out_cols):
    rows = qs[0].shape[0]
    slots = order.shape[0]
    heads = width // HEAD_SIZE
    rest = rows + slots * BLOCK_TOKENS
    tokens = rows + -(-rest // KEY_CHUNK) * KEY_CHUNK
    anywhere = pl.BlockSpec(memory_space=pl.ANY)
    vmem = pl.BlockSpec(memory_space=pltpu.VMEM)
    smem = pl.BlockSpec(memory_space=pltpu.SMEM)
    operands = [scal, order, *qs, *caches, *news]
    in_specs = [smem] * 2 + [vmem] * 4 + [anywhere] * 6
    aliases = {}
    if so_far is not None:
        aliases = {len(operands): 0}
        operands.append(so_far)
        in_specs.append(anywhere)
    return pl.pallas_call(
        functools.partial(attend_kernel, first, width, so_far is not None),
        out_shape=jax.ShapeDtypeStruct((rows, out_cols), jnp.bfloat16),
        in_specs=in_specs,
        out_specs=anywhere,
        input_output_aliases=aliases,
        scratch_shapes=[
            pltpu.VMEM((tokens, HEAD_SIZE), jnp.bfloat16),
            pltpu.VMEM((tokens, HEAD_SIZE), jnp.bfloat16),
            pltpu.VMEM((HEAD_SIZE, tokens), jnp.bfloat16),
            pltpu.VMEM((GROUP, heads * rows, HEAD_SIZE), jnp.bfloat16),
            pltpu.VMEM((GROUP, rows, width), jnp.bfloat16),
            pltpu.VMEM((GROUP, 1, heads * rows), jnp.float32),
            pltpu.VMEM((GROUP, 8, heads * rows), jnp.float32),
            pltpu.VMEM((GROUP, HEAD_SIZE, heads * rows), jnp.float32),
            pltpu.SemaphoreType.DMA((2, slots)),
            pltpu.SemaphoreType.DMA((4,)),
            pltpu.SemaphoreType.DMA((GROUP,)),
        ],
        compiler_params=pltpu.CompilerParams(vmem_limit_bytes=VMEM_LIMIT),
        cost_estimate=pl.CostEstimate(
            flops=4 * GROUP * heads * rows * tokens * HEAD_SIZE,
            bytes_accessed=4 * tokens * HEAD_SIZE,
            transcendentals=GROUP * heads * rows * tokens,
        ),
    )(*operands)


def on_device(
    hidden,
    w_query,
    key_weight,
    value_weight,
    q_gain,
    key_norm_gain,
    earlier_keys,
    earlier_values,
    counts,
    place,
):
    planes = lax.axis_size("ctx") // GROUP
    ctx = lax.axis_index("ctx")
    plane = ctx // GROUP
    pos = ctx % GROUP
    rows = hidden.shape[0]
    w_rows = w_query.shape[0]
    group_cols = w_query.shape[1] // GROUP
    widths = (group_cols // 2, group_cols - group_cols // 2)

    x = lax.all_gather(hidden, ("ctx", "tp"), axis_index_groups=ring_members(planes))

    def columns_for(r):
        return lax.dynamic_slice(w_query, (0, group_cols * (pos ^ r)), (w_rows, group_cols))

    got = [swap(columns_for(r), r) for r in range(1, GROUP)]
    own_w = spread(jnp.concatenate([columns_for(0), key_weight, value_weight], axis=1), planes)
    far = planes // 2
    first_source = jnp.concatenate([piece[:, : widths[0]] for piece in got], axis=1)
    rest_first = spread(after(first_source, *own_w[: far + 1]), planes)
    second_source = jnp.concatenate([piece[:, widths[0] :] for piece in got], axis=1)
    rest_second = spread(after(second_source, rest_first[far], own_w[-1]), planes)

    count = lax.dynamic_index_in_dim(counts, ctx // 2, 0, keepdims=False)
    order = lax.dynamic_index_in_dim(place, ctx // 2, 0, keepdims=False)
    scal = jnp.stack([plane, pos, count]).astype(jnp.int32)
    spots = pos ^ jnp.arange(GROUP, dtype=jnp.int32)
    spot_counts = counts[plane * 2 + spots // 2]
    token_position = (
        spot_counts[:, None] * BLOCK_TOKENS
        + (spots % 2)[:, None] * rows
        + jnp.arange(rows, dtype=jnp.int32)[None, :]
    )
    cosine, sine = rope_tables(token_position.reshape(GROUP * rows))

    x_late = after(x, rest_first[far], own_w[-1])
    partial = project_kv(scal, x_late, own_w, group_cols)
    summed = partial[0]
    for r in range(1, GROUP):
        summed = summed + swap(partial[r], r)
    keys = summed[:, :HEAD_SIZE]
    mean = jnp.mean(keys * keys, axis=-1, keepdims=True)
    scaled = keys * lax.rsqrt(mean + 1e-06) * key_norm_gain
    turned = scaled * cosine[:rows] + jnp.roll(scaled, HEAD_SIZE // 2, axis=-1) * sine[:rows]
    keys_mine = turned.astype(jnp.bfloat16)
    values_mine = summed[:, HEAD_SIZE:].astype(jnp.bfloat16)
    new_mine = jnp.stack([keys_mine, values_mine])
    new_theirs = swap(new_mine, 1)

    earlier_keys, earlier_values = lax.optimization_barrier(
        (earlier_keys, earlier_values, x_late)
    )[:2]
    caches = (
        earlier_keys,
        swap(earlier_keys, 1),
        earlier_values,
        swap(earlier_values, 1),
    )
    news = (new_mine, new_theirs)
    gain = q_gain[None, :]

    def queries(scal, rest_w, first, width):
        q = project(scal, x_late, own_w, rest_w, cosine, sine, gain, first, width)
        return [q[0]] + [swap(q[r], r) for r in range(1, GROUP)]

    out_cols = w_query.shape[1]
    q_first = queries(scal, rest_first, 0, widths[0])
    scal = after(scal, rest_second[far])
    attended = attend(scal, order, q_first, caches, news, None, 0, widths[0], out_cols)
    scal = after(scal, attended)
    q_second = queries(scal, rest_second, widths[0], widths[1])
    attended = attend(
        scal, order, q_second, caches, news, attended, widths[0], widths[1], out_cols
    )
    return (attended, keys_mine, values_mine)


def solution(mesh):
    placed = (
        P("ctx", "tp"),
        P("ctx", "tp"),
        P("ctx", "tp"),
        P("ctx", "tp"),
        P(),
        P(),
        P("ctx", "tp"),
        P("ctx", "tp"),
        P(),
        P(),
    )
    return jax.shard_map(
        on_device,
        mesh=mesh,
        in_specs=placed,
        out_specs=(P("ctx", "tp"), P("ctx", "tp"), P("ctx", "tp")),
        check_vma=False,
    )
```

```python
import functools
import math

import jax
import jax.numpy as jnp
from jax import lax
from jax.experimental import pallas as pl
from jax.experimental.pallas import tpu as pltpu
from jax.sharding import PartitionSpec as P

HEAD_SIZE = 128
BLOCK_TOKENS = 128
GROUP = 4
KEY_CHUNK = 512
VMEM_LIMIT = 28 * 1024 * 1024


def swap(value, mask):
    pairs = [(source, source ^ mask) for source in range(lax.axis_size("ctx"))]
    return lax.ppermute(value, "ctx", pairs)


def swap_core(value):
    return lax.ppermute(value, "tp", [(0, 1), (1, 0)])


def after(value, *others):
    return lax.optimization_barrier((value, *others))[0]


def spread(own, planes):
    pieces = {0: own}
    bit = planes // 2
    while bit:
        for apart in list(pieces):
            pieces[apart ^ bit] = swap(pieces[apart], GROUP * bit)
        bit //= 2
    return [pieces[apart] for apart in range(planes)]


def rope_tables(token_position):
    half = HEAD_SIZE // 2
    freq = jnp.exp(jnp.arange(half, dtype=jnp.float32) * (-2.0 / HEAD_SIZE) * math.log(1000000.0))
    angle = token_position.astype(jnp.float32)[..., None] * freq
    cosine, sine = jnp.cos(angle), jnp.sin(angle)
    return (
        jnp.concatenate([cosine, cosine], axis=-1),
        jnp.concatenate([-sine, sine], axis=-1),
    )


def half_slot(scal, planes, apart):
    there = scal[0] ^ apart
    other = (there // (planes // 2)) ^ scal[3]
    return other * (planes // 2) + there % (planes // 2)


def project_kernel(planes, first, width, *refs):
    scal, refs = refs[0], refs[1:]
    xs, refs = refs[:10], refs[10:]
    own_w, rest_w, refs = refs[:planes], refs[planes : 2 * planes], refs[2 * planes :]
    cosine, sine, gain, q_out, w_all, w_sem = refs
    pos = scal[1]
    half_cols = xs[0].shape[1]
    w_rows = own_w[0].shape[0]

    copies = []
    for apart in range(planes):
        base = half_slot(scal, planes, apart) * GROUP
        for r in range(GROUP):
            if r == 0:
                src = own_w[apart].at[:, pl.ds(first, width)]
            else:
                src = rest_w[apart].at[:, pl.ds((r - 1) * width, width)]
            row = pl.multiple_of((base + (pos ^ r)) * w_rows, w_rows)
            copy = pltpu.make_async_copy(
                src, w_all.at[pl.ds(row, w_rows)], w_sem.at[apart, r]
            )
            copy.start()
            copies.append(copy)
    for copy in copies:
        copy.wait()

    begin = 0
    for part in range(5):
        size = xs[part].shape[0]
        result = jnp.dot(
            xs[part][...], w_all[pl.ds(0, half_cols), :], preferred_element_type=jnp.float32
        ) + jnp.dot(
            xs[5 + part][...],
            w_all[pl.ds(half_cols, half_cols), :],
            preferred_element_type=jnp.float32,
        )
        tokens = pl.ds(begin, size)
        for head in range(width // HEAD_SIZE):
            values = result[:, head * HEAD_SIZE : (head + 1) * HEAD_SIZE]
            mean = jnp.mean(values * values, axis=-1, keepdims=True)
            scaled = values * lax.rsqrt(mean + 1e-06) * gain[...]
            turned = (
                scaled * cosine[tokens, :]
                + pltpu.roll(scaled, HEAD_SIZE // 2, 1) * sine[tokens, :]
            )
            q_out[tokens, pl.ds(head * HEAD_SIZE, HEAD_SIZE)] = turned.astype(jnp.bfloat16)
        begin += size


def project(scal, xs, own_w, rest_w, cosine, sine, gain, first, width):
    planes = len(own_w)
    rows, half_cols = xs[0].shape
    depth = 2 * half_cols
    anywhere = pl.BlockSpec(memory_space=pl.ANY)
    vmem = pl.BlockSpec(memory_space=pltpu.VMEM)
    return pl.pallas_call(
        functools.partial(project_kernel, planes, first, width),
        out_shape=jax.ShapeDtypeStruct((GROUP * rows, width), jnp.bfloat16),
        in_specs=[pl.BlockSpec(memory_space=pltpu.SMEM)]
        + [vmem] * 10
        + [anywhere] * (2 * planes)
        + [vmem] * 3,
        out_specs=vmem,
        scratch_shapes=[
            pltpu.VMEM((depth, width), jnp.bfloat16),
            pltpu.SemaphoreType.DMA((planes, GROUP)),
        ],
        compiler_params=pltpu.CompilerParams(vmem_limit_bytes=VMEM_LIMIT),
        cost_estimate=pl.CostEstimate(
            flops=2 * GROUP * rows * depth * width,
            bytes_accessed=2 * depth * (GROUP * rows + width),
            transcendentals=0,
        ),
    )(scal, *xs, *own_w, *rest_w, cosine, sine, gain)


def project_kv_kernel(planes, skip, *refs):
    scal, refs = refs[0], refs[1:]
    xs, own_w, refs = refs[:10], refs[10 : 10 + planes], refs[10 + planes :]
    kv_out, x_all, w_all, x_sem, w_sem = refs
    pos = scal[1]
    w_rows = own_w[0].shape[0]
    _, depth, width = w_all.shape
    compact = depth == w_rows
    offset = pos * w_rows if compact else 0

    copies = []
    for apart in range(planes):
        slot = half_slot(scal, planes, apart)
        row = 0
        if not compact:
            w_all[slot] = jnp.zeros((depth, width), jnp.bfloat16)
            row = pl.multiple_of(pos * w_rows, w_rows)
        copy = pltpu.make_async_copy(
            own_w[apart].at[:, pl.ds(skip, width)],
            w_all.at[slot, pl.ds(row, w_rows)],
            w_sem.at[apart],
        )
        copy.start()
        copies.append(copy)
    for slot in range(planes):
        half, within = slot // (planes // 2), slot % (planes // 2)
        column = pl.multiple_of(within * GROUP * w_rows + offset, HEAD_SIZE)
        begin = 0
        for part in range(5):
            src = xs[5 * half + part]
            copy = pltpu.make_async_copy(
                src.at[:, pl.ds(column, depth)],
                x_all.at[slot, pl.ds(begin, src.shape[0])],
                x_sem.at[slot, part],
            )
            copy.start()
            copies.append(copy)
            begin += src.shape[0]
    for copy in copies:
        copy.wait()
    result = None
    for slot in range(planes):
        term = jnp.dot(x_all[slot], w_all[slot], preferred_element_type=jnp.float32)
        result = term if result is None else result + term
    kv_out[...] = result


def project_kv(scal, xs, own_w, skip):
    planes = len(own_w)
    rows = xs[0].shape[0]
    w_rows = own_w[0].shape[0]
    width = own_w[0].shape[1] - skip
    depth = w_rows if w_rows % HEAD_SIZE == 0 else GROUP * w_rows
    anywhere = pl.BlockSpec(memory_space=pl.ANY)
    return pl.pallas_call(
        functools.partial(project_kv_kernel, planes, skip),
        out_shape=jax.ShapeDtypeStruct((GROUP * rows, width), jnp.float32),
        in_specs=[pl.BlockSpec(memory_space=pltpu.SMEM)] + [anywhere] * (10 + planes),
        out_specs=pl.BlockSpec(memory_space=pltpu.VMEM),
        scratch_shapes=[
            pltpu.VMEM((planes, GROUP * rows, depth), jnp.bfloat16),
            pltpu.VMEM((planes, depth, width), jnp.bfloat16),
            pltpu.SemaphoreType.DMA((planes, 5)),
            pltpu.SemaphoreType.DMA((planes,)),
        ],
        compiler_params=pltpu.CompilerParams(vmem_limit_bytes=VMEM_LIMIT),
        cost_estimate=pl.CostEstimate(
            flops=2 * GROUP * rows * depth * planes * width,
            bytes_accessed=2 * depth * planes * (GROUP * rows + width),
            transcendentals=0,
        ),
    )(scal, *xs, *own_w)


def attend_kernel(first, width, aliased, *refs):
    scal, order = refs[:2]
    qs = refs[2:6]
    keys_mine, keys_theirs, vals_mine, vals_theirs, new_mine, new_theirs = refs[6:12]
    refs = refs[12 + int(aliased) :]
    out, k_all, v_all, vt_all, q_all, o_all, tops, totals, sums = refs[:9]
    kv_sem, new_sem, out_sem = refs[9:]
    pos, count = scal[1], scal[2]
    side = pos % 2
    rows = qs[0].shape[0]
    heads = width // HEAD_SIZE
    slots = order.shape[0]
    half_slots = slots // 2
    scale = HEAD_SIZE ** (-0.5) * math.log2(math.e)
    units = GROUP * heads
    lanes = rows

    def new_copy(new, kind, row, index):
        into = v_all if kind else k_all
        return pltpu.make_async_copy(
            new.at[kind], into.at[pl.ds(row, rows)], new_sem.at[index]
        )

    for kind in range(2):
        new_copy(new_mine, kind, 0, kind).start()

    @pl.when(side == 1)
    def _():
        for kind in range(2):
            new_copy(new_theirs, kind, rows, 2 + kind).start()

    lead = rows + side * rows

    def block_copies(j):
        slot = order[j]
        src_row = pl.multiple_of((slot % half_slots) * BLOCK_TOKENS, BLOCK_TOKENS)
        dst_row = pl.multiple_of(lead + j * BLOCK_TOKENS, BLOCK_TOKENS)
        near = (slot // half_slots) == side

        def pair(k_src, v_src):
            return (
                pltpu.make_async_copy(
                    k_src.at[pl.ds(src_row, BLOCK_TOKENS)],
                    k_all.at[pl.ds(dst_row, BLOCK_TOKENS)],
                    kv_sem.at[0, j],
                ),
                pltpu.make_async_copy(
                    v_src.at[pl.ds(src_row, BLOCK_TOKENS)],
                    v_all.at[pl.ds(dst_row, BLOCK_TOKENS)],
                    kv_sem.at[1, j],
                ),
            )

        return near, pair(keys_mine, vals_mine), pair(keys_theirs, vals_theirs)

    def start_block(j, carry):
        near, mine, theirs = block_copies(j)

        @pl.when(near)
        def _():
            for copy in mine:
                copy.start()

        @pl.when(jnp.logical_not(near))
        def _():
            for copy in theirs:
                copy.start()

        return carry

    def wait_block(j, carry):
        _, mine, _ = block_copies(j)
        for copy in mine:
            copy.wait()
        return carry

    def clear_block(j, carry):
        row = pl.multiple_of(rows + j * BLOCK_TOKENS, BLOCK_TOKENS)
        blank = jnp.zeros((BLOCK_TOKENS, HEAD_SIZE), jnp.bfloat16)
        k_all[pl.ds(row, BLOCK_TOKENS), :] = blank
        v_all[pl.ds(row, BLOCK_TOKENS), :] = blank
        return carry

    per_chunk = KEY_CHUNK // BLOCK_TOKENS
    blocks = count + side * (rows // BLOCK_TOKENS)
    full = blocks // per_chunk
    chunks = (blocks + per_chunk - 1) // per_chunk
    lax.fori_loop(0, count, start_block, 0)
    lax.fori_loop(blocks, chunks * per_chunk, clear_block, 0)
    for r in range(GROUP):
        for head in range(heads):
            q_all[r * heads + head] = qs[r][:, pl.ds(head * HEAD_SIZE, HEAD_SIZE)]

    def turn_values(row, size):
        values = v_all[pl.ds(row, size), :].astype(jnp.float32)
        vt_all[:, pl.ds(row, size)] = values.T.astype(jnp.bfloat16)

    def fold(values, combine):
        parts = values.reshape(values.shape[0] // 8, 8, lanes)
        return combine(parts, axis=0)

    def absorb(row, size, allowed, fresh):
        keys = k_all[pl.ds(row, size), :]
        values = vt_all[:, pl.ds(row, size)]

        def score(unit):
            return lax.dot_general(
                keys, q_all[unit], (((1,), (1,)), ((), ())), preferred_element_type=jnp.float32
            )

        ahead = score(0)
        for unit in range(units):
            s = ahead
            if unit + 1 < units:
                ahead = score(unit + 1)
            if allowed is not None:
                s = jnp.where(allowed, s, -1e30)
            top = jnp.max(fold(s, jnp.max), axis=0, keepdims=True)
            if not fresh:
                before = tops[unit]
                top = jnp.maximum(before, top)
            weight = jnp.exp2((s - top) * scale)
            total = fold(weight, jnp.sum)
            mixed = jnp.dot(
                values, weight.astype(jnp.bfloat16), preferred_element_type=jnp.float32
            )
            if not fresh:
                shrink = jnp.exp2((before - top) * scale)
                total = total + totals[unit] * shrink
                mixed = mixed + sums[unit] * shrink
            tops[unit] = top
            totals[unit] = total
            sums[unit] = mixed

    for kind in range(2):
        new_copy(new_mine, kind, 0, kind).wait()
    turn_values(0, rows)
    key = lax.broadcasted_iota(jnp.int32, (rows, lanes), 0)
    token = lax.broadcasted_iota(jnp.int32, (rows, lanes), 1)
    absorb(0, rows, key <= token, True)

    @pl.when(side == 1)
    def _():
        for kind in range(2):
            new_copy(new_theirs, kind, rows, 2 + kind).wait()

    lax.fori_loop(0, count, wait_block, 0)

    def chunk_row(chunk):
        return pl.multiple_of(rows + chunk * KEY_CHUNK, BLOCK_TOKENS)

    def step(chunk, carry):
        turn_values(chunk_row(chunk), KEY_CHUNK)
        absorb(chunk_row(chunk), KEY_CHUNK, None, False)
        return carry

    lax.fori_loop(0, full, step, 0)

    @pl.when(chunks > full)
    def _():
        turn_values(chunk_row(full), KEY_CHUNK)
        key = lax.broadcasted_iota(jnp.int32, (KEY_CHUNK, lanes), 0)
        allowed = key < (blocks - full * per_chunk) * BLOCK_TOKENS
        absorb(chunk_row(full), KEY_CHUNK, allowed, False)

    group_cols = out.shape[1] // GROUP
    copies = []
    for r in range(GROUP):
        for head in range(heads):
            unit = r * heads + head
            total = jnp.sum(totals[unit], axis=0, keepdims=True)
            result = (sums[unit] / total).T.astype(jnp.bfloat16)
            o_all[r, :, pl.ds(head * HEAD_SIZE, HEAD_SIZE)] = result
        column = pl.multiple_of((pos ^ r) * group_cols + first, HEAD_SIZE)
        copy = pltpu.make_async_copy(
            o_all.at[r], out.at[:, pl.ds(column, width)], out_sem.at[r]
        )
        copy.start()
        copies.append(copy)
    for copy in copies:
        copy.wait()


def attend(scal, order, qs, caches, news, so_far, first, width, out_cols):
    rows = qs[0].shape[0]
    slots = order.shape[0]
    heads = width // HEAD_SIZE
    rest = rows + slots * BLOCK_TOKENS
    tokens = rows + -(-rest // KEY_CHUNK) * KEY_CHUNK
    anywhere = pl.BlockSpec(memory_space=pl.ANY)
    vmem = pl.BlockSpec(memory_space=pltpu.VMEM)
    smem = pl.BlockSpec(memory_space=pltpu.SMEM)
    operands = [scal, order, *qs, *caches, *news]
    in_specs = [smem] * 2 + [vmem] * 4 + [anywhere] * 6
    aliases = {}
    if so_far is not None:
        aliases = {len(operands): 0}
        operands.append(so_far)
        in_specs.append(anywhere)
    return pl.pallas_call(
        functools.partial(attend_kernel, first, width, so_far is not None),
        out_shape=jax.ShapeDtypeStruct((rows, out_cols), jnp.bfloat16),
        in_specs=in_specs,
        out_specs=anywhere,
        input_output_aliases=aliases,
        scratch_shapes=[
            pltpu.VMEM((tokens, HEAD_SIZE), jnp.bfloat16),
            pltpu.VMEM((tokens, HEAD_SIZE), jnp.bfloat16),
            pltpu.VMEM((HEAD_SIZE, tokens), jnp.bfloat16),
            pltpu.VMEM((GROUP * heads, rows, HEAD_SIZE), jnp.bfloat16),
            pltpu.VMEM((GROUP, rows, width), jnp.bfloat16),
            pltpu.VMEM((GROUP * heads, 1, rows), jnp.float32),
            pltpu.VMEM((GROUP * heads, 8, rows), jnp.float32),
            pltpu.VMEM((GROUP * heads, HEAD_SIZE, rows), jnp.float32),
            pltpu.SemaphoreType.DMA((2, slots)),
            pltpu.SemaphoreType.DMA((4,)),
            pltpu.SemaphoreType.DMA((GROUP,)),
        ],
        compiler_params=pltpu.CompilerParams(vmem_limit_bytes=VMEM_LIMIT),
        cost_estimate=pl.CostEstimate(
            flops=4 * GROUP * heads * rows * tokens * HEAD_SIZE,
            bytes_accessed=4 * tokens * HEAD_SIZE,
            transcendentals=GROUP * heads * rows * tokens,
        ),
    )(*operands)


def on_device(
    hidden,
    w_query,
    key_weight,
    value_weight,
    q_gain,
    key_norm_gain,
    earlier_keys,
    earlier_values,
    counts,
    place,
):
    planes = lax.axis_size("ctx") // GROUP
    ctx = lax.axis_index("ctx")
    plane = ctx // GROUP
    pos = ctx % GROUP
    rows = hidden.shape[0]
    w_rows = w_query.shape[0]
    group_cols = w_query.shape[1] // GROUP
    widths = (group_cols // 2, group_cols - group_cols // 2)

    def columns_for(r):
        return lax.dynamic_slice(w_query, (0, group_cols * (pos ^ r)), (w_rows, group_cols))

    got = [swap(columns_for(r), r) for r in range(1, GROUP)]
    own_w = spread(jnp.concatenate([columns_for(0), key_weight, value_weight], axis=1), planes)
    far = planes // 2

    half_rows = rows // 2
    x_1 = swap(hidden, 1)
    x_2 = swap(hidden, 2)
    x_mine = [hidden, x_1, x_2, swap(x_2[:half_rows], 1), swap(x_1[half_rows:], 2)]
    xs = x_mine + [swap_core(x) for x in x_mine]

    first_source = jnp.concatenate([piece[:, : widths[0]] for piece in got], axis=1)
    rest_first = spread(after(first_source, *own_w[: far + 1]), planes)
    second_source = jnp.concatenate([piece[:, widths[0] :] for piece in got], axis=1)
    rest_second = spread(after(second_source, rest_first[far], own_w[-1]), planes)

    count = lax.dynamic_index_in_dim(counts, ctx // 2, 0, keepdims=False)
    order = lax.dynamic_index_in_dim(place, ctx // 2, 0, keepdims=False)
    scal = jnp.stack([plane, pos, count, lax.axis_index("tp")]).astype(jnp.int32)
    spots = pos ^ jnp.arange(GROUP, dtype=jnp.int32)
    spot_counts = counts[plane * 2 + spots // 2]
    token_position = (
        spot_counts[:, None] * BLOCK_TOKENS
        + (spots % 2)[:, None] * rows
        + jnp.arange(rows, dtype=jnp.int32)[None, :]
    )
    cosine, sine = rope_tables(token_position.reshape(GROUP * rows))

    partial = project_kv(scal, xs, own_w, group_cols).reshape(GROUP, rows, 2 * HEAD_SIZE)
    summed = partial[0]
    for r in range(1, GROUP):
        summed = summed + swap(partial[r], r)
    keys = summed[:, :HEAD_SIZE]
    mean = jnp.mean(keys * keys, axis=-1, keepdims=True)
    scaled = keys * lax.rsqrt(mean + 1e-06) * key_norm_gain
    turned = scaled * cosine[:rows] + jnp.roll(scaled, HEAD_SIZE // 2, axis=-1) * sine[:rows]
    keys_mine = turned.astype(jnp.bfloat16)
    values_mine = summed[:, HEAD_SIZE:].astype(jnp.bfloat16)
    new_mine = jnp.stack([keys_mine, values_mine])
    new_theirs = swap(new_mine, 1)

    earlier_keys, earlier_values = lax.optimization_barrier(
        (earlier_keys, earlier_values, *x_mine)
    )[:2]
    caches = (
        earlier_keys,
        swap(earlier_keys, 1),
        earlier_values,
        swap(earlier_values, 1),
    )
    news = (new_mine, new_theirs)
    gain = q_gain[None, :]

    def queries(scal, rest_w, first, width):
        q = project(scal, xs, own_w, rest_w, cosine, sine, gain, first, width)
        q = q.reshape(GROUP, rows, width)
        return [q[0]] + [swap(q[r], r) for r in range(1, GROUP)]

    out_cols = w_query.shape[1]
    q_first = queries(
        after(scal, rest_second[far], *caches), rest_first, 0, widths[0]
    )
    q_second = queries(after(scal, q_first[0]), rest_second, widths[0], widths[1])
    attended = attend(
        after(scal, q_second[0]), order, q_first, caches, news, None, 0, widths[0], out_cols
    )
    attended = attend(
        scal, order, q_second, caches, news, attended, widths[0], widths[1], out_cols
    )
    return (attended, keys_mine, values_mine)


def solution(mesh):
    placed = (
        P("ctx", "tp"),
        P("ctx", "tp"),
        P("ctx", "tp"),
        P("ctx", "tp"),
        P(),
        P(),
        P("ctx", "tp"),
        P("ctx", "tp"),
        P(),
        P(),
    )
    return jax.shard_map(
        on_device,
        mesh=mesh,
        in_specs=placed,
        out_specs=(P("ctx", "tp"), P("ctx", "tp"), P("ctx", "tp")),
        check_vma=False,
    )
```

```python
import functools
import math

import jax
import jax.numpy as jnp
from jax import lax
from jax.experimental import pallas as pl
from jax.experimental.pallas import tpu as pltpu
from jax.sharding import PartitionSpec as P

HEAD_SIZE = 128
BLOCK_TOKENS = 128
GROUP = 4
KEY_CHUNK = 512
VMEM_LIMIT = 28 * 1024 * 1024


def swap(value, mask):
    pairs = [(source, source ^ mask) for source in range(lax.axis_size("ctx"))]
    return lax.ppermute(value, "ctx", pairs)


def swap_core(value):
    return lax.ppermute(value, "tp", [(0, 1), (1, 0)])


def after(value, *others):
    return lax.optimization_barrier((value, *others))[0]


def spread(own, planes):
    pieces = {0: own}
    bit = planes // 2
    while bit:
        for apart in list(pieces):
            pieces[apart ^ bit] = swap(pieces[apart], GROUP * bit)
        bit //= 2
    return [pieces[apart] for apart in range(planes)]


def rope_tables(token_position):
    half = HEAD_SIZE // 2
    freq = jnp.exp(jnp.arange(half, dtype=jnp.float32) * (-2.0 / HEAD_SIZE) * math.log(1000000.0))
    angle = token_position.astype(jnp.float32)[..., None] * freq
    cosine, sine = jnp.cos(angle), jnp.sin(angle)
    return (
        jnp.concatenate([cosine, cosine], axis=-1),
        jnp.concatenate([-sine, sine], axis=-1),
    )


def half_slot(scal, planes, apart):
    there = scal[0] ^ apart
    other = (there // (planes // 2)) ^ scal[3]
    return other * (planes // 2) + there % (planes // 2)


def project_kernel(planes, first, width, *refs):
    scal, refs = refs[0], refs[1:]
    xs, refs = refs[:6], refs[6:]
    own_w, rest_w, refs = refs[:planes], refs[planes : 2 * planes], refs[2 * planes :]
    cosine, sine, gain, q_out, w_all, w_sem = refs
    pos = scal[1]
    half_cols = xs[0].shape[1]
    w_rows = own_w[0].shape[0]

    copies = []
    for apart in range(planes):
        base = half_slot(scal, planes, apart) * GROUP
        for r in range(GROUP):
            if r == 0:
                src = own_w[apart].at[:, pl.ds(first, width)]
            else:
                src = rest_w[apart].at[:, pl.ds((r - 1) * width, width)]
            row = pl.multiple_of((base + (pos ^ r)) * w_rows, w_rows)
            copy = pltpu.make_async_copy(
                src, w_all.at[pl.ds(row, w_rows)], w_sem.at[apart, r]
            )
            copy.start()
            copies.append(copy)
    for copy in copies:
        copy.wait()

    begin = 0
    for part in range(3):
        size = xs[part].shape[0]
        result = jnp.dot(
            xs[part][...], w_all[pl.ds(0, half_cols), :], preferred_element_type=jnp.float32
        ) + jnp.dot(
            xs[3 + part][...],
            w_all[pl.ds(half_cols, half_cols), :],
            preferred_element_type=jnp.float32,
        )
        tokens = pl.ds(begin, size)
        for head in range(width // HEAD_SIZE):
            values = result[:, head * HEAD_SIZE : (head + 1) * HEAD_SIZE]
            mean = jnp.mean(values * values, axis=-1, keepdims=True)
            scaled = values * lax.rsqrt(mean + 1e-06) * gain[...]
            turned = (
                scaled * cosine[tokens, :]
                + pltpu.roll(scaled, HEAD_SIZE // 2, 1) * sine[tokens, :]
            )
            q_out[tokens, pl.ds(head * HEAD_SIZE, HEAD_SIZE)] = turned.astype(jnp.bfloat16)
        begin += size


def project(scal, xs, own_w, rest_w, cosine, sine, gain, first, width):
    planes = len(own_w)
    rows, half_cols = xs[0].shape
    depth = 2 * half_cols
    anywhere = pl.BlockSpec(memory_space=pl.ANY)
    vmem = pl.BlockSpec(memory_space=pltpu.VMEM)
    return pl.pallas_call(
        functools.partial(project_kernel, planes, first, width),
        out_shape=jax.ShapeDtypeStruct((GROUP * rows, width), jnp.bfloat16),
        in_specs=[pl.BlockSpec(memory_space=pltpu.SMEM)]
        + [vmem] * 6
        + [anywhere] * (2 * planes)
        + [vmem] * 3,
        out_specs=vmem,
        scratch_shapes=[
            pltpu.VMEM((depth, width), jnp.bfloat16),
            pltpu.SemaphoreType.DMA((planes, GROUP)),
        ],
        compiler_params=pltpu.CompilerParams(vmem_limit_bytes=VMEM_LIMIT),
        cost_estimate=pl.CostEstimate(
            flops=2 * GROUP * rows * depth * width,
            bytes_accessed=2 * depth * (GROUP * rows + width),
            transcendentals=0,
        ),
    )(scal, *xs, *own_w, *rest_w, cosine, sine, gain)


def project_kv_kernel(planes, skip, *refs):
    scal, refs = refs[0], refs[1:]
    xs, own_w, refs = refs[:6], refs[6 : 6 + planes], refs[6 + planes :]
    kv_out, x_all, w_all, x_sem, w_sem = refs
    pos = scal[1]
    w_rows = own_w[0].shape[0]
    _, depth, width = w_all.shape
    compact = depth == w_rows
    offset = pos * w_rows if compact else 0

    copies = []
    for apart in range(planes):
        slot = half_slot(scal, planes, apart)
        row = 0
        if not compact:
            w_all[slot] = jnp.zeros((depth, width), jnp.bfloat16)
            row = pl.multiple_of(pos * w_rows, w_rows)
        copy = pltpu.make_async_copy(
            own_w[apart].at[:, pl.ds(skip, width)],
            w_all.at[slot, pl.ds(row, w_rows)],
            w_sem.at[apart],
        )
        copy.start()
        copies.append(copy)
    for slot in range(planes):
        half, within = slot // (planes // 2), slot % (planes // 2)
        column = pl.multiple_of(within * GROUP * w_rows + offset, HEAD_SIZE)
        begin = 0
        for part in range(3):
            src = xs[3 * half + part]
            copy = pltpu.make_async_copy(
                src.at[:, pl.ds(column, depth)],
                x_all.at[slot, pl.ds(begin, src.shape[0])],
                x_sem.at[slot, part],
            )
            copy.start()
            copies.append(copy)
            begin += src.shape[0]
    for copy in copies:
        copy.wait()
    result = None
    for slot in range(planes):
        term = jnp.dot(x_all[slot], w_all[slot], preferred_element_type=jnp.float32)
        result = term if result is None else result + term
    kv_out[...] = result


def project_kv(scal, xs, own_w, skip):
    planes = len(own_w)
    rows = xs[0].shape[0]
    w_rows = own_w[0].shape[0]
    width = own_w[0].shape[1] - skip
    depth = w_rows if w_rows % HEAD_SIZE == 0 else GROUP * w_rows
    anywhere = pl.BlockSpec(memory_space=pl.ANY)
    return pl.pallas_call(
        functools.partial(project_kv_kernel, planes, skip),
        out_shape=jax.ShapeDtypeStruct((GROUP * rows, width), jnp.float32),
        in_specs=[pl.BlockSpec(memory_space=pltpu.SMEM)] + [anywhere] * (6 + planes),
        out_specs=pl.BlockSpec(memory_space=pltpu.VMEM),
        scratch_shapes=[
            pltpu.VMEM((planes, GROUP * rows, depth), jnp.bfloat16),
            pltpu.VMEM((planes, depth, width), jnp.bfloat16),
            pltpu.SemaphoreType.DMA((planes, 3)),
            pltpu.SemaphoreType.DMA((planes,)),
        ],
        compiler_params=pltpu.CompilerParams(vmem_limit_bytes=VMEM_LIMIT),
        cost_estimate=pl.CostEstimate(
            flops=2 * GROUP * rows * depth * planes * width,
            bytes_accessed=2 * depth * planes * (GROUP * rows + width),
            transcendentals=0,
        ),
    )(scal, *xs, *own_w)


def attend_kernel(first, width, aliased, *refs):
    scal, order = refs[:2]
    qs = refs[2:6]
    cache_mine, cache_theirs, new_mine, new_theirs = refs[6:10]
    refs = refs[10 + int(aliased) :]
    out, k_all, v_all, vt_all, q_all, o_all, tops, totals, sums = refs[:9]
    kv_sem, new_sem, out_sem = refs[9:]
    pos, count = scal[1], scal[2]
    side = pos % 2
    rows = qs[0].shape[0]
    heads = width // HEAD_SIZE
    slots = order.shape[0]
    half_slots = slots // 2
    scale = HEAD_SIZE ** (-0.5) * math.log2(math.e)
    units = GROUP * heads
    lanes = rows

    def new_copy(new, kind, row, index):
        into = v_all if kind else k_all
        return pltpu.make_async_copy(
            new.at[kind], into.at[pl.ds(row, rows)], new_sem.at[index]
        )

    for kind in range(2):
        new_copy(new_mine, kind, 0, kind).start()

    @pl.when(side == 1)
    def _():
        for kind in range(2):
            new_copy(new_theirs, kind, rows, 2 + kind).start()

    lead = rows + side * rows

    def block_copies(j):
        slot = order[j]
        src_row = pl.multiple_of((slot % half_slots) * BLOCK_TOKENS, BLOCK_TOKENS)
        dst_row = pl.multiple_of(lead + j * BLOCK_TOKENS, BLOCK_TOKENS)
        near = (slot // half_slots) == side

        def pair(cache):
            return (
                pltpu.make_async_copy(
                    cache.at[0, pl.ds(src_row, BLOCK_TOKENS)],
                    k_all.at[pl.ds(dst_row, BLOCK_TOKENS)],
                    kv_sem.at[0, j],
                ),
                pltpu.make_async_copy(
                    cache.at[1, pl.ds(src_row, BLOCK_TOKENS)],
                    v_all.at[pl.ds(dst_row, BLOCK_TOKENS)],
                    kv_sem.at[1, j],
                ),
            )

        return near, pair(cache_mine), pair(cache_theirs)

    def start_block(j, carry):
        near, mine, theirs = block_copies(j)

        @pl.when(near)
        def _():
            for copy in mine:
                copy.start()

        @pl.when(jnp.logical_not(near))
        def _():
            for copy in theirs:
                copy.start()

        return carry

    def wait_block(j, carry):
        _, mine, _ = block_copies(j)
        for copy in mine:
            copy.wait()
        return carry

    def clear_block(j, carry):
        row = pl.multiple_of(rows + j * BLOCK_TOKENS, BLOCK_TOKENS)
        blank = jnp.zeros((BLOCK_TOKENS, HEAD_SIZE), jnp.bfloat16)
        k_all[pl.ds(row, BLOCK_TOKENS), :] = blank
        v_all[pl.ds(row, BLOCK_TOKENS), :] = blank
        return carry

    per_chunk = KEY_CHUNK // BLOCK_TOKENS
    blocks = count + side * (rows // BLOCK_TOKENS)
    full = blocks // per_chunk
    chunks = (blocks + per_chunk - 1) // per_chunk
    lax.fori_loop(0, count, start_block, 0)
    lax.fori_loop(blocks, chunks * per_chunk, clear_block, 0)
    for r in range(GROUP):
        for head in range(heads):
            q_all[r * heads + head] = qs[r][:, pl.ds(head * HEAD_SIZE, HEAD_SIZE)]

    def turn_values(row, size):
        values = v_all[pl.ds(row, size), :].astype(jnp.float32)
        vt_all[:, pl.ds(row, size)] = values.T.astype(jnp.bfloat16)

    def fold(values, combine):
        parts = values.reshape(values.shape[0] // 8, 8, lanes)
        return combine(parts, axis=0)

    def absorb(row, size, allowed, fresh):
        keys = k_all[pl.ds(row, size), :]
        values = vt_all[:, pl.ds(row, size)]

        def score(unit):
            return lax.dot_general(
                keys, q_all[unit], (((1,), (1,)), ((), ())), preferred_element_type=jnp.float32
            )

        ahead = score(0)
        for unit in range(units):
            s = ahead
            if unit + 1 < units:
                ahead = score(unit + 1)
            if allowed is not None:
                s = jnp.where(allowed, s, -1e30)
            top = jnp.max(fold(s, jnp.max), axis=0, keepdims=True)
            if not fresh:
                before = tops[unit]
                top = jnp.maximum(before, top)
            weight = jnp.exp2((s - top) * scale)
            total = fold(weight, jnp.sum)
            mixed = jnp.dot(
                values, weight.astype(jnp.bfloat16), preferred_element_type=jnp.float32
            )
            if not fresh:
                shrink = jnp.exp2((before - top) * scale)
                total = total + totals[unit] * shrink
                mixed = mixed + sums[unit] * shrink
            tops[unit] = top
            totals[unit] = total
            sums[unit] = mixed

    for kind in range(2):
        new_copy(new_mine, kind, 0, kind).wait()
    turn_values(0, rows)
    key = lax.broadcasted_iota(jnp.int32, (rows, lanes), 0)
    token = lax.broadcasted_iota(jnp.int32, (rows, lanes), 1)
    absorb(0, rows, key <= token, True)

    @pl.when(side == 1)
    def _():
        for kind in range(2):
            new_copy(new_theirs, kind, rows, 2 + kind).wait()

    lax.fori_loop(0, count, wait_block, 0)

    def chunk_row(chunk):
        return pl.multiple_of(rows + chunk * KEY_CHUNK, BLOCK_TOKENS)

    def step(chunk, carry):
        turn_values(chunk_row(chunk), KEY_CHUNK)
        absorb(chunk_row(chunk), KEY_CHUNK, None, False)
        return carry

    lax.fori_loop(0, full, step, 0)

    @pl.when(chunks > full)
    def _():
        turn_values(chunk_row(full), KEY_CHUNK)
        key = lax.broadcasted_iota(jnp.int32, (KEY_CHUNK, lanes), 0)
        allowed = key < (blocks - full * per_chunk) * BLOCK_TOKENS
        absorb(chunk_row(full), KEY_CHUNK, allowed, False)

    group_cols = out.shape[1] // GROUP
    copies = []
    for r in range(GROUP):
        for head in range(heads):
            unit = r * heads + head
            total = jnp.sum(totals[unit], axis=0, keepdims=True)
            result = (sums[unit] / total).T.astype(jnp.bfloat16)
            o_all[r, :, pl.ds(head * HEAD_SIZE, HEAD_SIZE)] = result
        column = pl.multiple_of((pos ^ r) * group_cols + first, HEAD_SIZE)
        copy = pltpu.make_async_copy(
            o_all.at[r], out.at[:, pl.ds(column, width)], out_sem.at[r]
        )
        copy.start()
        copies.append(copy)
    for copy in copies:
        copy.wait()


def attend(scal, order, qs, caches, news, so_far, first, width, out_cols):
    rows = qs[0].shape[0]
    slots = order.shape[0]
    heads = width // HEAD_SIZE
    rest = rows + slots * BLOCK_TOKENS
    tokens = rows + -(-rest // KEY_CHUNK) * KEY_CHUNK
    anywhere = pl.BlockSpec(memory_space=pl.ANY)
    vmem = pl.BlockSpec(memory_space=pltpu.VMEM)
    smem = pl.BlockSpec(memory_space=pltpu.SMEM)
    operands = [scal, order, *qs, *caches, *news]
    in_specs = [smem] * 2 + [vmem] * 4 + [anywhere] * 4
    aliases = {}
    if so_far is not None:
        aliases = {len(operands): 0}
        operands.append(so_far)
        in_specs.append(anywhere)
    return pl.pallas_call(
        functools.partial(attend_kernel, first, width, so_far is not None),
        out_shape=jax.ShapeDtypeStruct((rows, out_cols), jnp.bfloat16),
        in_specs=in_specs,
        out_specs=anywhere,
        input_output_aliases=aliases,
        scratch_shapes=[
            pltpu.VMEM((tokens, HEAD_SIZE), jnp.bfloat16),
            pltpu.VMEM((tokens, HEAD_SIZE), jnp.bfloat16),
            pltpu.VMEM((HEAD_SIZE, tokens), jnp.bfloat16),
            pltpu.VMEM((GROUP * heads, rows, HEAD_SIZE), jnp.bfloat16),
            pltpu.VMEM((GROUP, rows, width), jnp.bfloat16),
            pltpu.VMEM((GROUP * heads, 1, rows), jnp.float32),
            pltpu.VMEM((GROUP * heads, 8, rows), jnp.float32),
            pltpu.VMEM((GROUP * heads, HEAD_SIZE, rows), jnp.float32),
            pltpu.SemaphoreType.DMA((2, slots)),
            pltpu.SemaphoreType.DMA((4,)),
            pltpu.SemaphoreType.DMA((GROUP,)),
        ],
        compiler_params=pltpu.CompilerParams(vmem_limit_bytes=VMEM_LIMIT),
        cost_estimate=pl.CostEstimate(
            flops=4 * GROUP * heads * rows * tokens * HEAD_SIZE,
            bytes_accessed=4 * tokens * HEAD_SIZE,
            transcendentals=GROUP * heads * rows * tokens,
        ),
    )(*operands)


def on_device(
    hidden,
    w_query,
    key_weight,
    value_weight,
    q_gain,
    key_norm_gain,
    earlier_keys,
    earlier_values,
    counts,
    place,
):
    planes = lax.axis_size("ctx") // GROUP
    ctx = lax.axis_index("ctx")
    plane = ctx // GROUP
    pos = ctx % GROUP
    rows = hidden.shape[0]
    w_rows = w_query.shape[0]
    group_cols = w_query.shape[1] // GROUP
    widths = (group_cols // 2, group_cols - group_cols // 2)

    def columns_for(r):
        return lax.dynamic_slice(w_query, (0, group_cols * (pos ^ r)), (w_rows, group_cols))

    got = [swap(columns_for(r), r) for r in range(1, GROUP)]
    own_w = spread(jnp.concatenate([columns_for(0), key_weight, value_weight], axis=1), planes)
    far = planes // 2

    half_rows = rows // 2
    hidden_late = after(hidden, *got, own_w[far])
    x_1 = swap(hidden_late, 1)
    x_2 = swap(hidden_late, 2)
    first_source = jnp.concatenate([piece[:, : widths[0]] for piece in got], axis=1)
    rest_first = spread(after(first_source, *own_w[: far + 1]), planes)
    second_source = jnp.concatenate([piece[:, widths[0] :] for piece in got], axis=1)
    rest_second = spread(after(second_source, rest_first[far], own_w[-1]), planes)

    x_1, x_2, *_ = lax.optimization_barrier(
        (x_1, x_2, rest_first[far], rest_first[1], own_w[-1])
    )
    x_3 = jnp.concatenate([swap(x_2[:half_rows], 1), swap(x_1[half_rows:], 2)])
    x_near = jnp.concatenate([x_1, x_2])
    x_mine = [hidden, x_near, x_3]
    xs = x_mine + [
        swap_core(after(hidden, own_w[-1])),
        swap_core(after(x_near, x_3, rest_second[far], rest_first[-1])),
        swap_core(after(x_3, rest_second[far], rest_first[-1])),
    ]

    count = lax.dynamic_index_in_dim(counts, ctx // 2, 0, keepdims=False)
    order = lax.dynamic_index_in_dim(place, ctx // 2, 0, keepdims=False)
    scal = jnp.stack([plane, pos, count, lax.axis_index("tp")]).astype(jnp.int32)
    spots = pos ^ jnp.arange(GROUP, dtype=jnp.int32)
    spot_counts = counts[plane * 2 + spots // 2]
    token_position = (
        spot_counts[:, None] * BLOCK_TOKENS
        + (spots % 2)[:, None] * rows
        + jnp.arange(rows, dtype=jnp.int32)[None, :]
    )
    cosine, sine = rope_tables(token_position.reshape(GROUP * rows))

    partial = project_kv(after(scal, rest_first[-1]), xs, own_w, group_cols).reshape(GROUP, rows, 2 * HEAD_SIZE)
    summed = partial[0]
    for r in range(1, GROUP):
        summed = summed + swap(partial[r], r)
    keys = summed[:, :HEAD_SIZE]
    mean = jnp.mean(keys * keys, axis=-1, keepdims=True)
    scaled = keys * lax.rsqrt(mean + 1e-06) * key_norm_gain
    turned = scaled * cosine[:rows] + jnp.roll(scaled, HEAD_SIZE // 2, axis=-1) * sine[:rows]
    keys_mine = turned.astype(jnp.bfloat16)
    values_mine = summed[:, HEAD_SIZE:].astype(jnp.bfloat16)
    new_mine = jnp.stack([keys_mine, values_mine])
    new_theirs = swap(new_mine, 1)

    cache_mine = jnp.stack([earlier_keys, earlier_values])
    caches = (cache_mine, swap(after(cache_mine, partial), 1))
    news = (new_mine, new_theirs)
    gain = q_gain[None, :]

    def queries(scal, rest_w, first, width):
        q = project(scal, xs, own_w, rest_w, cosine, sine, gain, first, width)
        q = q.reshape(GROUP, rows, width)
        return [q[0]] + [swap(q[r], r) for r in range(1, GROUP)]

    out_cols = w_query.shape[1]
    q_first = queries(
        after(scal, rest_second[far]), rest_first, 0, widths[0]
    )
    q_second = queries(after(scal, q_first[0], new_mine, caches[1]), rest_second, widths[0], widths[1])
    attended = attend(
        after(scal, q_second[0]), order, q_first, caches, news, None, 0, widths[0], out_cols
    )
    attended = attend(
        scal, order, q_second, caches, news, attended, widths[0], widths[1], out_cols
    )
    return (attended, keys_mine, values_mine)


def solution(mesh):
    placed = (
        P("ctx", "tp"),
        P("ctx", "tp"),
        P("ctx", "tp"),
        P("ctx", "tp"),
        P(),
        P(),
        P("ctx", "tp"),
        P("ctx", "tp"),
        P(),
        P(),
    )
    return jax.shard_map(
        on_device,
        mesh=mesh,
        in_specs=placed,
        out_specs=(P("ctx", "tp"), P("ctx", "tp"), P("ctx", "tp")),
        check_vma=False,
    )
```

```python
import functools
import math

import jax
import jax.numpy as jnp
from jax import lax
from jax.experimental import pallas as pl
from jax.experimental.pallas import tpu as pltpu
from jax.sharding import PartitionSpec as P

HEAD_SIZE = 128
BLOCK_TOKENS = 128
GROUP = 4
KEY_CHUNK = 512
VMEM_LIMIT = 28 * 1024 * 1024


def swap(value, mask):
    pairs = [(source, source ^ mask) for source in range(lax.axis_size("ctx"))]
    return lax.ppermute(value, "ctx", pairs)


def swap_core(value):
    return lax.ppermute(value, "tp", [(0, 1), (1, 0)])


def after(value, *others):
    return lax.optimization_barrier((value, *others))[0]


def spread(own, planes):
    pieces = {0: own}
    bit = planes // 2
    while bit:
        for apart in list(pieces):
            pieces[apart ^ bit] = swap(pieces[apart], GROUP * bit)
        bit //= 2
    return [pieces[apart] for apart in range(planes)]


def rope_tables(token_position):
    half = HEAD_SIZE // 2
    freq = jnp.exp(jnp.arange(half, dtype=jnp.float32) * (-2.0 / HEAD_SIZE) * math.log(1000000.0))
    angle = token_position.astype(jnp.float32)[..., None] * freq
    cosine, sine = jnp.cos(angle), jnp.sin(angle)
    return (
        jnp.concatenate([cosine, cosine], axis=-1),
        jnp.concatenate([-sine, sine], axis=-1),
    )


def half_slot(scal, planes, apart):
    there = scal[0] ^ apart
    other = (there // (planes // 2)) ^ scal[3]
    return other * (planes // 2) + there % (planes // 2)


def project_kernel(planes, first, width, *refs):
    scal, refs = refs[0], refs[1:]
    xs, refs = refs[:6], refs[6:]
    own_w, rest_w, refs = refs[:planes], refs[planes : 2 * planes], refs[2 * planes :]
    cosine, sine, gain, q_out, w_all, w_sem = refs
    pos = scal[1]
    half_cols = xs[0].shape[1]
    w_rows = own_w[0].shape[0]

    copies = []
    for apart in range(planes):
        base = half_slot(scal, planes, apart) * GROUP
        for r in range(GROUP):
            if r == 0:
                src = own_w[apart].at[:, pl.ds(first, width)]
            else:
                src = rest_w[apart].at[:, pl.ds((r - 1) * width, width)]
            row = pl.multiple_of((base + (pos ^ r)) * w_rows, w_rows)
            copy = pltpu.make_async_copy(
                src, w_all.at[pl.ds(row, w_rows)], w_sem.at[apart, r]
            )
            copy.start()
            copies.append(copy)
    for copy in copies:
        copy.wait()

    begin = 0
    for part in range(3):
        size = xs[part].shape[0]
        result = jnp.dot(
            xs[part][...], w_all[pl.ds(0, half_cols), :], preferred_element_type=jnp.float32
        ) + jnp.dot(
            xs[3 + part][...],
            w_all[pl.ds(half_cols, half_cols), :],
            preferred_element_type=jnp.float32,
        )
        tokens = pl.ds(begin, size)
        for head in range(width // HEAD_SIZE):
            values = result[:, head * HEAD_SIZE : (head + 1) * HEAD_SIZE]
            mean = jnp.mean(values * values, axis=-1, keepdims=True)
            scaled = values * lax.rsqrt(mean + 1e-06) * gain[...]
            turned = (
                scaled * cosine[tokens, :]
                + pltpu.roll(scaled, HEAD_SIZE // 2, 1) * sine[tokens, :]
            )
            q_out[tokens, pl.ds(head * HEAD_SIZE, HEAD_SIZE)] = turned.astype(jnp.bfloat16)
        begin += size


def project(scal, xs, own_w, rest_w, cosine, sine, gain, first, width):
    planes = len(own_w)
    rows, half_cols = xs[0].shape
    depth = 2 * half_cols
    anywhere = pl.BlockSpec(memory_space=pl.ANY)
    vmem = pl.BlockSpec(memory_space=pltpu.VMEM)
    return pl.pallas_call(
        functools.partial(project_kernel, planes, first, width),
        out_shape=jax.ShapeDtypeStruct((GROUP * rows, width), jnp.bfloat16),
        in_specs=[pl.BlockSpec(memory_space=pltpu.SMEM)]
        + [vmem] * 6
        + [anywhere] * (2 * planes)
        + [vmem] * 3,
        out_specs=vmem,
        scratch_shapes=[
            pltpu.VMEM((depth, width), jnp.bfloat16),
            pltpu.SemaphoreType.DMA((planes, GROUP)),
        ],
        compiler_params=pltpu.CompilerParams(vmem_limit_bytes=VMEM_LIMIT),
        cost_estimate=pl.CostEstimate(
            flops=2 * GROUP * rows * depth * width,
            bytes_accessed=2 * depth * (GROUP * rows + width),
            transcendentals=0,
        ),
    )(scal, *xs, *own_w, *rest_w, cosine, sine, gain)


def project_kv_kernel(planes, skip, *refs):
    scal, refs = refs[0], refs[1:]
    xs, own_w, refs = refs[:6], refs[6 : 6 + planes], refs[6 + planes :]
    kv_out, x_all, w_all, x_sem, w_sem = refs
    pos = scal[1]
    w_rows = own_w[0].shape[0]
    _, depth, width = w_all.shape
    compact = depth == w_rows
    offset = pos * w_rows if compact else 0

    copies = []
    for apart in range(planes):
        slot = half_slot(scal, planes, apart)
        row = 0
        if not compact:
            w_all[slot] = jnp.zeros((depth, width), jnp.bfloat16)
            row = pl.multiple_of(pos * w_rows, w_rows)
        copy = pltpu.make_async_copy(
            own_w[apart].at[:, pl.ds(skip, width)],
            w_all.at[slot, pl.ds(row, w_rows)],
            w_sem.at[apart],
        )
        copy.start()
        copies.append(copy)
    for slot in range(planes):
        half, within = slot // (planes // 2), slot % (planes // 2)
        column = pl.multiple_of(within * GROUP * w_rows + offset, HEAD_SIZE)
        begin = 0
        for part in range(3):
            src = xs[3 * half + part]
            copy = pltpu.make_async_copy(
                src.at[:, pl.ds(column, depth)],
                x_all.at[slot, pl.ds(begin, src.shape[0])],
                x_sem.at[slot, part],
            )
            copy.start()
            copies.append(copy)
            begin += src.shape[0]
    for copy in copies:
        copy.wait()
    result = None
    for slot in range(planes):
        term = jnp.dot(x_all[slot], w_all[slot], preferred_element_type=jnp.float32)
        result = term if result is None else result + term
    kv_out[...] = result


def project_kv(scal, xs, own_w, skip):
    planes = len(own_w)
    rows = xs[0].shape[0]
    w_rows = own_w[0].shape[0]
    width = own_w[0].shape[1] - skip
    depth = w_rows if w_rows % HEAD_SIZE == 0 else GROUP * w_rows
    anywhere = pl.BlockSpec(memory_space=pl.ANY)
    return pl.pallas_call(
        functools.partial(project_kv_kernel, planes, skip),
        out_shape=jax.ShapeDtypeStruct((GROUP * rows, width), jnp.float32),
        in_specs=[pl.BlockSpec(memory_space=pltpu.SMEM)] + [anywhere] * (6 + planes),
        out_specs=pl.BlockSpec(memory_space=pltpu.VMEM),
        scratch_shapes=[
            pltpu.VMEM((planes, GROUP * rows, depth), jnp.bfloat16),
            pltpu.VMEM((planes, depth, width), jnp.bfloat16),
            pltpu.SemaphoreType.DMA((planes, 3)),
            pltpu.SemaphoreType.DMA((planes,)),
        ],
        compiler_params=pltpu.CompilerParams(vmem_limit_bytes=VMEM_LIMIT),
        cost_estimate=pl.CostEstimate(
            flops=2 * GROUP * rows * depth * planes * width,
            bytes_accessed=2 * depth * planes * (GROUP * rows + width),
            transcendentals=0,
        ),
    )(scal, *xs, *own_w)


def attend_kernel(first, width, aliased, *refs):
    scal, order = refs[:2]
    qs = refs[2:6]
    cache_mine, cache_theirs, new_mine, new_theirs = refs[6:10]
    refs = refs[10 + int(aliased) :]
    out, k_all, v_all, vt_all, q_all, o_all, tops, totals, sums = refs[:9]
    kv_sem, new_sem, out_sem = refs[9:]
    pos, count = scal[1], scal[2]
    side = pos % 2
    rows = qs[0].shape[0]
    heads = width // HEAD_SIZE
    slots = order.shape[0]
    half_slots = slots // 2
    scale = HEAD_SIZE ** (-0.5) * math.log2(math.e)
    units = GROUP * heads
    lanes = rows

    def new_copy(new, kind, row, index):
        into = v_all if kind else k_all
        return pltpu.make_async_copy(
            new.at[kind], into.at[pl.ds(row, rows)], new_sem.at[index]
        )

    for kind in range(2):
        new_copy(new_mine, kind, 0, kind).start()

    @pl.when(side == 1)
    def _():
        for kind in range(2):
            new_copy(new_theirs, kind, rows, 2 + kind).start()

    lead = rows + side * rows

    def block_copies(j):
        slot = order[j]
        src_row = pl.multiple_of((slot % half_slots) * BLOCK_TOKENS, BLOCK_TOKENS)
        dst_row = pl.multiple_of(lead + j * BLOCK_TOKENS, BLOCK_TOKENS)
        near = (slot // half_slots) == side

        def pair(cache):
            return (
                pltpu.make_async_copy(
                    cache.at[0, pl.ds(src_row, BLOCK_TOKENS)],
                    k_all.at[pl.ds(dst_row, BLOCK_TOKENS)],
                    kv_sem.at[0, j],
                ),
                pltpu.make_async_copy(
                    cache.at[1, pl.ds(src_row, BLOCK_TOKENS)],
                    v_all.at[pl.ds(dst_row, BLOCK_TOKENS)],
                    kv_sem.at[1, j],
                ),
            )

        return near, pair(cache_mine), pair(cache_theirs)

    def start_block(j, carry):
        near, mine, theirs = block_copies(j)

        @pl.when(near)
        def _():
            for copy in mine:
                copy.start()

        @pl.when(jnp.logical_not(near))
        def _():
            for copy in theirs:
                copy.start()

        return carry

    def wait_block(j, carry):
        _, mine, _ = block_copies(j)
        for copy in mine:
            copy.wait()
        return carry

    def clear_block(j, carry):
        row = pl.multiple_of(rows + j * BLOCK_TOKENS, BLOCK_TOKENS)
        blank = jnp.zeros((BLOCK_TOKENS, HEAD_SIZE), jnp.bfloat16)
        k_all[pl.ds(row, BLOCK_TOKENS), :] = blank
        v_all[pl.ds(row, BLOCK_TOKENS), :] = blank
        return carry

    per_chunk = KEY_CHUNK // BLOCK_TOKENS
    blocks = count + side * (rows // BLOCK_TOKENS)
    full = blocks // per_chunk
    chunks = (blocks + per_chunk - 1) // per_chunk
    lax.fori_loop(0, count, start_block, 0)
    lax.fori_loop(blocks, chunks * per_chunk, clear_block, 0)
    for r in range(GROUP):
        for head in range(heads):
            q_all[r * heads + head] = qs[r][:, pl.ds(head * HEAD_SIZE, HEAD_SIZE)]

    def turn_values(row, size):
        values = v_all[pl.ds(row, size), :].astype(jnp.float32)
        vt_all[:, pl.ds(row, size)] = values.T.astype(jnp.bfloat16)

    def fold(values, combine):
        parts = values.reshape(values.shape[0] // 8, 8, lanes)
        return combine(parts, axis=0)

    def absorb(row, size, allowed, fresh):
        keys = k_all[pl.ds(row, size), :]
        values = vt_all[:, pl.ds(row, size)]

        def score(unit):
            return lax.dot_general(
                keys, q_all[unit], (((1,), (1,)), ((), ())), preferred_element_type=jnp.float32
            )

        ahead = score(0)
        for unit in range(units):
            s = ahead
            if unit + 1 < units:
                ahead = score(unit + 1)
            if allowed is not None:
                s = jnp.where(allowed, s, -1e30)
            top = jnp.max(fold(s, jnp.max), axis=0, keepdims=True)
            if not fresh:
                before = tops[unit]
                top = jnp.maximum(before, top)
            weight = jnp.exp2((s - top) * scale)
            total = fold(weight, jnp.sum)
            mixed = jnp.dot(
                values, weight.astype(jnp.bfloat16), preferred_element_type=jnp.float32
            )
            if not fresh:
                shrink = jnp.exp2((before - top) * scale)
                total = total + totals[unit] * shrink
                mixed = mixed + sums[unit] * shrink
            tops[unit] = top
            totals[unit] = total
            sums[unit] = mixed

    for kind in range(2):
        new_copy(new_mine, kind, 0, kind).wait()
    turn_values(0, rows)
    key = lax.broadcasted_iota(jnp.int32, (rows, lanes), 0)
    token = lax.broadcasted_iota(jnp.int32, (rows, lanes), 1)
    absorb(0, rows, key <= token, True)

    @pl.when(side == 1)
    def _():
        for kind in range(2):
            new_copy(new_theirs, kind, rows, 2 + kind).wait()

    lax.fori_loop(0, count, wait_block, 0)

    def chunk_row(chunk):
        return pl.multiple_of(rows + chunk * KEY_CHUNK, BLOCK_TOKENS)

    def step(chunk, carry):
        turn_values(chunk_row(chunk), KEY_CHUNK)
        absorb(chunk_row(chunk), KEY_CHUNK, None, False)
        return carry

    lax.fori_loop(0, full, step, 0)

    @pl.when(chunks > full)
    def _():
        turn_values(chunk_row(full), KEY_CHUNK)
        key = lax.broadcasted_iota(jnp.int32, (KEY_CHUNK, lanes), 0)
        allowed = key < (blocks - full * per_chunk) * BLOCK_TOKENS
        absorb(chunk_row(full), KEY_CHUNK, allowed, False)

    group_cols = out.shape[1] // GROUP
    copies = []
    for r in range(GROUP):
        for head in range(heads):
            unit = r * heads + head
            total = jnp.sum(totals[unit], axis=0, keepdims=True)
            result = (sums[unit] / total).T.astype(jnp.bfloat16)
            o_all[r, :, pl.ds(head * HEAD_SIZE, HEAD_SIZE)] = result
        column = pl.multiple_of((pos ^ r) * group_cols + first, HEAD_SIZE)
        copy = pltpu.make_async_copy(
            o_all.at[r], out.at[:, pl.ds(column, width)], out_sem.at[r]
        )
        copy.start()
        copies.append(copy)
    for copy in copies:
        copy.wait()


def attend(scal, order, qs, caches, news, so_far, first, width, out_cols):
    rows = qs[0].shape[0]
    slots = order.shape[0]
    heads = width // HEAD_SIZE
    rest = rows + slots * BLOCK_TOKENS
    tokens = rows + -(-rest // KEY_CHUNK) * KEY_CHUNK
    anywhere = pl.BlockSpec(memory_space=pl.ANY)
    vmem = pl.BlockSpec(memory_space=pltpu.VMEM)
    smem = pl.BlockSpec(memory_space=pltpu.SMEM)
    operands = [scal, order, *qs, *caches, *news]
    in_specs = [smem] * 2 + [vmem] * 4 + [anywhere] * 4
    aliases = {}
    if so_far is not None:
        aliases = {len(operands): 0}
        operands.append(so_far)
        in_specs.append(anywhere)
    return pl.pallas_call(
        functools.partial(attend_kernel, first, width, so_far is not None),
        out_shape=jax.ShapeDtypeStruct((rows, out_cols), jnp.bfloat16),
        in_specs=in_specs,
        out_specs=anywhere,
        input_output_aliases=aliases,
        scratch_shapes=[
            pltpu.VMEM((tokens, HEAD_SIZE), jnp.bfloat16),
            pltpu.VMEM((tokens, HEAD_SIZE), jnp.bfloat16),
            pltpu.VMEM((HEAD_SIZE, tokens), jnp.bfloat16),
            pltpu.VMEM((GROUP * heads, rows, HEAD_SIZE), jnp.bfloat16),
            pltpu.VMEM((GROUP, rows, width), jnp.bfloat16),
            pltpu.VMEM((GROUP * heads, 1, rows), jnp.float32),
            pltpu.VMEM((GROUP * heads, 8, rows), jnp.float32),
            pltpu.VMEM((GROUP * heads, HEAD_SIZE, rows), jnp.float32),
            pltpu.SemaphoreType.DMA((2, slots)),
            pltpu.SemaphoreType.DMA((4,)),
            pltpu.SemaphoreType.DMA((GROUP,)),
        ],
        compiler_params=pltpu.CompilerParams(vmem_limit_bytes=VMEM_LIMIT),
        cost_estimate=pl.CostEstimate(
            flops=4 * GROUP * heads * rows * tokens * HEAD_SIZE,
            bytes_accessed=4 * tokens * HEAD_SIZE,
            transcendentals=GROUP * heads * rows * tokens,
        ),
    )(*operands)


def on_device(
    hidden,
    w_query,
    key_weight,
    value_weight,
    q_gain,
    key_norm_gain,
    earlier_keys,
    earlier_values,
    counts,
    place,
):
    planes = lax.axis_size("ctx") // GROUP
    ctx = lax.axis_index("ctx")
    plane = ctx // GROUP
    pos = ctx % GROUP
    rows = hidden.shape[0]
    w_rows = w_query.shape[0]
    group_cols = w_query.shape[1] // GROUP
    widths = (group_cols // 2, group_cols - group_cols // 2)

    def columns_for(r):
        return lax.dynamic_slice(w_query, (0, group_cols * (pos ^ r)), (w_rows, group_cols))

    got = [swap(columns_for(r), r) for r in range(1, GROUP)]
    own_w = spread(jnp.concatenate([columns_for(0), key_weight, value_weight], axis=1), planes)
    far = planes // 2

    half_rows = rows // 2
    hidden_late = after(hidden, *got, own_w[far])
    x_1 = swap(hidden_late, 1)
    x_2 = swap(hidden_late, 2)
    first_source = jnp.concatenate([piece[:, : widths[0]] for piece in got], axis=1)
    rest_first = spread(after(first_source, *own_w[: far + 1]), planes)
    second_source = jnp.concatenate([piece[:, widths[0] :] for piece in got], axis=1)
    rest_second = spread(after(second_source, rest_first[far]), planes)

    x_1, x_2, *_ = lax.optimization_barrier((x_1, x_2, *rest_first[1 : far + 1]))
    x_3 = jnp.concatenate([swap(x_2[:half_rows], 1), swap(x_1[half_rows:], 2)])
    x_near = jnp.concatenate([x_1, x_2])
    x_mine = [hidden, x_near, x_3]
    xs = x_mine + [
        swap_core(after(hidden, rest_first[far])),
        swap_core(x_near),
        swap_core(after(x_3, rest_second[far], own_w[-1])),
    ]

    count = lax.dynamic_index_in_dim(counts, ctx // 2, 0, keepdims=False)
    order = lax.dynamic_index_in_dim(place, ctx // 2, 0, keepdims=False)
    scal = jnp.stack([plane, pos, count, lax.axis_index("tp")]).astype(jnp.int32)
    spots = pos ^ jnp.arange(GROUP, dtype=jnp.int32)
    spot_counts = counts[plane * 2 + spots // 2]
    token_position = (
        spot_counts[:, None] * BLOCK_TOKENS
        + (spots % 2)[:, None] * rows
        + jnp.arange(rows, dtype=jnp.int32)[None, :]
    )
    cosine, sine = rope_tables(token_position.reshape(GROUP * rows))

    partial = project_kv(after(scal, rest_first[-1]), xs, own_w, group_cols).reshape(GROUP, rows, 2 * HEAD_SIZE)
    summed = partial[0]
    for r in range(1, GROUP):
        summed = summed + swap(partial[r], r)
    keys = summed[:, :HEAD_SIZE]
    mean = jnp.mean(keys * keys, axis=-1, keepdims=True)
    scaled = keys * lax.rsqrt(mean + 1e-06) * key_norm_gain
    turned = scaled * cosine[:rows] + jnp.roll(scaled, HEAD_SIZE // 2, axis=-1) * sine[:rows]
    keys_mine = turned.astype(jnp.bfloat16)
    values_mine = summed[:, HEAD_SIZE:].astype(jnp.bfloat16)
    new_mine = jnp.stack([keys_mine, values_mine])
    new_theirs = swap(new_mine, 1)

    cache_mine = jnp.stack([earlier_keys, earlier_values])
    caches = (cache_mine, swap(after(cache_mine, partial), 1))
    news = (new_mine, new_theirs)
    gain = q_gain[None, :]

    def queries(scal, rest_w, first, width):
        q = project(scal, xs, own_w, rest_w, cosine, sine, gain, first, width)
        q = q.reshape(GROUP, rows, width)
        return [q[0]] + [swap(q[r], r) for r in range(1, GROUP)]

    out_cols = w_query.shape[1]
    q_first = queries(
        after(scal, rest_second[far]), rest_first, 0, widths[0]
    )
    q_second = queries(after(scal, q_first[0], new_mine, caches[1]), rest_second, widths[0], widths[1])
    attended = attend(
        after(scal, q_second[0]), order, q_first, caches, news, None, 0, widths[0], out_cols
    )
    attended = attend(
        scal, order, q_second, caches, news, attended, widths[0], widths[1], out_cols
    )
    return (attended, keys_mine, values_mine)


def solution(mesh):
    placed = (
        P("ctx", "tp"),
        P("ctx", "tp"),
        P("ctx", "tp"),
        P("ctx", "tp"),
        P(),
        P(),
        P("ctx", "tp"),
        P("ctx", "tp"),
        P(),
        P(),
    )
    return jax.shard_map(
        on_device,
        mesh=mesh,
        in_specs=placed,
        out_specs=(P("ctx", "tp"), P("ctx", "tp"), P("ctx", "tp")),
        check_vma=False,
    )
```

```python
import functools
import math

import jax
import jax.numpy as jnp
from jax import lax
from jax.experimental import pallas as pl
from jax.experimental.pallas import tpu as pltpu
from jax.sharding import PartitionSpec as P

HEAD_SIZE = 128
BLOCK_TOKENS = 128
GROUP = 4
KEY_CHUNK = 512
VMEM_LIMIT = 28 * 1024 * 1024


def swap(value, mask):
    pairs = [(source, source ^ mask) for source in range(lax.axis_size("ctx"))]
    return lax.ppermute(value, "ctx", pairs)


def swap_core(value):
    return lax.ppermute(value, "tp", [(0, 1), (1, 0)])


def after(value, *others):
    return lax.optimization_barrier((value, *others))[0]


def near(source, planes):
    pieces = [source]
    bit = 1
    while bit < planes // 2:
        pieces = pieces + [swap(piece, GROUP * bit) for piece in pieces]
        bit *= 2
    return pieces


def gate(values, done):
    return lax.optimization_barrier((tuple(values), tuple(done)))[0]


def rope_tables(token_position):
    half = HEAD_SIZE // 2
    freq = jnp.exp(jnp.arange(half, dtype=jnp.float32) * (-2.0 / HEAD_SIZE) * math.log(1000000.0))
    angle = token_position.astype(jnp.float32)[..., None] * freq
    cosine, sine = jnp.cos(angle), jnp.sin(angle)
    return (
        jnp.concatenate([cosine, cosine], axis=-1),
        jnp.concatenate([-sine, sine], axis=-1),
    )


def half_slot(scal, planes, apart):
    there = scal[0] ^ apart
    other = (there // (planes // 2)) ^ scal[3]
    return other * (planes // 2) + there % (planes // 2)


def project_kernel(planes, first, width, *refs):
    scal, refs = refs[0], refs[1:]
    xs, refs = refs[:6], refs[6:]
    own_w, rest_w, refs = refs[:planes], refs[planes : 2 * planes], refs[2 * planes :]
    cosine, sine, gain, q_out, w_all, w_sem = refs
    pos = scal[1]
    half_cols = xs[0].shape[1]
    w_rows = own_w[0].shape[0]

    copies = []
    for apart in range(planes):
        base = half_slot(scal, planes, apart) * GROUP
        for r in range(GROUP):
            if r == 0:
                src = own_w[apart].at[:, pl.ds(first, width)]
            else:
                src = rest_w[apart].at[:, pl.ds((r - 1) * width, width)]
            row = pl.multiple_of((base + (pos ^ r)) * w_rows, w_rows)
            copy = pltpu.make_async_copy(
                src, w_all.at[pl.ds(row, w_rows)], w_sem.at[apart, r]
            )
            copy.start()
            copies.append(copy)
    for copy in copies:
        copy.wait()

    begin = 0
    for part in range(3):
        size = xs[part].shape[0]
        result = jnp.dot(
            xs[part][...], w_all[pl.ds(0, half_cols), :], preferred_element_type=jnp.float32
        ) + jnp.dot(
            xs[3 + part][...],
            w_all[pl.ds(half_cols, half_cols), :],
            preferred_element_type=jnp.float32,
        )
        tokens = pl.ds(begin, size)
        for head in range(width // HEAD_SIZE):
            values = result[:, head * HEAD_SIZE : (head + 1) * HEAD_SIZE]
            mean = jnp.mean(values * values, axis=-1, keepdims=True)
            scaled = values * lax.rsqrt(mean + 1e-06) * gain[...]
            turned = (
                scaled * cosine[tokens, :]
                + pltpu.roll(scaled, HEAD_SIZE // 2, 1) * sine[tokens, :]
            )
            q_out[tokens, pl.ds(head * HEAD_SIZE, HEAD_SIZE)] = turned.astype(jnp.bfloat16)
        begin += size


def project(scal, xs, own_w, rest_w, cosine, sine, gain, first, width):
    planes = len(own_w)
    rows, half_cols = xs[0].shape
    depth = 2 * half_cols
    anywhere = pl.BlockSpec(memory_space=pl.ANY)
    vmem = pl.BlockSpec(memory_space=pltpu.VMEM)
    return pl.pallas_call(
        functools.partial(project_kernel, planes, first, width),
        out_shape=jax.ShapeDtypeStruct((GROUP * rows, width), jnp.bfloat16),
        in_specs=[pl.BlockSpec(memory_space=pltpu.SMEM)]
        + [vmem] * 6
        + [anywhere] * (2 * planes)
        + [vmem] * 3,
        out_specs=vmem,
        scratch_shapes=[
            pltpu.VMEM((depth, width), jnp.bfloat16),
            pltpu.SemaphoreType.DMA((planes, GROUP)),
        ],
        compiler_params=pltpu.CompilerParams(vmem_limit_bytes=VMEM_LIMIT),
        cost_estimate=pl.CostEstimate(
            flops=2 * GROUP * rows * depth * width,
            bytes_accessed=2 * depth * (GROUP * rows + width),
            transcendentals=0,
        ),
    )(scal, *xs, *own_w, *rest_w, cosine, sine, gain)


def project_kv_kernel(planes, skip, *refs):
    scal, refs = refs[0], refs[1:]
    xs, own_w, refs = refs[:6], refs[6 : 6 + planes], refs[6 + planes :]
    kv_out, x_all, w_all, x_sem, w_sem = refs
    pos = scal[1]
    w_rows = own_w[0].shape[0]
    _, depth, width = w_all.shape
    compact = depth == w_rows
    offset = pos * w_rows if compact else 0

    copies = []
    for apart in range(planes):
        slot = half_slot(scal, planes, apart)
        row = 0
        if not compact:
            w_all[slot] = jnp.zeros((depth, width), jnp.bfloat16)
            row = pl.multiple_of(pos * w_rows, w_rows)
        copy = pltpu.make_async_copy(
            own_w[apart].at[:, pl.ds(skip, width)],
            w_all.at[slot, pl.ds(row, w_rows)],
            w_sem.at[apart],
        )
        copy.start()
        copies.append(copy)
    for slot in range(planes):
        half, within = slot // (planes // 2), slot % (planes // 2)
        column = pl.multiple_of(within * GROUP * w_rows + offset, HEAD_SIZE)
        begin = 0
        for part in range(3):
            src = xs[3 * half + part]
            copy = pltpu.make_async_copy(
                src.at[:, pl.ds(column, depth)],
                x_all.at[slot, pl.ds(begin, src.shape[0])],
                x_sem.at[slot, part],
            )
            copy.start()
            copies.append(copy)
            begin += src.shape[0]
    for copy in copies:
        copy.wait()
    result = None
    for slot in range(planes):
        term = jnp.dot(x_all[slot], w_all[slot], preferred_element_type=jnp.float32)
        result = term if result is None else result + term
    kv_out[...] = result


def project_kv(scal, xs, own_w, skip):
    planes = len(own_w)
    rows = xs[0].shape[0]
    w_rows = own_w[0].shape[0]
    width = own_w[0].shape[1] - skip
    depth = w_rows if w_rows % HEAD_SIZE == 0 else GROUP * w_rows
    anywhere = pl.BlockSpec(memory_space=pl.ANY)
    return pl.pallas_call(
        functools.partial(project_kv_kernel, planes, skip),
        out_shape=jax.ShapeDtypeStruct((GROUP * rows, width), jnp.float32),
        in_specs=[pl.BlockSpec(memory_space=pltpu.SMEM)] + [anywhere] * (6 + planes),
        out_specs=pl.BlockSpec(memory_space=pltpu.VMEM),
        scratch_shapes=[
            pltpu.VMEM((planes, GROUP * rows, depth), jnp.bfloat16),
            pltpu.VMEM((planes, depth, width), jnp.bfloat16),
            pltpu.SemaphoreType.DMA((planes, 3)),
            pltpu.SemaphoreType.DMA((planes,)),
        ],
        compiler_params=pltpu.CompilerParams(vmem_limit_bytes=VMEM_LIMIT),
        cost_estimate=pl.CostEstimate(
            flops=2 * GROUP * rows * depth * planes * width,
            bytes_accessed=2 * depth * planes * (GROUP * rows + width),
            transcendentals=0,
        ),
    )(scal, *xs, *own_w)


def attend_kernel(first, width, aliased, *refs):
    scal, order = refs[:2]
    qs = refs[2:6]
    cache_mine, cache_theirs, new_mine, new_theirs = refs[6:10]
    refs = refs[10 + int(aliased) :]
    out, k_all, v_all, vt_all, q_all, o_all, tops, totals, sums = refs[:9]
    kv_sem, new_sem, out_sem = refs[9:]
    pos, count = scal[1], scal[2]
    side = pos % 2
    rows = qs[0].shape[0]
    heads = width // HEAD_SIZE
    slots = order.shape[0]
    half_slots = slots // 2
    scale = HEAD_SIZE ** (-0.5) * math.log2(math.e)
    units = GROUP * heads
    lanes = rows

    def new_copy(new, kind, row, index):
        into = v_all if kind else k_all
        return pltpu.make_async_copy(
            new.at[kind], into.at[pl.ds(row, rows)], new_sem.at[index]
        )

    for kind in range(2):
        new_copy(new_mine, kind, 0, kind).start()

    @pl.when(side == 1)
    def _():
        for kind in range(2):
            new_copy(new_theirs, kind, rows, 2 + kind).start()

    lead = rows + side * rows

    def block_copies(j):
        slot = order[j]
        src_row = pl.multiple_of((slot % half_slots) * BLOCK_TOKENS, BLOCK_TOKENS)
        dst_row = pl.multiple_of(lead + j * BLOCK_TOKENS, BLOCK_TOKENS)
        near = (slot // half_slots) == side

        def pair(cache):
            return (
                pltpu.make_async_copy(
                    cache.at[0, pl.ds(src_row, BLOCK_TOKENS)],
                    k_all.at[pl.ds(dst_row, BLOCK_TOKENS)],
                    kv_sem.at[0, j],
                ),
                pltpu.make_async_copy(
                    cache.at[1, pl.ds(src_row, BLOCK_TOKENS)],
                    v_all.at[pl.ds(dst_row, BLOCK_TOKENS)],
                    kv_sem.at[1, j],
                ),
            )

        return near, pair(cache_mine), pair(cache_theirs)

    def start_block(j, carry):
        near, mine, theirs = block_copies(j)

        @pl.when(near)
        def _():
            for copy in mine:
                copy.start()

        @pl.when(jnp.logical_not(near))
        def _():
            for copy in theirs:
                copy.start()

        return carry

    def wait_block(j, carry):
        _, mine, _ = block_copies(j)
        for copy in mine:
            copy.wait()
        return carry

    def clear_block(j, carry):
        row = pl.multiple_of(rows + j * BLOCK_TOKENS, BLOCK_TOKENS)
        blank = jnp.zeros((BLOCK_TOKENS, HEAD_SIZE), jnp.bfloat16)
        k_all[pl.ds(row, BLOCK_TOKENS), :] = blank
        v_all[pl.ds(row, BLOCK_TOKENS), :] = blank
        return carry

    per_chunk = KEY_CHUNK // BLOCK_TOKENS
    blocks = count + side * (rows // BLOCK_TOKENS)
    full = blocks // per_chunk
    chunks = (blocks + per_chunk - 1) // per_chunk
    lax.fori_loop(0, count, start_block, 0)
    lax.fori_loop(blocks, chunks * per_chunk, clear_block, 0)
    for r in range(GROUP):
        for head in range(heads):
            q_all[r * heads + head] = qs[r][:, pl.ds(head * HEAD_SIZE, HEAD_SIZE)]

    def turn_values(row, size):
        values = v_all[pl.ds(row, size), :].astype(jnp.float32)
        vt_all[:, pl.ds(row, size)] = values.T.astype(jnp.bfloat16)

    def fold(values, combine):
        parts = values.reshape(values.shape[0] // 8, 8, lanes)
        return combine(parts, axis=0)

    def absorb(row, size, allowed, fresh):
        keys = k_all[pl.ds(row, size), :]
        values = vt_all[:, pl.ds(row, size)]

        def score(unit):
            return lax.dot_general(
                keys, q_all[unit], (((1,), (1,)), ((), ())), preferred_element_type=jnp.float32
            )

        ahead = score(0)
        for unit in range(units):
            s = ahead
            if unit + 1 < units:
                ahead = score(unit + 1)
            if allowed is not None:
                s = jnp.where(allowed, s, -1e30)
            top = jnp.max(fold(s, jnp.max), axis=0, keepdims=True)
            if not fresh:
                before = tops[unit]
                top = jnp.maximum(before, top)
            weight = jnp.exp2((s - top) * scale)
            total = fold(weight, jnp.sum)
            mixed = jnp.dot(
                values, weight.astype(jnp.bfloat16), preferred_element_type=jnp.float32
            )
            if not fresh:
                shrink = jnp.exp2((before - top) * scale)
                total = total + totals[unit] * shrink
                mixed = mixed + sums[unit] * shrink
            tops[unit] = top
            totals[unit] = total
            sums[unit] = mixed

    for kind in range(2):
        new_copy(new_mine, kind, 0, kind).wait()
    turn_values(0, rows)
    key = lax.broadcasted_iota(jnp.int32, (rows, lanes), 0)
    token = lax.broadcasted_iota(jnp.int32, (rows, lanes), 1)
    absorb(0, rows, key <= token, True)

    @pl.when(side == 1)
    def _():
        for kind in range(2):
            new_copy(new_theirs, kind, rows, 2 + kind).wait()

    lax.fori_loop(0, count, wait_block, 0)

    def chunk_row(chunk):
        return pl.multiple_of(rows + chunk * KEY_CHUNK, BLOCK_TOKENS)

    def step(chunk, carry):
        turn_values(chunk_row(chunk), KEY_CHUNK)
        absorb(chunk_row(chunk), KEY_CHUNK, None, False)
        return carry

    lax.fori_loop(0, full, step, 0)

    @pl.when(chunks > full)
    def _():
        turn_values(chunk_row(full), KEY_CHUNK)
        key = lax.broadcasted_iota(jnp.int32, (KEY_CHUNK, lanes), 0)
        allowed = key < (blocks - full * per_chunk) * BLOCK_TOKENS
        absorb(chunk_row(full), KEY_CHUNK, allowed, False)

    group_cols = out.shape[1] // GROUP
    copies = []
    for r in range(GROUP):
        for head in range(heads):
            unit = r * heads + head
            total = jnp.sum(totals[unit], axis=0, keepdims=True)
            result = (sums[unit] / total).T.astype(jnp.bfloat16)
            o_all[r, :, pl.ds(head * HEAD_SIZE, HEAD_SIZE)] = result
        column = pl.multiple_of((pos ^ r) * group_cols + first, HEAD_SIZE)
        copy = pltpu.make_async_copy(
            o_all.at[r], out.at[:, pl.ds(column, width)], out_sem.at[r]
        )
        copy.start()
        copies.append(copy)
    for copy in copies:
        copy.wait()


def attend(scal, order, qs, caches, news, so_far, first, width, out_cols):
    rows = qs[0].shape[0]
    slots = order.shape[0]
    heads = width // HEAD_SIZE
    rest = rows + slots * BLOCK_TOKENS
    tokens = rows + -(-rest // KEY_CHUNK) * KEY_CHUNK
    anywhere = pl.BlockSpec(memory_space=pl.ANY)
    vmem = pl.BlockSpec(memory_space=pltpu.VMEM)
    smem = pl.BlockSpec(memory_space=pltpu.SMEM)
    operands = [scal, order, *qs, *caches, *news]
    in_specs = [smem] * 2 + [vmem] * 4 + [anywhere] * 4
    aliases = {}
    if so_far is not None:
        aliases = {len(operands): 0}
        operands.append(so_far)
        in_specs.append(anywhere)
    return pl.pallas_call(
        functools.partial(attend_kernel, first, width, so_far is not None),
        out_shape=jax.ShapeDtypeStruct((rows, out_cols), jnp.bfloat16),
        in_specs=in_specs,
        out_specs=anywhere,
        input_output_aliases=aliases,
        scratch_shapes=[
            pltpu.VMEM((tokens, HEAD_SIZE), jnp.bfloat16),
            pltpu.VMEM((tokens, HEAD_SIZE), jnp.bfloat16),
            pltpu.VMEM((HEAD_SIZE, tokens), jnp.bfloat16),
            pltpu.VMEM((GROUP * heads, rows, HEAD_SIZE), jnp.bfloat16),
            pltpu.VMEM((GROUP, rows, width), jnp.bfloat16),
            pltpu.VMEM((GROUP * heads, 1, rows), jnp.float32),
            pltpu.VMEM((GROUP * heads, 8, rows), jnp.float32),
            pltpu.VMEM((GROUP * heads, HEAD_SIZE, rows), jnp.float32),
            pltpu.SemaphoreType.DMA((2, slots)),
            pltpu.SemaphoreType.DMA((4,)),
            pltpu.SemaphoreType.DMA((GROUP,)),
        ],
        compiler_params=pltpu.CompilerParams(vmem_limit_bytes=VMEM_LIMIT),
        cost_estimate=pl.CostEstimate(
            flops=4 * GROUP * heads * rows * tokens * HEAD_SIZE,
            bytes_accessed=4 * tokens * HEAD_SIZE,
            transcendentals=GROUP * heads * rows * tokens,
        ),
    )(*operands)


def on_device(
    hidden,
    w_query,
    key_weight,
    value_weight,
    q_gain,
    key_norm_gain,
    earlier_keys,
    earlier_values,
    counts,
    place,
):
    planes = lax.axis_size("ctx") // GROUP
    ctx = lax.axis_index("ctx")
    plane = ctx // GROUP
    pos = ctx % GROUP
    rows = hidden.shape[0]
    w_rows = w_query.shape[0]
    group_cols = w_query.shape[1] // GROUP
    widths = (group_cols // 2, group_cols - group_cols // 2)

    def columns_for(r):
        return lax.dynamic_slice(w_query, (0, group_cols * (pos ^ r)), (w_rows, group_cols))

    count = lax.dynamic_index_in_dim(counts, ctx // 2, 0, keepdims=False)
    order = lax.dynamic_index_in_dim(place, ctx // 2, 0, keepdims=False)
    scal = jnp.stack([plane, pos, count, lax.axis_index("tp")]).astype(jnp.int32)
    spots = pos ^ jnp.arange(GROUP, dtype=jnp.int32)
    spot_counts = counts[plane * 2 + spots // 2]
    token_position = (
        spot_counts[:, None] * BLOCK_TOKENS
        + (spots % 2)[:, None] * rows
        + jnp.arange(rows, dtype=jnp.int32)[None, :]
    )
    cosine, sine = rope_tables(token_position.reshape(GROUP * rows))
    cache_mine = jnp.stack([earlier_keys, earlier_values])
    across = GROUP * (planes // 2)
    half_rows = rows // 2

    own = jnp.concatenate([columns_for(0), key_weight, value_weight], axis=1)
    own_far = swap(own, across)
    got = [swap(columns_for(r), r) for r in range(1, GROUP)]
    own_near = near(own, planes)
    first = jnp.concatenate([piece[:, : widths[0]] for piece in got], axis=1)
    second = jnp.concatenate([piece[:, widths[0] :] for piece in got], axis=1)
    hidden, first, second, own_far, cosine, sine, scal, order, cache_mine = gate(
        (hidden, first, second, own_far, cosine, sine, scal, order, cache_mine),
        (*got, *own_near),
    )

    x_1, x_2 = swap(hidden, 1), swap(hidden, 2)
    core_0 = swap_core(hidden)
    first_far = swap(first, across)
    first_near = near(first, planes)
    x_1, x_2, second, own_far, first_far = gate(
        (x_1, x_2, second, own_far, first_far), (core_0, *first_near)
    )

    x_3 = jnp.concatenate([swap(x_2[:half_rows], 1), swap(x_1[half_rows:], 2)])
    x_near = jnp.concatenate([x_1, x_2])
    core_near = swap_core(x_near)
    second_far = swap(second, across)
    own_w = own_near + near(own_far, planes)
    x_3, first_far, second, second_far = gate(
        (x_3, first_far, second, second_far), (core_near, *own_w[planes // 2 + 1 :])
    )

    xs = [hidden, x_near, x_3, core_0, core_near, swap_core(x_3)]
    rest_first = first_near + near(first_far, planes)
    rest_second = near(second, planes) + near(second_far, planes)

    partial = project_kv(scal, xs, own_w, group_cols)
    partial = partial.reshape(GROUP, rows, 2 * HEAD_SIZE)
    summed = partial[0]
    for r in range(1, GROUP):
        summed = summed + swap(partial[r], r)
    keys = summed[:, :HEAD_SIZE]
    mean = jnp.mean(keys * keys, axis=-1, keepdims=True)
    scaled = keys * lax.rsqrt(mean + 1e-06) * key_norm_gain
    turned = scaled * cosine[:rows] + jnp.roll(scaled, HEAD_SIZE // 2, axis=-1) * sine[:rows]
    keys_mine = turned.astype(jnp.bfloat16)
    values_mine = summed[:, HEAD_SIZE:].astype(jnp.bfloat16)
    new_mine = jnp.stack([keys_mine, values_mine])
    new_theirs = swap(new_mine, 1)

    caches = (cache_mine, swap(after(cache_mine, partial), 1))
    news = (new_mine, new_theirs)
    gain = q_gain[None, :]

    def queries(scal, rest_w, first, width):
        q = project(scal, xs, own_w, rest_w, cosine, sine, gain, first, width)
        q = q.reshape(GROUP, rows, width)
        return [q[0]] + [swap(q[r], r) for r in range(1, GROUP)]

    out_cols = w_query.shape[1]
    q_first = queries(
        scal, rest_first, 0, widths[0]
    )
    q_second = queries(after(scal, q_first[0], new_mine, caches[1]), rest_second, widths[0], widths[1])
    attended = attend(
        after(scal, q_second[0]), order, q_first, caches, news, None, 0, widths[0], out_cols
    )
    attended = attend(
        scal, order, q_second, caches, news, attended, widths[0], widths[1], out_cols
    )
    return (attended, keys_mine, values_mine)


def solution(mesh):
    placed = (
        P("ctx", "tp"),
        P("ctx", "tp"),
        P("ctx", "tp"),
        P("ctx", "tp"),
        P(),
        P(),
        P("ctx", "tp"),
        P("ctx", "tp"),
        P(),
        P(),
    )
    return jax.shard_map(
        on_device,
        mesh=mesh,
        in_specs=placed,
        out_specs=(P("ctx", "tp"), P("ctx", "tp"), P("ctx", "tp")),
        check_vma=False,
    )
```

```python
import functools
import math

import jax
import jax.numpy as jnp
from jax import lax
from jax.experimental import pallas as pl
from jax.experimental.pallas import tpu as pltpu
from jax.sharding import PartitionSpec as P

HEAD_SIZE = 128
BLOCK_TOKENS = 128
GROUP = 4
KEY_CHUNK = 512
VMEM_LIMIT = 28 * 1024 * 1024


def swap(value, mask):
    pairs = [(source, source ^ mask) for source in range(lax.axis_size("ctx"))]
    return lax.ppermute(value, "ctx", pairs)


def swap_core(value):
    return lax.ppermute(value, "tp", [(0, 1), (1, 0)])


def after(value, *others):
    return lax.optimization_barrier((value, *others))[0]


def near(source, planes):
    pieces = [source]
    bit = 1
    while bit < planes // 2:
        pieces = pieces + [swap(piece, GROUP * bit) for piece in pieces]
        bit *= 2
    return pieces


def gate(values, done):
    return lax.optimization_barrier((tuple(values), tuple(done)))[0]


def rope_tables(token_position):
    half = HEAD_SIZE // 2
    freq = jnp.exp(jnp.arange(half, dtype=jnp.float32) * (-2.0 / HEAD_SIZE) * math.log(1000000.0))
    angle = token_position.astype(jnp.float32)[..., None] * freq
    cosine, sine = jnp.cos(angle), jnp.sin(angle)
    return (
        jnp.concatenate([cosine, cosine], axis=-1),
        jnp.concatenate([-sine, sine], axis=-1),
    )


def half_slot(scal, planes, apart):
    there = scal[0] ^ apart
    other = (there // (planes // 2)) ^ scal[3]
    return other * (planes // 2) + there % (planes // 2)


def project_kernel(planes, first, width, *refs):
    scal, refs = refs[0], refs[1:]
    xs, refs = refs[:4], refs[4:]
    own_w, rest_w, refs = refs[:planes], refs[planes : 2 * planes], refs[2 * planes :]
    cosine, sine, gain, *q_out, w_all, w_sem = refs
    pos = scal[1]
    half_cols = xs[0].shape[1]
    w_rows = own_w[0].shape[0]

    copies = []
    for apart in range(planes):
        base = half_slot(scal, planes, apart) * GROUP
        for r in range(GROUP):
            if r == 0:
                src = own_w[apart].at[:, pl.ds(first, width)]
            else:
                src = rest_w[apart].at[:, pl.ds((r - 1) * width, width)]
            row = pl.multiple_of((base + (pos ^ r)) * w_rows, w_rows)
            copy = pltpu.make_async_copy(
                src, w_all.at[pl.ds(row, w_rows)], w_sem.at[apart, r]
            )
            copy.start()
            copies.append(copy)
    for copy in copies:
        copy.wait()

    rows = q_out[0].shape[0]
    for block in range(GROUP):
        part, begin = (0, block * rows) if block < GROUP - 1 else (1, 0)
        result = jnp.dot(
            xs[part][pl.ds(begin, rows), :],
            w_all[pl.ds(0, half_cols), :],
            preferred_element_type=jnp.float32,
        ) + jnp.dot(
            xs[2 + part][pl.ds(begin, rows), :],
            w_all[pl.ds(half_cols, half_cols), :],
            preferred_element_type=jnp.float32,
        )
        tokens = pl.ds(block * rows, rows)
        for head in range(width // HEAD_SIZE):
            values = result[:, head * HEAD_SIZE : (head + 1) * HEAD_SIZE]
            mean = jnp.mean(values * values, axis=-1, keepdims=True)
            scaled = values * lax.rsqrt(mean + 1e-06) * gain[...]
            turned = (
                scaled * cosine[tokens, :]
                + pltpu.roll(scaled, HEAD_SIZE // 2, 1) * sine[tokens, :]
            )
            q_out[block][:, pl.ds(head * HEAD_SIZE, HEAD_SIZE)] = turned.astype(jnp.bfloat16)


def project(scal, xs, own_w, rest_w, cosine, sine, gain, first, width):
    planes = len(own_w)
    rows, half_cols = xs[1].shape
    depth = 2 * half_cols
    anywhere = pl.BlockSpec(memory_space=pl.ANY)
    vmem = pl.BlockSpec(memory_space=pltpu.VMEM)
    return pl.pallas_call(
        functools.partial(project_kernel, planes, first, width),
        out_shape=[jax.ShapeDtypeStruct((rows, width), jnp.bfloat16)] * GROUP,
        in_specs=[pl.BlockSpec(memory_space=pltpu.SMEM)]
        + [vmem] * 4
        + [anywhere] * (2 * planes)
        + [vmem] * 3,
        out_specs=[vmem] * GROUP,
        scratch_shapes=[
            pltpu.VMEM((depth, width), jnp.bfloat16),
            pltpu.SemaphoreType.DMA((planes, GROUP)),
        ],
        compiler_params=pltpu.CompilerParams(vmem_limit_bytes=VMEM_LIMIT),
        cost_estimate=pl.CostEstimate(
            flops=2 * GROUP * rows * depth * width,
            bytes_accessed=2 * depth * (GROUP * rows + width),
            transcendentals=0,
        ),
    )(scal, *xs, *own_w, *rest_w, cosine, sine, gain)


def project_kv_kernel(planes, skip, *refs):
    scal, refs = refs[0], refs[1:]
    xs, own_w, refs = refs[:4], refs[4 : 4 + planes], refs[4 + planes :]
    *kv_out, x_all, w_all, x_sem, w_sem = refs
    pos = scal[1]
    w_rows = own_w[0].shape[0]
    _, depth, width = w_all.shape
    compact = depth == w_rows
    offset = pos * w_rows if compact else 0

    copies = []
    for apart in range(planes):
        slot = half_slot(scal, planes, apart)
        row = 0
        if not compact:
            w_all[slot] = jnp.zeros((depth, width), jnp.bfloat16)
            row = pl.multiple_of(pos * w_rows, w_rows)
        copy = pltpu.make_async_copy(
            own_w[apart].at[:, pl.ds(skip, width)],
            w_all.at[slot, pl.ds(row, w_rows)],
            w_sem.at[apart],
        )
        copy.start()
        copies.append(copy)
    for slot in range(planes):
        half, within = slot // (planes // 2), slot % (planes // 2)
        column = pl.multiple_of(within * GROUP * w_rows + offset, HEAD_SIZE)
        begin = 0
        for part in range(2):
            src = xs[2 * half + part]
            copy = pltpu.make_async_copy(
                src.at[:, pl.ds(column, depth)],
                x_all.at[slot, pl.ds(begin, src.shape[0])],
                x_sem.at[slot, part],
            )
            copy.start()
            copies.append(copy)
            begin += src.shape[0]
    for copy in copies:
        copy.wait()
    result = None
    for slot in range(planes):
        term = jnp.dot(x_all[slot], w_all[slot], preferred_element_type=jnp.float32)
        result = term if result is None else result + term
    rows = kv_out[0].shape[0]
    for block in range(GROUP):
        term = result[block * rows : (block + 1) * rows]
        kv_out[block][...] = term.astype(kv_out[block].dtype)


def project_kv(scal, xs, own_w, skip):
    planes = len(own_w)
    rows = xs[1].shape[0]
    w_rows = own_w[0].shape[0]
    width = own_w[0].shape[1] - skip
    depth = w_rows if w_rows % HEAD_SIZE == 0 else GROUP * w_rows
    anywhere = pl.BlockSpec(memory_space=pl.ANY)
    return pl.pallas_call(
        functools.partial(project_kv_kernel, planes, skip),
        out_shape=[jax.ShapeDtypeStruct((rows, width), jnp.float32)]
        + [jax.ShapeDtypeStruct((rows, width), jnp.bfloat16)] * (GROUP - 1),
        in_specs=[pl.BlockSpec(memory_space=pltpu.SMEM)] + [anywhere] * (4 + planes),
        out_specs=[pl.BlockSpec(memory_space=pltpu.VMEM)] * GROUP,
        scratch_shapes=[
            pltpu.VMEM((planes, GROUP * rows, depth), jnp.bfloat16),
            pltpu.VMEM((planes, depth, width), jnp.bfloat16),
            pltpu.SemaphoreType.DMA((planes, 2)),
            pltpu.SemaphoreType.DMA((planes,)),
        ],
        compiler_params=pltpu.CompilerParams(vmem_limit_bytes=VMEM_LIMIT),
        cost_estimate=pl.CostEstimate(
            flops=2 * GROUP * rows * depth * planes * width,
            bytes_accessed=2 * depth * planes * (GROUP * rows + width),
            transcendentals=0,
        ),
    )(scal, *xs, *own_w)


def finish_kv_kernel(mine, *refs):
    *others, cosine, sine, gain, keys_out, values_out, both_out = refs
    summed = mine[...]
    for other in others:
        summed = summed + other[...].astype(jnp.float32)
    keys = summed[:, :HEAD_SIZE]
    mean = jnp.mean(keys * keys, axis=-1, keepdims=True)
    scaled = keys * lax.rsqrt(mean + 1e-06) * gain[...]
    own = pl.ds(0, keys.shape[0])
    turned = scaled * cosine[own, :] + pltpu.roll(scaled, HEAD_SIZE // 2, 1) * sine[own, :]
    keys_out[...] = turned.astype(jnp.bfloat16)
    values_out[...] = summed[:, HEAD_SIZE:].astype(jnp.bfloat16)
    both_out[0] = keys_out[...]
    both_out[1] = values_out[...]


def finish_kv(parts, cosine, sine, gain):
    rows = parts[0].shape[0]
    one = jax.ShapeDtypeStruct((rows, HEAD_SIZE), jnp.bfloat16)
    vmem = pl.BlockSpec(memory_space=pltpu.VMEM)
    return pl.pallas_call(
        finish_kv_kernel,
        out_shape=[one, one, jax.ShapeDtypeStruct((2, rows, HEAD_SIZE), jnp.bfloat16)],
        in_specs=[vmem] * (len(parts) + 3),
        out_specs=[vmem] * 3,
    )(*parts, cosine, sine, gain)


def attend_kernel(first, width, aliased, *refs):
    scal, order = refs[:2]
    qs = refs[2:6]
    keys_mine, values_mine, theirs, new_mine, new_theirs = refs[6:11]
    refs = refs[11 + int(aliased) :]
    out, k_all, v_all, vt_all, q_all, o_all, tops, totals, sums = refs[:9]
    kv_sem, new_sem, out_sem = refs[9:]
    pos, count = scal[1], scal[2]
    side = pos % 2
    rows = qs[0].shape[0]
    heads = width // HEAD_SIZE
    slots = order.shape[0]
    half_slots = slots // 2
    scale = HEAD_SIZE ** (-0.5) * math.log2(math.e)
    units = GROUP * heads
    lanes = rows

    def new_copy(new, kind, row, index):
        into = v_all if kind else k_all
        return pltpu.make_async_copy(
            new.at[kind], into.at[pl.ds(row, rows)], new_sem.at[index]
        )

    for kind in range(2):
        new_copy(new_mine, kind, 0, kind).start()

    @pl.when(side == 1)
    def _():
        for kind in range(2):
            new_copy(new_theirs, kind, rows, 2 + kind).start()

    lead = rows + side * rows

    their_row = theirs.shape[0] - BLOCK_TOKENS

    def block_copies(j):
        slot = order[j]
        within = pl.multiple_of((slot % half_slots) * BLOCK_TOKENS, BLOCK_TOKENS)
        dst_row = pl.multiple_of(lead + j * BLOCK_TOKENS, BLOCK_TOKENS)
        near = (slot // half_slots) == side

        def pair(k_src, v_src):
            rows_at = pl.ds(dst_row, BLOCK_TOKENS)
            return (
                pltpu.make_async_copy(k_src, k_all.at[rows_at], kv_sem.at[0, j]),
                pltpu.make_async_copy(v_src, v_all.at[rows_at], kv_sem.at[1, j]),
            )

        block = pl.ds(within, BLOCK_TOKENS)
        apart = half_slots * BLOCK_TOKENS
        beyond = pl.ds(pl.multiple_of(apart + within, BLOCK_TOKENS), BLOCK_TOKENS)
        there = pl.ds(their_row, BLOCK_TOKENS)
        return (
            near,
            pair(keys_mine.at[block], values_mine.at[block]),
            pair(theirs.at[there, block], theirs.at[there, beyond]),
        )

    def start_block(j, carry):
        near, mine, theirs = block_copies(j)

        @pl.when(near)
        def _():
            for copy in mine:
                copy.start()

        @pl.when(jnp.logical_not(near))
        def _():
            for copy in theirs:
                copy.start()

        return carry

    def wait_block(j, carry):
        _, mine, _ = block_copies(j)
        for copy in mine:
            copy.wait()
        return carry

    per_chunk = KEY_CHUNK // BLOCK_TOKENS
    blocks = count + side * (rows // BLOCK_TOKENS)
    full = blocks // per_chunk
    lax.fori_loop(0, count, start_block, 0)
    for r in range(GROUP):
        for head in range(heads):
            query = qs[r][:, pl.ds(head * HEAD_SIZE, HEAD_SIZE)].astype(jnp.float32)
            q_all[r * heads + head] = query.T.astype(jnp.bfloat16)

    def turn_values(row, size):
        values = v_all[pl.ds(row, size), :].astype(jnp.float32)
        vt_all[:, pl.ds(row, size)] = values.T.astype(jnp.bfloat16)

    def fold(values, combine):
        parts = values.reshape(values.shape[0] // 8, 8, lanes)
        return combine(parts, axis=0)

    def absorb(row, size, allowed, fresh):
        keys = k_all[pl.ds(row, size), :]
        values = vt_all[:, pl.ds(row, size)]

        def score(unit):
            return jnp.dot(keys, q_all[unit], preferred_element_type=jnp.float32)

        ahead = score(0)
        for unit in range(units):
            s = ahead
            if unit + 1 < units:
                ahead = score(unit + 1)
            if allowed is not None:
                s = jnp.where(allowed, s, -1e30)
            top = jnp.max(fold(s, jnp.max), axis=0, keepdims=True)
            if not fresh:
                before = tops[unit]
                top = jnp.maximum(before, top)
            weight = jnp.exp2((s - top) * scale)
            total = fold(weight, jnp.sum)
            mixed = jnp.dot(
                values, weight.astype(jnp.bfloat16), preferred_element_type=jnp.float32
            )
            if not fresh:
                shrink = jnp.exp2((before - top) * scale)
                total = total + totals[unit] * shrink
                mixed = mixed + sums[unit] * shrink
            tops[unit] = top
            totals[unit] = total
            sums[unit] = mixed

    for kind in range(2):
        new_copy(new_mine, kind, 0, kind).wait()
    turn_values(0, rows)
    key = lax.broadcasted_iota(jnp.int32, (rows, lanes), 0)
    token = lax.broadcasted_iota(jnp.int32, (rows, lanes), 1)
    absorb(0, rows, key <= token, True)

    @pl.when(side == 1)
    def _():
        for kind in range(2):
            new_copy(new_theirs, kind, rows, 2 + kind).wait()

    lax.fori_loop(0, count, wait_block, 0)

    def chunk_row(chunk):
        return pl.multiple_of(rows + chunk * KEY_CHUNK, BLOCK_TOKENS)

    def step(chunk, carry):
        turn_values(chunk_row(chunk), KEY_CHUNK)
        absorb(chunk_row(chunk), KEY_CHUNK, None, False)
        return carry

    lax.fori_loop(0, full, step, 0)

    part = per_chunk // 2
    while part:
        size = part * BLOCK_TOKENS

        @pl.when((blocks // part) % 2 == 1)
        def _(part=part, size=size):
            row = pl.multiple_of(
                rows + (blocks // (2 * part)) * 2 * size, BLOCK_TOKENS
            )
            turn_values(row, size)
            absorb(row, size, None, False)

        part //= 2

    group_cols = out.shape[1] // GROUP
    copies = []
    for r in range(GROUP):
        for head in range(heads):
            unit = r * heads + head
            total = jnp.sum(totals[unit], axis=0, keepdims=True)
            result = (sums[unit] / total).T.astype(jnp.bfloat16)
            o_all[r, :, pl.ds(head * HEAD_SIZE, HEAD_SIZE)] = result
        column = pl.multiple_of((pos ^ r) * group_cols + first, HEAD_SIZE)
        copy = pltpu.make_async_copy(
            o_all.at[r], out.at[:, pl.ds(column, width)], out_sem.at[r]
        )
        copy.start()
        copies.append(copy)
    for copy in copies:
        copy.wait()


def attend(scal, order, qs, caches, news, so_far, first, width, out_cols):
    rows = qs[0].shape[0]
    slots = order.shape[0]
    heads = width // HEAD_SIZE
    tokens = 2 * rows + slots * BLOCK_TOKENS
    anywhere = pl.BlockSpec(memory_space=pl.ANY)
    vmem = pl.BlockSpec(memory_space=pltpu.VMEM)
    smem = pl.BlockSpec(memory_space=pltpu.SMEM)
    operands = [scal, order, *qs, *caches, *news]
    in_specs = [smem] * 2 + [vmem] * 4 + [anywhere] * 5
    aliases = {}
    if so_far is not None:
        aliases = {len(operands): 0}
        operands.append(so_far)
        in_specs.append(anywhere)
    return pl.pallas_call(
        functools.partial(attend_kernel, first, width, so_far is not None),
        out_shape=jax.ShapeDtypeStruct((rows, out_cols), jnp.bfloat16),
        in_specs=in_specs,
        out_specs=anywhere,
        input_output_aliases=aliases,
        scratch_shapes=[
            pltpu.VMEM((tokens, HEAD_SIZE), jnp.bfloat16),
            pltpu.VMEM((tokens, HEAD_SIZE), jnp.bfloat16),
            pltpu.VMEM((HEAD_SIZE, tokens), jnp.bfloat16),
            pltpu.VMEM((GROUP * heads, HEAD_SIZE, rows), jnp.bfloat16),
            pltpu.VMEM((GROUP, rows, width), jnp.bfloat16),
            pltpu.VMEM((GROUP * heads, 1, rows), jnp.float32),
            pltpu.VMEM((GROUP * heads, 8, rows), jnp.float32),
            pltpu.VMEM((GROUP * heads, HEAD_SIZE, rows), jnp.float32),
            pltpu.SemaphoreType.DMA((2, slots)),
            pltpu.SemaphoreType.DMA((4,)),
            pltpu.SemaphoreType.DMA((GROUP,)),
        ],
        compiler_params=pltpu.CompilerParams(vmem_limit_bytes=VMEM_LIMIT),
        cost_estimate=pl.CostEstimate(
            flops=4 * GROUP * heads * rows * tokens * HEAD_SIZE,
            bytes_accessed=4 * tokens * HEAD_SIZE,
            transcendentals=GROUP * heads * rows * tokens,
        ),
    )(*operands)


def on_device(
    hidden,
    w_query,
    key_weight,
    value_weight,
    q_gain,
    key_norm_gain,
    earlier_keys,
    earlier_values,
    counts,
    place,
):
    planes = lax.axis_size("ctx") // GROUP
    ctx = lax.axis_index("ctx")
    plane = ctx // GROUP
    pos = ctx % GROUP
    rows = hidden.shape[0]
    w_rows = w_query.shape[0]
    group_cols = w_query.shape[1] // GROUP
    widths = (group_cols // 2, group_cols - group_cols // 2)

    def columns_for(r):
        return lax.dynamic_slice(w_query, (0, group_cols * (pos ^ r)), (w_rows, group_cols))

    count = lax.dynamic_index_in_dim(counts, ctx // 2, 0, keepdims=False)
    order = lax.dynamic_index_in_dim(place, ctx // 2, 0, keepdims=False)
    scal = jnp.stack([plane, pos, count, lax.axis_index("tp")]).astype(jnp.int32)
    spots = pos ^ jnp.arange(GROUP, dtype=jnp.int32)
    spot_counts = counts[plane * 2 + spots // 2]
    token_position = (
        spot_counts[:, None] * BLOCK_TOKENS
        + (spots % 2)[:, None] * rows
        + jnp.arange(rows, dtype=jnp.int32)[None, :]
    )
    cosine, sine = rope_tables(token_position.reshape(GROUP * rows))
    cache_mine = jnp.concatenate(
        [
            jnp.transpose(cache.reshape(-1, BLOCK_TOKENS, HEAD_SIZE), (1, 0, 2)).reshape(
                BLOCK_TOKENS, cache.shape[0]
            )
            for cache in (earlier_keys, earlier_values)
        ],
        axis=1,
    )
    across = GROUP * (planes // 2)
    few = rows // 4

    own = jnp.concatenate([columns_for(0), key_weight, value_weight], axis=1)
    own_far = swap(own, across)
    got = [swap(columns_for(r), r) for r in range(1, GROUP)]
    own_near = near(own, planes)
    first = jnp.concatenate([piece[:, : widths[0]] for piece in got], axis=1)
    second = jnp.concatenate([piece[:, widths[0] :] for piece in got], axis=1)
    hidden, first, second, own_far, cosine, sine, scal, order, cache_mine = gate(
        (hidden, first, second, own_far, cosine, sine, scal, order, cache_mine),
        (*got, *own_near),
    )

    x_1, x_2 = swap(hidden, 1), swap(hidden, 2)
    first_far = swap(first, across)
    first_near = near(first, planes)
    own_w = own_near + near(own_far, planes)
    x_1, x_2, second, first_far = gate(
        (x_1, x_2, second, first_far), (*first_near, *own_w[planes // 2 + 1 :])
    )

    message = swap(jnp.concatenate([x_2[:few], cache_mine]), 1)
    x_3 = jnp.concatenate([message[:few], swap(x_1[few:], 2)])
    x_near = jnp.concatenate([hidden, x_1, x_2])
    core_near = swap_core(x_near)
    second_far = swap(second, across)
    rest_first = first_near + near(first_far, planes)
    x_3, second, second_far = gate(
        (x_3, second, second_far), (core_near, *rest_first[planes // 2 + 1 :])
    )

    xs = [x_near, x_3, core_near, swap_core(x_3)]
    rest_second = near(second, planes) + near(second_far, planes)

    parts = project_kv(scal, xs, own_w, group_cols)
    parts = [parts[0]] + [swap(parts[r], r) for r in range(1, GROUP)]
    keys_mine, values_mine, new_mine = finish_kv(parts, cosine, sine, key_norm_gain[None, :])
    caches = (earlier_keys, earlier_values, message)
    news = (new_mine, swap(new_mine, 1))
    gain = q_gain[None, :]

    def queries(scal, rest_w, first, width):
        q = project(scal, xs, own_w, rest_w, cosine, sine, gain, first, width)
        return [q[0]] + [swap(q[r], r) for r in range(1, GROUP)]

    out_cols = w_query.shape[1]
    q_first = queries(
        scal, rest_first, 0, widths[0]
    )
    q_second = queries(after(scal, q_first[0], new_mine), rest_second, widths[0], widths[1])
    attended = attend(
        after(scal, q_second[0]), order, q_first, caches, news, None, 0, widths[0], out_cols
    )
    attended = attend(
        scal, order, q_second, caches, news, attended, widths[0], widths[1], out_cols
    )
    return (attended, keys_mine, values_mine)


def solution(mesh):
    placed = (
        P("ctx", "tp"),
        P("ctx", "tp"),
        P("ctx", "tp"),
        P("ctx", "tp"),
        P(),
        P(),
        P("ctx", "tp"),
        P("ctx", "tp"),
        P(),
        P(),
    )
    return jax.shard_map(
        on_device,
        mesh=mesh,
        in_specs=placed,
        out_specs=(P("ctx", "tp"), P("ctx", "tp"), P("ctx", "tp")),
        check_vma=False,
    )
```

```python
import functools
import math

import jax
import jax.numpy as jnp
from jax import lax
from jax.experimental import pallas as pl
from jax.experimental.pallas import tpu as pltpu
from jax.sharding import PartitionSpec as P

HEAD_SIZE = 128
BLOCK_TOKENS = 128
GROUP = 4
KEY_CHUNK = 512
VMEM_LIMIT = 16 * 1024 * 1024


def swap(value, mask):
    pairs = [(source, source ^ mask) for source in range(lax.axis_size("ctx"))]
    return lax.ppermute(value, "ctx", pairs)


def swap_core(value):
    return lax.ppermute(value, "tp", [(0, 1), (1, 0)])


def after(value, *others):
    return lax.optimization_barrier((value, *others))[0]


def near(source, planes):
    pieces = [source]
    bit = 1
    while bit < planes // 2:
        pieces = pieces + [swap(piece, GROUP * bit) for piece in pieces]
        bit *= 2
    return pieces


def gate(values, done):
    return lax.optimization_barrier((tuple(values), tuple(done)))[0]


def rope_tables(token_position):
    half = HEAD_SIZE // 2
    freq = jnp.exp(jnp.arange(half, dtype=jnp.float32) * (-2.0 / HEAD_SIZE) * math.log(1000000.0))
    angle = token_position.astype(jnp.float32)[..., None] * freq
    cosine, sine = jnp.cos(angle), jnp.sin(angle)
    return (
        jnp.concatenate([cosine, cosine], axis=-1),
        jnp.concatenate([-sine, sine], axis=-1),
    )


def half_slot(scal, planes, apart):
    there = scal[0] ^ apart
    other = (there // (planes // 2)) ^ scal[3]
    return other * (planes // 2) + there % (planes // 2)


def split_columns_kernel(widths, *refs):
    *got, first, second, sems = refs
    copies = []
    for index, piece in enumerate(got):
        begin = 0
        for part, out in enumerate((first, second)):
            cols = pl.ds(begin, widths[part])
            copy = pltpu.make_async_copy(
                piece.at[:, cols],
                out.at[:, pl.ds(index * widths[part], widths[part])],
                sems.at[index, part],
            )
            copy.start()
            copies.append(copy)
            begin += widths[part]
    for copy in copies:
        copy.wait()


def split_columns(got, widths):
    rows = got[0].shape[0]
    anywhere = pl.BlockSpec(memory_space=pl.ANY)
    return pl.pallas_call(
        functools.partial(split_columns_kernel, widths),
        out_shape=[
            jax.ShapeDtypeStruct((rows, len(got) * width), jnp.bfloat16) for width in widths
        ],
        in_specs=[anywhere] * len(got),
        out_specs=[anywhere] * 2,
        scratch_shapes=[pltpu.SemaphoreType.DMA((len(got), 2))],
        compiler_params=pltpu.CompilerParams(vmem_limit_bytes=VMEM_LIMIT // 16),
    )(*got)


def project_kernel(planes, first, width, *refs):
    scal, refs = refs[0], refs[1:]
    xs, refs = refs[:4], refs[4:]
    own_w, rest_w, refs = refs[:planes], refs[planes : 2 * planes], refs[2 * planes :]
    cosine, sine, gain, *q_out, w_all, w_sem = refs
    pos = scal[1]
    half_cols = xs[0].shape[1]
    w_rows = own_w[0].shape[0]

    copies = []
    for apart in range(planes):
        base = half_slot(scal, planes, apart) * GROUP
        for r in range(GROUP):
            if r == 0:
                src = own_w[apart].at[:, pl.ds(first, width)]
            else:
                src = rest_w[apart].at[:, pl.ds((r - 1) * width, width)]
            row = pl.multiple_of((base + (pos ^ r)) * w_rows, w_rows)
            copy = pltpu.make_async_copy(
                src, w_all.at[pl.ds(row, w_rows)], w_sem.at[apart, r]
            )
            copy.start()
            copies.append(copy)
    for copy in copies:
        copy.wait()

    rows = q_out[0].shape[0]
    for block in range(GROUP):
        part, begin = (0, block * rows) if block < GROUP - 1 else (1, 0)
        result = jnp.dot(
            xs[part][pl.ds(begin, rows), :],
            w_all[pl.ds(0, half_cols), :],
            preferred_element_type=jnp.float32,
        ) + jnp.dot(
            xs[2 + part][pl.ds(begin, rows), :],
            w_all[pl.ds(half_cols, half_cols), :],
            preferred_element_type=jnp.float32,
        )
        tokens = pl.ds(block * rows, rows)
        for head in range(width // HEAD_SIZE):
            values = result[:, head * HEAD_SIZE : (head + 1) * HEAD_SIZE]
            mean = jnp.mean(values * values, axis=-1, keepdims=True)
            scaled = values * lax.rsqrt(mean + 1e-06) * gain[...]
            turned = (
                scaled * cosine[tokens, :]
                + pltpu.roll(scaled, HEAD_SIZE // 2, 1) * sine[tokens, :]
            )
            q_out[block][:, pl.ds(head * HEAD_SIZE, HEAD_SIZE)] = turned.astype(jnp.bfloat16)


def project(scal, xs, own_w, rest_w, cosine, sine, gain, first, width):
    planes = len(own_w)
    rows, half_cols = xs[1].shape
    depth = 2 * half_cols
    anywhere = pl.BlockSpec(memory_space=pl.ANY)
    vmem = pl.BlockSpec(memory_space=pltpu.VMEM)
    return pl.pallas_call(
        functools.partial(project_kernel, planes, first, width),
        out_shape=[jax.ShapeDtypeStruct((rows, width), jnp.bfloat16)] * GROUP,
        in_specs=[pl.BlockSpec(memory_space=pltpu.SMEM)]
        + [vmem] * 4
        + [anywhere] * (2 * planes)
        + [vmem] * 3,
        out_specs=[vmem] * GROUP,
        scratch_shapes=[
            pltpu.VMEM((depth, width), jnp.bfloat16),
            pltpu.SemaphoreType.DMA((planes, GROUP)),
        ],
        compiler_params=pltpu.CompilerParams(vmem_limit_bytes=VMEM_LIMIT),
        cost_estimate=pl.CostEstimate(
            flops=2 * GROUP * rows * depth * width,
            bytes_accessed=2 * depth * (GROUP * rows + width),
            transcendentals=0,
        ),
    )(scal, *xs, *own_w, *rest_w, cosine, sine, gain)


def project_kv_kernel(planes, skip, *refs):
    scal, refs = refs[0], refs[1:]
    xs, own_w, refs = refs[:4], refs[4 : 4 + planes], refs[4 + planes :]
    *kv_out, x_all, w_all, x_sem, w_sem = refs
    pos = scal[1]
    w_rows = own_w[0].shape[0]
    _, depth, width = w_all.shape
    compact = depth == w_rows
    offset = pos * w_rows if compact else 0

    copies = []
    for apart in range(planes):
        slot = half_slot(scal, planes, apart)
        row = 0
        if not compact:
            w_all[slot] = jnp.zeros((depth, width), jnp.bfloat16)
            row = pl.multiple_of(pos * w_rows, w_rows)
        copy = pltpu.make_async_copy(
            own_w[apart].at[:, pl.ds(skip, width)],
            w_all.at[slot, pl.ds(row, w_rows)],
            w_sem.at[apart],
        )
        copy.start()
        copies.append(copy)
    for slot in range(planes):
        half, within = slot // (planes // 2), slot % (planes // 2)
        column = pl.multiple_of(within * GROUP * w_rows + offset, HEAD_SIZE)
        begin = 0
        for part in range(2):
            src = xs[2 * half + part]
            copy = pltpu.make_async_copy(
                src.at[:, pl.ds(column, depth)],
                x_all.at[slot, pl.ds(begin, src.shape[0])],
                x_sem.at[slot, part],
            )
            copy.start()
            copies.append(copy)
            begin += src.shape[0]
    for copy in copies:
        copy.wait()
    result = None
    for slot in range(planes):
        term = jnp.dot(x_all[slot], w_all[slot], preferred_element_type=jnp.float32)
        result = term if result is None else result + term
    rows = kv_out[0].shape[0]
    for block in range(GROUP):
        term = result[block * rows : (block + 1) * rows]
        kv_out[block][...] = term.astype(kv_out[block].dtype)


def project_kv(scal, xs, own_w, skip):
    planes = len(own_w)
    rows = xs[1].shape[0]
    w_rows = own_w[0].shape[0]
    width = own_w[0].shape[1] - skip
    depth = w_rows if w_rows % HEAD_SIZE == 0 else GROUP * w_rows
    anywhere = pl.BlockSpec(memory_space=pl.ANY)
    return pl.pallas_call(
        functools.partial(project_kv_kernel, planes, skip),
        out_shape=[jax.ShapeDtypeStruct((rows, width), jnp.float32)]
        + [jax.ShapeDtypeStruct((rows, width), jnp.bfloat16)] * (GROUP - 1),
        in_specs=[pl.BlockSpec(memory_space=pltpu.SMEM)] + [anywhere] * (4 + planes),
        out_specs=[pl.BlockSpec(memory_space=pltpu.VMEM)] * GROUP,
        scratch_shapes=[
            pltpu.VMEM((planes, GROUP * rows, depth), jnp.bfloat16),
            pltpu.VMEM((planes, depth, width), jnp.bfloat16),
            pltpu.SemaphoreType.DMA((planes, 2)),
            pltpu.SemaphoreType.DMA((planes,)),
        ],
        compiler_params=pltpu.CompilerParams(vmem_limit_bytes=VMEM_LIMIT),
        cost_estimate=pl.CostEstimate(
            flops=2 * GROUP * rows * depth * planes * width,
            bytes_accessed=2 * depth * planes * (GROUP * rows + width),
            transcendentals=0,
        ),
    )(scal, *xs, *own_w)


def finish_kv_kernel(mine, *refs):
    *others, cosine, sine, gain, keys_out, values_out, both_out = refs
    summed = mine[...]
    for other in others:
        summed = summed + other[...].astype(jnp.float32)
    keys = summed[:, :HEAD_SIZE]
    mean = jnp.mean(keys * keys, axis=-1, keepdims=True)
    scaled = keys * lax.rsqrt(mean + 1e-06) * gain[...]
    own = pl.ds(0, keys.shape[0])
    turned = scaled * cosine[own, :] + pltpu.roll(scaled, HEAD_SIZE // 2, 1) * sine[own, :]
    keys_out[...] = turned.astype(jnp.bfloat16)
    values_out[...] = summed[:, HEAD_SIZE:].astype(jnp.bfloat16)
    both_out[0] = keys_out[...]
    both_out[1] = values_out[...]


def finish_kv(parts, cosine, sine, gain):
    rows = parts[0].shape[0]
    one = jax.ShapeDtypeStruct((rows, HEAD_SIZE), jnp.bfloat16)
    vmem = pl.BlockSpec(memory_space=pltpu.VMEM)
    return pl.pallas_call(
        finish_kv_kernel,
        out_shape=[one, one, jax.ShapeDtypeStruct((2, rows, HEAD_SIZE), jnp.bfloat16)],
        in_specs=[vmem] * (len(parts) + 3),
        out_specs=[vmem] * 3,
        compiler_params=pltpu.CompilerParams(vmem_limit_bytes=VMEM_LIMIT // 4),
    )(*parts, cosine, sine, gain)


def attend_kernel(first, width, rows, aliased, *refs):
    scal, order = refs[:2]
    qs = refs[2:6]
    if aliased:
        k_all, vt_all, _, out, *refs = refs[6:]
    else:
        keys_mine, values_mine, theirs, new_mine, new_theirs, out, k_all, vt_all, *refs = refs[6:]
        v_all, kv_sem, new_sem, *refs = refs
    q_all, o_all, tops, totals, sums, out_sem = refs
    pos, count = scal[1], scal[2]
    side = pos % 2
    heads = width // HEAD_SIZE
    slots = order.shape[0]
    half_slots = slots // 2
    scale = HEAD_SIZE ** (-0.5) * math.log2(math.e)
    units = GROUP * heads
    lanes = rows

    lead = rows + side * rows

    def new_copy(new, kind, row, index):
        into = v_all if kind else k_all
        return pltpu.make_async_copy(
            new.at[kind], into.at[pl.ds(row, rows)], new_sem.at[index]
        )

    def block_copies(j):
        slot = order[j]
        within = pl.multiple_of((slot % half_slots) * BLOCK_TOKENS, BLOCK_TOKENS)
        dst_row = pl.multiple_of(lead + j * BLOCK_TOKENS, BLOCK_TOKENS)
        near = (slot // half_slots) == side

        def pair(k_src, v_src):
            rows_at = pl.ds(dst_row, BLOCK_TOKENS)
            return (
                pltpu.make_async_copy(k_src, k_all.at[rows_at], kv_sem.at[0, j]),
                pltpu.make_async_copy(v_src, v_all.at[rows_at], kv_sem.at[1, j]),
            )

        block = pl.ds(within, BLOCK_TOKENS)
        apart = half_slots * BLOCK_TOKENS
        beyond = pl.ds(pl.multiple_of(apart + within, BLOCK_TOKENS), BLOCK_TOKENS)
        there = pl.ds(theirs.shape[0] - BLOCK_TOKENS, BLOCK_TOKENS)
        return (
            near,
            pair(keys_mine.at[block], values_mine.at[block]),
            pair(theirs.at[there, block], theirs.at[there, beyond]),
        )

    def start_block(j, carry):
        near, mine, theirs = block_copies(j)

        @pl.when(near)
        def _():
            for copy in mine:
                copy.start()

        @pl.when(jnp.logical_not(near))
        def _():
            for copy in theirs:
                copy.start()

        return carry

    def wait_block(j, carry):
        _, mine, _ = block_copies(j)
        for copy in mine:
            copy.wait()
        return carry

    per_chunk = KEY_CHUNK // BLOCK_TOKENS
    blocks = count + side * (rows // BLOCK_TOKENS)
    full = blocks // per_chunk

    if not aliased:
        for kind in range(2):
            new_copy(new_mine, kind, 0, kind).start()

        @pl.when(side == 1)
        def _():
            for kind in range(2):
                new_copy(new_theirs, kind, rows, 2 + kind).start()

        lax.fori_loop(0, count, start_block, 0)

    for r in range(GROUP):
        for head in range(heads):
            q_all[r * heads + head] = qs[r][:, pl.ds(head * HEAD_SIZE, HEAD_SIZE)]

    def turn_values(row, size):
        if not aliased:
            values = v_all[pl.ds(row, size), :].astype(jnp.float32)
            vt_all[:, pl.ds(row, size)] = values.T.astype(jnp.bfloat16)

    def fold(values, combine):
        parts = values.reshape(values.shape[0] // 8, 8, lanes)
        return combine(parts, axis=0)

    def absorb(row, size, how, allowed=None):
        keys = k_all[pl.ds(row, size), :]
        values = vt_all[:, pl.ds(row, size)]

        def score(unit):
            return lax.dot_general(
                keys, q_all[unit], (((1,), (1,)), ((), ())), preferred_element_type=jnp.float32
            )

        ahead = score(0)
        for unit in range(units):
            s = ahead
            if unit + 1 < units:
                ahead = score(unit + 1)
            if allowed is not None:
                s = jnp.where(allowed, s, -1e30)
            top = before = None if how == "first" else tops[unit]
            if how != "same":
                top = jnp.max(fold(s, jnp.max), axis=0, keepdims=True)
                if how == "rising":
                    top = jnp.maximum(before, top)
                tops[unit] = top
            weight = jnp.exp2((s - top) * scale)
            total = fold(weight, jnp.sum)
            mixed = jnp.dot(
                values, weight.astype(jnp.bfloat16), preferred_element_type=jnp.float32
            )
            if how == "first":
                totals[unit] = total
                sums[unit] = mixed
            elif how == "same":
                totals[unit] += total
                sums[unit] += mixed
            else:
                shrink = jnp.exp2((before - top) * scale)
                totals[unit] = totals[unit] * shrink + total
                sums[unit] = sums[unit] * shrink + mixed

    def absorb_own():
        key = lax.broadcasted_iota(jnp.int32, (rows, lanes), 0)
        token = lax.broadcasted_iota(jnp.int32, (rows, lanes), 1)
        absorb(0, rows, "first", key <= token)

    def absorb_rest(how):
        def step(chunk, carry):
            row = pl.multiple_of(rows + chunk * KEY_CHUNK, BLOCK_TOKENS)
            if how == "same":
                turn_values(row, KEY_CHUNK)
            absorb(row, KEY_CHUNK, how)
            return carry

        lax.fori_loop(0, full, step, 0)
        part = per_chunk // 2
        while part:
            size = part * BLOCK_TOKENS

            @pl.when((blocks // part) % 2 == 1)
            def _(part=part, size=size):
                row = pl.multiple_of(rows + (blocks // (2 * part)) * 2 * size, BLOCK_TOKENS)
                if how == "same":
                    turn_values(row, size)
                absorb(row, size, how)

            part //= 2

    if not aliased:
        for kind in range(2):
            new_copy(new_mine, kind, 0, kind).wait()
        turn_values(0, rows)
    absorb_own()
    if not aliased:

        @pl.when(side == 1)
        def _():
            for kind in range(2):
                new_copy(new_theirs, kind, rows, 2 + kind).wait()

        lax.fori_loop(0, count, wait_block, 0)

    absorb_rest("same")
    fits = jnp.max(totals[...]) < 2.0**100

    @pl.when(jnp.logical_not(fits))
    def _():
        absorb_own()
        absorb_rest("rising")

    group_cols = out.shape[1] // GROUP
    copies = []
    for r in range(GROUP):
        for head in range(heads):
            unit = r * heads + head
            total = jnp.sum(totals[unit], axis=0, keepdims=True)
            result = (sums[unit] / total).T.astype(jnp.bfloat16)
            o_all[r, :, pl.ds(head * HEAD_SIZE, HEAD_SIZE)] = result
        column = pl.multiple_of((pos ^ r) * group_cols + first, HEAD_SIZE)
        copy = pltpu.make_async_copy(
            o_all.at[r], out.at[:, pl.ds(column, width)], out_sem.at[r]
        )
        copy.start()
        copies.append(copy)
    for copy in copies:
        copy.wait()


def attend(scal, order, qs, sources, first, width, out_cols, tokens):
    rows = qs[0].shape[0]
    slots = order.shape[0]
    heads = width // HEAD_SIZE
    units = GROUP * heads
    aliased = len(sources) == 3
    anywhere = pl.BlockSpec(memory_space=pl.ANY)
    vmem = pl.BlockSpec(memory_space=pltpu.VMEM)
    smem = pl.BlockSpec(memory_space=pltpu.SMEM)
    in_specs = [smem] * 2 + [vmem] * 4
    out_shape = [jax.ShapeDtypeStruct((rows, out_cols), jnp.bfloat16)]
    scratch = []
    if aliased:
        in_specs += [vmem, vmem, anywhere]
    else:
        in_specs += [anywhere] * len(sources)
        out_shape += [
            jax.ShapeDtypeStruct((tokens, HEAD_SIZE), jnp.bfloat16),
            jax.ShapeDtypeStruct((HEAD_SIZE, tokens), jnp.bfloat16),
        ]
        scratch += [
            pltpu.VMEM((tokens, HEAD_SIZE), jnp.bfloat16),
            pltpu.SemaphoreType.DMA((2, slots)),
            pltpu.SemaphoreType.DMA((4,)),
        ]
    scratch += [
        pltpu.VMEM((units, rows, HEAD_SIZE), jnp.bfloat16),
        pltpu.VMEM((GROUP, rows, width), jnp.bfloat16),
        pltpu.VMEM((units, 1, rows), jnp.float32),
        pltpu.VMEM((units, 8, rows), jnp.float32),
        pltpu.VMEM((units, HEAD_SIZE, rows), jnp.float32),
        pltpu.SemaphoreType.DMA((GROUP,)),
    ]
    return pl.pallas_call(
        functools.partial(attend_kernel, first, width, rows, aliased),
        out_shape=out_shape,
        in_specs=in_specs,
        out_specs=[anywhere] + [vmem] * (len(out_shape) - 1),
        input_output_aliases={8: 0} if aliased else {},
        scratch_shapes=scratch,
        compiler_params=pltpu.CompilerParams(vmem_limit_bytes=VMEM_LIMIT),
        cost_estimate=pl.CostEstimate(
            flops=4 * units * rows * tokens * HEAD_SIZE,
            bytes_accessed=4 * tokens * HEAD_SIZE,
            transcendentals=units * rows * tokens,
        ),
    )(scal, order, *qs, *sources)


def on_device(
    hidden,
    w_query,
    key_weight,
    value_weight,
    q_gain,
    key_norm_gain,
    earlier_keys,
    earlier_values,
    counts,
    place,
):
    planes = lax.axis_size("ctx") // GROUP
    ctx = lax.axis_index("ctx")
    plane = ctx // GROUP
    pos = ctx % GROUP
    rows = hidden.shape[0]
    w_rows = w_query.shape[0]
    group_cols = w_query.shape[1] // GROUP
    widths = (group_cols // 2, group_cols - group_cols // 2)

    def columns_for(r):
        return lax.dynamic_slice(w_query, (0, group_cols * (pos ^ r)), (w_rows, group_cols))

    count = lax.dynamic_index_in_dim(counts, ctx // 2, 0, keepdims=False)
    order = lax.dynamic_index_in_dim(place, ctx // 2, 0, keepdims=False)
    scal = jnp.stack([plane, pos, count, lax.axis_index("tp")]).astype(jnp.int32)
    spots = pos ^ jnp.arange(GROUP, dtype=jnp.int32)
    spot_counts = counts[plane * 2 + spots // 2]
    token_position = (
        spot_counts[:, None] * BLOCK_TOKENS
        + (spots % 2)[:, None] * rows
        + jnp.arange(rows, dtype=jnp.int32)[None, :]
    )
    cosine, sine = rope_tables(token_position.reshape(GROUP * rows))
    cache_mine = jnp.concatenate(
        [
            jnp.transpose(cache.reshape(-1, BLOCK_TOKENS, HEAD_SIZE), (1, 0, 2)).reshape(
                BLOCK_TOKENS, cache.shape[0]
            )
            for cache in (earlier_keys, earlier_values)
        ],
        axis=1,
    )
    across = GROUP * (planes // 2)
    few = rows // 4

    own = jnp.concatenate([columns_for(0), key_weight, value_weight], axis=1)
    own_far = swap(own, across)
    got = [swap(columns_for(r), r) for r in range(1, GROUP)]
    own_near = near(own, planes)
    first, second = split_columns(got, widths)
    hidden, first, second, own_far, cosine, sine, scal, order, cache_mine = gate(
        (hidden, first, second, own_far, cosine, sine, scal, order, cache_mine),
        (*got, *own_near),
    )

    x_1, x_2 = swap(hidden, 1), swap(hidden, 2)
    first_far = swap(first, across)
    first_near = near(first, planes)
    own_w = own_near + near(own_far, planes)
    x_1, x_2, second, first_far = gate(
        (x_1, x_2, second, first_far), (*first_near, *own_w[planes // 2 + 1 :])
    )

    message = swap(jnp.concatenate([x_2[:few], cache_mine]), 1)
    x_3 = jnp.concatenate([message[:few], swap(x_1[few:], 2)])
    x_near = jnp.concatenate([hidden, x_1, x_2])
    core_near = swap_core(x_near)
    second_far = swap(second, across)
    rest_first = first_near + near(first_far, planes)
    x_3, second, second_far = gate(
        (x_3, second, second_far), (core_near, *rest_first[planes // 2 + 1 :])
    )

    xs = [x_near, x_3, core_near, swap_core(x_3)]
    rest_second = near(second, planes) + near(second_far, planes)

    parts = project_kv(scal, xs, own_w, group_cols)
    parts = [parts[0]] + [swap(parts[r], r) for r in range(1, GROUP)]
    keys_mine, values_mine, new_mine = finish_kv(parts, cosine, sine, key_norm_gain[None, :])
    caches = (earlier_keys, earlier_values, message)
    news = (new_mine, swap(new_mine, 1))
    gain = q_gain[None, :]

    def queries(scal, rest_w, first, width):
        q = project(scal, xs, own_w, rest_w, cosine, sine, gain, first, width)
        return [q[0]] + [swap(q[r], r) for r in range(1, GROUP)]

    out_cols = w_query.shape[1]
    q_first = queries(
        scal, rest_first, 0, widths[0]
    )
    q_second = queries(after(scal, q_first[0], new_mine), rest_second, widths[0], widths[1])
    tokens = 2 * rows + place.shape[1] * BLOCK_TOKENS
    attended, all_keys, all_values = attend(
        after(scal, q_second[0]), order, q_first, (*caches, *news), 0, widths[0], out_cols, tokens
    )
    (attended,) = attend(
        scal,
        order,
        q_second,
        (all_keys, all_values, attended),
        widths[0],
        widths[1],
        out_cols,
        tokens,
    )
    return (attended, keys_mine, values_mine)


def solution(mesh):
    placed = (
        P("ctx", "tp"),
        P("ctx", "tp"),
        P("ctx", "tp"),
        P("ctx", "tp"),
        P(),
        P(),
        P("ctx", "tp"),
        P("ctx", "tp"),
        P(),
        P(),
    )
    return jax.shard_map(
        on_device,
        mesh=mesh,
        in_specs=placed,
        out_specs=(P("ctx", "tp"), P("ctx", "tp"), P("ctx", "tp")),
        check_vma=False,
    )
```

```python
import functools
import math

import jax
import jax.numpy as jnp
from jax import lax
from jax.experimental import pallas as pl
from jax.experimental.pallas import tpu as pltpu
from jax.sharding import PartitionSpec as P

HEAD_SIZE = 128
BLOCK_TOKENS = 128
GROUP = 4
KEY_CHUNK = 512
VMEM_LIMIT = 16 * 1024 * 1024


def swap(value, mask):
    pairs = [(source, source ^ mask) for source in range(lax.axis_size("ctx"))]
    return lax.ppermute(value, "ctx", pairs)


def swap_core(value):
    return lax.ppermute(value, "tp", [(0, 1), (1, 0)])


def after(value, *others):
    return lax.optimization_barrier((value, *others))[0]


def near(source, planes):
    pieces = [source]
    bit = 1
    while bit < planes // 2:
        pieces = pieces + [swap(piece, GROUP * bit) for piece in pieces]
        bit *= 2
    return pieces


def gate(values, done):
    return lax.optimization_barrier((tuple(values), tuple(done)))[0]


def rope_tables(token_position):
    half = HEAD_SIZE // 2
    freq = jnp.exp(jnp.arange(half, dtype=jnp.float32) * (-2.0 / HEAD_SIZE) * math.log(1000000.0))
    angle = token_position.astype(jnp.float32)[..., None] * freq
    cosine, sine = jnp.cos(angle), jnp.sin(angle)
    return (
        jnp.concatenate([cosine, cosine], axis=-1),
        jnp.concatenate([-sine, sine], axis=-1),
    )


def half_slot(scal, planes, apart):
    there = scal[0] ^ apart
    other = (there // (planes // 2)) ^ scal[3]
    return other * (planes // 2) + there % (planes // 2)


def pick_columns_kernel(w_ref, key_ref, value_ref, own, *refs):
    *others, sems = refs
    pos = lax.axis_index("ctx") % GROUP
    cols = others[0].shape[1]

    def columns_for(r):
        return w_ref.at[:, pl.ds(pl.multiple_of((pos ^ r) * cols, cols), cols)]

    pairs = [
        (columns_for(0), own.at[:, pl.ds(0, cols)]),
        (key_ref, own.at[:, pl.ds(cols, HEAD_SIZE)]),
        (value_ref, own.at[:, pl.ds(cols + HEAD_SIZE, HEAD_SIZE)]),
    ]
    pairs += [(columns_for(1 + index), out) for index, out in enumerate(others)]
    copies = []
    for index, (src, dst) in enumerate(pairs):
        copy = pltpu.make_async_copy(src, dst, sems.at[index])
        copy.start()
        copies.append(copy)
    for copy in copies:
        copy.wait()


def pick_columns(w_query, key_weight, value_weight):
    rows = w_query.shape[0]
    cols = w_query.shape[1] // GROUP
    anywhere = pl.BlockSpec(memory_space=pl.ANY)
    widths = [cols + 2 * HEAD_SIZE] + [cols] * (GROUP - 1)
    return pl.pallas_call(
        pick_columns_kernel,
        out_shape=[jax.ShapeDtypeStruct((rows, width), jnp.bfloat16) for width in widths],
        in_specs=[anywhere] * 3,
        out_specs=[anywhere] * GROUP,
        scratch_shapes=[pltpu.SemaphoreType.DMA((GROUP + 2,))],
        compiler_params=pltpu.CompilerParams(vmem_limit_bytes=60 * 1024 * 1024),
    )(w_query, key_weight, value_weight)


def split_columns_kernel(widths, *refs):
    *got, first, second, sems = refs
    copies = []
    for index, piece in enumerate(got):
        begin = 0
        for part, out in enumerate((first, second)):
            cols = pl.ds(begin, widths[part])
            copy = pltpu.make_async_copy(
                piece.at[:, cols],
                out.at[:, pl.ds(index * widths[part], widths[part])],
                sems.at[index, part],
            )
            copy.start()
            copies.append(copy)
            begin += widths[part]
    for copy in copies:
        copy.wait()


def split_columns(got, widths):
    rows = got[0].shape[0]
    anywhere = pl.BlockSpec(memory_space=pl.ANY)
    return pl.pallas_call(
        functools.partial(split_columns_kernel, widths),
        out_shape=[
            jax.ShapeDtypeStruct((rows, len(got) * width), jnp.bfloat16) for width in widths
        ],
        in_specs=[anywhere] * len(got),
        out_specs=[anywhere] * 2,
        scratch_shapes=[pltpu.SemaphoreType.DMA((len(got), 2))],
        compiler_params=pltpu.CompilerParams(vmem_limit_bytes=VMEM_LIMIT // 16),
    )(*got)


def project_kernel(planes, first, width, *refs):
    scal, refs = refs[0], refs[1:]
    xs, refs = refs[:4], refs[4:]
    own_w, rest_w, refs = refs[:planes], refs[planes : 2 * planes], refs[2 * planes :]
    cosine, sine, gain, *q_out, w_all, w_sem = refs
    pos = scal[1]
    half_cols = xs[0].shape[1]
    w_rows = own_w[0].shape[0]

    copies = []
    for apart in range(planes):
        base = half_slot(scal, planes, apart) * GROUP
        for r in range(GROUP):
            if r == 0:
                src = own_w[apart].at[:, pl.ds(first, width)]
            else:
                src = rest_w[apart].at[:, pl.ds((r - 1) * width, width)]
            row = pl.multiple_of((base + (pos ^ r)) * w_rows, w_rows)
            copy = pltpu.make_async_copy(
                src, w_all.at[pl.ds(row, w_rows)], w_sem.at[apart, r]
            )
            copy.start()
            copies.append(copy)
    for copy in copies:
        copy.wait()

    rows = q_out[0].shape[0]
    for block in range(GROUP):
        part, begin = (0, block * rows) if block < GROUP - 1 else (1, 0)
        result = jnp.dot(
            xs[part][pl.ds(begin, rows), :],
            w_all[pl.ds(0, half_cols), :],
            preferred_element_type=jnp.float32,
        ) + jnp.dot(
            xs[2 + part][pl.ds(begin, rows), :],
            w_all[pl.ds(half_cols, half_cols), :],
            preferred_element_type=jnp.float32,
        )
        tokens = pl.ds(block * rows, rows)
        for head in range(width // HEAD_SIZE):
            values = result[:, head * HEAD_SIZE : (head + 1) * HEAD_SIZE]
            mean = jnp.mean(values * values, axis=-1, keepdims=True)
            scaled = values * lax.rsqrt(mean + 1e-06) * gain[...]
            turned = (
                scaled * cosine[tokens, :]
                + pltpu.roll(scaled, HEAD_SIZE // 2, 1) * sine[tokens, :]
            )
            q_out[block][:, pl.ds(head * HEAD_SIZE, HEAD_SIZE)] = turned.astype(jnp.bfloat16)


def project(scal, xs, own_w, rest_w, cosine, sine, gain, first, width):
    planes = len(own_w)
    rows, half_cols = xs[1].shape
    depth = 2 * half_cols
    anywhere = pl.BlockSpec(memory_space=pl.ANY)
    vmem = pl.BlockSpec(memory_space=pltpu.VMEM)
    return pl.pallas_call(
        functools.partial(project_kernel, planes, first, width),
        out_shape=[jax.ShapeDtypeStruct((rows, width), jnp.bfloat16)] * GROUP,
        in_specs=[pl.BlockSpec(memory_space=pltpu.SMEM)]
        + [vmem] * 4
        + [anywhere] * (2 * planes)
        + [vmem] * 3,
        out_specs=[vmem] * GROUP,
        scratch_shapes=[
            pltpu.VMEM((depth, width), jnp.bfloat16),
            pltpu.SemaphoreType.DMA((planes, GROUP)),
        ],
        compiler_params=pltpu.CompilerParams(vmem_limit_bytes=VMEM_LIMIT),
        cost_estimate=pl.CostEstimate(
            flops=2 * GROUP * rows * depth * width,
            bytes_accessed=2 * depth * (GROUP * rows + width),
            transcendentals=0,
        ),
    )(scal, *xs, *own_w, *rest_w, cosine, sine, gain)


def project_kv_kernel(planes, skip, *refs):
    scal, refs = refs[0], refs[1:]
    xs, own_w, refs = refs[:2], refs[2 : 2 + planes], refs[2 + planes :]
    *kv_out, x_all, w_all, x_sem, w_sem = refs
    pos = scal[1]
    w_rows = own_w[0].shape[0]
    _, depth, width = w_all.shape
    compact = depth == w_rows
    offset = pos * w_rows if compact else 0

    copies = []
    for apart in range(planes):
        slot = half_slot(scal, planes, apart)
        row = 0
        if not compact:
            w_all[slot] = jnp.zeros((depth, width), jnp.bfloat16)
            row = pl.multiple_of(pos * w_rows, w_rows)
        copy = pltpu.make_async_copy(
            own_w[apart].at[:, pl.ds(skip, width)],
            w_all.at[slot, pl.ds(row, w_rows)],
            w_sem.at[apart],
        )
        copy.start()
        copies.append(copy)
    for slot in range(planes):
        half, within = slot // (planes // 2), slot % (planes // 2)
        column = pl.multiple_of(within * GROUP * w_rows + offset, HEAD_SIZE)
        copy = pltpu.make_async_copy(
            xs[half].at[:, pl.ds(column, depth)], x_all.at[slot], x_sem.at[slot]
        )
        copy.start()
        copies.append(copy)
    for copy in copies:
        copy.wait()
    result = None
    for slot in range(planes):
        term = jnp.dot(x_all[slot], w_all[slot], preferred_element_type=jnp.float32)
        result = term if result is None else result + term
    rows = kv_out[0].shape[0]
    for block, out in enumerate(kv_out):
        out[...] = result[block * rows : (block + 1) * rows]


def project_kv(scal, xs, own_w, skip, rows):
    planes = len(own_w)
    tokens = xs[0].shape[0]
    w_rows = own_w[0].shape[0]
    width = own_w[0].shape[1] - skip
    depth = w_rows if w_rows % HEAD_SIZE == 0 else GROUP * w_rows
    anywhere = pl.BlockSpec(memory_space=pl.ANY)
    return pl.pallas_call(
        functools.partial(project_kv_kernel, planes, skip),
        out_shape=[jax.ShapeDtypeStruct((rows, width), jnp.float32)] * (tokens // rows),
        in_specs=[pl.BlockSpec(memory_space=pltpu.SMEM)] + [anywhere] * (2 + planes),
        out_specs=[pl.BlockSpec(memory_space=pltpu.VMEM)] * (tokens // rows),
        scratch_shapes=[
            pltpu.VMEM((planes, tokens, depth), jnp.bfloat16),
            pltpu.VMEM((planes, depth, width), jnp.bfloat16),
            pltpu.SemaphoreType.DMA((planes,)),
            pltpu.SemaphoreType.DMA((planes,)),
        ],
        compiler_params=pltpu.CompilerParams(vmem_limit_bytes=VMEM_LIMIT),
        cost_estimate=pl.CostEstimate(
            flops=2 * tokens * depth * planes * width,
            bytes_accessed=2 * depth * planes * (tokens + width),
            transcendentals=0,
        ),
    )(scal, *xs, *own_w)


def finish_kv_kernel(mine, *refs):
    *others, cosine, sine, gain, keys_out, values_out, both_out = refs
    summed = mine[...]
    for other in others:
        summed = summed + other[...]
    keys = summed[:, :HEAD_SIZE]
    mean = jnp.mean(keys * keys, axis=-1, keepdims=True)
    scaled = keys * lax.rsqrt(mean + 1e-06) * gain[...]
    own = pl.ds(0, keys.shape[0])
    turned = scaled * cosine[own, :] + pltpu.roll(scaled, HEAD_SIZE // 2, 1) * sine[own, :]
    keys_out[...] = turned.astype(jnp.bfloat16)
    values_out[...] = summed[:, HEAD_SIZE:].astype(jnp.bfloat16)
    both_out[0] = keys_out[...]
    both_out[1] = values_out[...]


def finish_kv(parts, cosine, sine, gain):
    rows = parts[0].shape[0]
    one = jax.ShapeDtypeStruct((rows, HEAD_SIZE), jnp.bfloat16)
    vmem = pl.BlockSpec(memory_space=pltpu.VMEM)
    return pl.pallas_call(
        finish_kv_kernel,
        out_shape=[one, one, jax.ShapeDtypeStruct((2, rows, HEAD_SIZE), jnp.bfloat16)],
        in_specs=[vmem] * (len(parts) + 3),
        out_specs=[vmem] * 3,
        compiler_params=pltpu.CompilerParams(vmem_limit_bytes=VMEM_LIMIT // 4),
    )(*parts, cosine, sine, gain)


def attend_kernel(first, width, rows, aliased, *refs):
    scal, order = refs[:2]
    qs = refs[2:6]
    if aliased:
        k_all, vt_all, _, out, *refs = refs[6:]
    else:
        keys_mine, values_mine, theirs, new_mine, new_theirs, out, k_all, vt_all, *refs = refs[6:]
        v_all, kv_sem, new_sem, *refs = refs
    q_all, o_all, tops, totals, sums, out_sem = refs
    pos, count = scal[1], scal[2]
    side = pos % 2
    heads = width // HEAD_SIZE
    slots = order.shape[0]
    half_slots = slots // 2
    scale = HEAD_SIZE ** (-0.5) * math.log2(math.e)
    units = GROUP * heads
    lanes = rows

    lead = rows + side * rows

    def new_copy(new, kind, row, index):
        into = v_all if kind else k_all
        return pltpu.make_async_copy(
            new.at[kind], into.at[pl.ds(row, rows)], new_sem.at[index]
        )

    def block_copies(j):
        slot = order[j]
        within = pl.multiple_of((slot % half_slots) * BLOCK_TOKENS, BLOCK_TOKENS)
        dst_row = pl.multiple_of(lead + j * BLOCK_TOKENS, BLOCK_TOKENS)
        near = (slot // half_slots) == side

        def pair(k_src, v_src):
            rows_at = pl.ds(dst_row, BLOCK_TOKENS)
            return (
                pltpu.make_async_copy(k_src, k_all.at[rows_at], kv_sem.at[0, j]),
                pltpu.make_async_copy(v_src, v_all.at[rows_at], kv_sem.at[1, j]),
            )

        block = pl.ds(within, BLOCK_TOKENS)
        apart = half_slots * BLOCK_TOKENS
        beyond = pl.ds(pl.multiple_of(apart + within, BLOCK_TOKENS), BLOCK_TOKENS)
        there = pl.ds(theirs.shape[0] - BLOCK_TOKENS, BLOCK_TOKENS)
        return (
            near,
            pair(keys_mine.at[block], values_mine.at[block]),
            pair(theirs.at[there, block], theirs.at[there, beyond]),
        )

    def start_block(j, carry):
        near, mine, theirs = block_copies(j)

        @pl.when(near)
        def _():
            for copy in mine:
                copy.start()

        @pl.when(jnp.logical_not(near))
        def _():
            for copy in theirs:
                copy.start()

        return carry

    def wait_block(j, carry):
        _, mine, _ = block_copies(j)
        for copy in mine:
            copy.wait()
        return carry

    per_chunk = KEY_CHUNK // BLOCK_TOKENS
    blocks = count + side * (rows // BLOCK_TOKENS)
    full = blocks // per_chunk

    if not aliased:
        for kind in range(2):
            new_copy(new_mine, kind, 0, kind).start()

        @pl.when(side == 1)
        def _():
            for kind in range(2):
                new_copy(new_theirs, kind, rows, 2 + kind).start()

        lax.fori_loop(0, count, start_block, 0)

    for r in range(GROUP):
        for head in range(heads):
            q_all[r * heads + head] = qs[r][:, pl.ds(head * HEAD_SIZE, HEAD_SIZE)]

    def turn_values(row, size):
        if not aliased:
            values = v_all[pl.ds(row, size), :].astype(jnp.float32)
            vt_all[:, pl.ds(row, size)] = values.T.astype(jnp.bfloat16)

    def fold(values, combine):
        parts = values.reshape(values.shape[0] // 8, 8, lanes)
        return combine(parts, axis=0)

    def absorb(row, size, how, allowed=None):
        keys = k_all[pl.ds(row, size), :]
        values = vt_all[:, pl.ds(row, size)]

        def score(unit):
            return lax.dot_general(
                keys, q_all[unit], (((1,), (1,)), ((), ())), preferred_element_type=jnp.float32
            )

        ahead = score(0)
        for unit in range(units):
            s = ahead
            if unit + 1 < units:
                ahead = score(unit + 1)
            if allowed is not None:
                s = jnp.where(allowed, s, -1e30)
            top = before = None if how == "first" else tops[unit]
            if how != "same":
                top = jnp.max(fold(s, jnp.max), axis=0, keepdims=True)
                if how == "rising":
                    top = jnp.maximum(before, top)
                tops[unit] = top
            weight = jnp.exp2((s - top) * scale)
            total = fold(weight, jnp.sum)
            mixed = jnp.dot(
                values, weight.astype(jnp.bfloat16), preferred_element_type=jnp.float32
            )
            if how == "first":
                totals[unit] = total
                sums[unit] = mixed
            elif how == "same":
                totals[unit] += total
                sums[unit] += mixed
            else:
                shrink = jnp.exp2((before - top) * scale)
                totals[unit] = totals[unit] * shrink + total
                sums[unit] = sums[unit] * shrink + mixed

    def absorb_own():
        key = lax.broadcasted_iota(jnp.int32, (rows, lanes), 0)
        token = lax.broadcasted_iota(jnp.int32, (rows, lanes), 1)
        absorb(0, rows, "first", key <= token)

    def absorb_rest(how):
        def step(chunk, carry):
            row = pl.multiple_of(rows + chunk * KEY_CHUNK, BLOCK_TOKENS)
            if how == "same":
                turn_values(row, KEY_CHUNK)
            absorb(row, KEY_CHUNK, how)
            return carry

        lax.fori_loop(0, full, step, 0)
        part = per_chunk // 2
        while part:
            size = part * BLOCK_TOKENS

            @pl.when((blocks // part) % 2 == 1)
            def _(part=part, size=size):
                row = pl.multiple_of(rows + (blocks // (2 * part)) * 2 * size, BLOCK_TOKENS)
                if how == "same":
                    turn_values(row, size)
                absorb(row, size, how)

            part //= 2

    if not aliased:
        for kind in range(2):
            new_copy(new_mine, kind, 0, kind).wait()
        turn_values(0, rows)
    absorb_own()
    if not aliased:

        @pl.when(side == 1)
        def _():
            for kind in range(2):
                new_copy(new_theirs, kind, rows, 2 + kind).wait()

        lax.fori_loop(0, count, wait_block, 0)

    absorb_rest("same")
    fits = jnp.max(totals[...]) < 2.0**100

    @pl.when(jnp.logical_not(fits))
    def _():
        absorb_own()
        absorb_rest("rising")

    group_cols = out.shape[1] // GROUP
    copies = []
    for r in range(GROUP):
        for head in range(heads):
            unit = r * heads + head
            total = jnp.sum(totals[unit], axis=0, keepdims=True)
            result = (sums[unit] / total).T.astype(jnp.bfloat16)
            o_all[r, :, pl.ds(head * HEAD_SIZE, HEAD_SIZE)] = result
        column = pl.multiple_of((pos ^ r) * group_cols + first, HEAD_SIZE)
        copy = pltpu.make_async_copy(
            o_all.at[r], out.at[:, pl.ds(column, width)], out_sem.at[r]
        )
        copy.start()
        copies.append(copy)
    for copy in copies:
        copy.wait()


def attend(scal, order, qs, sources, first, width, out_cols, tokens):
    rows = qs[0].shape[0]
    slots = order.shape[0]
    heads = width // HEAD_SIZE
    units = GROUP * heads
    aliased = len(sources) == 3
    anywhere = pl.BlockSpec(memory_space=pl.ANY)
    vmem = pl.BlockSpec(memory_space=pltpu.VMEM)
    smem = pl.BlockSpec(memory_space=pltpu.SMEM)
    in_specs = [smem] * 2 + [vmem] * 4
    out_shape = [jax.ShapeDtypeStruct((rows, out_cols), jnp.bfloat16)]
    scratch = []
    if aliased:
        in_specs += [vmem, vmem, anywhere]
    else:
        in_specs += [anywhere] * len(sources)
        out_shape += [
            jax.ShapeDtypeStruct((tokens, HEAD_SIZE), jnp.bfloat16),
            jax.ShapeDtypeStruct((HEAD_SIZE, tokens), jnp.bfloat16),
        ]
        scratch += [
            pltpu.VMEM((tokens, HEAD_SIZE), jnp.bfloat16),
            pltpu.SemaphoreType.DMA((2, slots)),
            pltpu.SemaphoreType.DMA((4,)),
        ]
    scratch += [
        pltpu.VMEM((units, rows, HEAD_SIZE), jnp.bfloat16),
        pltpu.VMEM((GROUP, rows, width), jnp.bfloat16),
        pltpu.VMEM((units, 1, rows), jnp.float32),
        pltpu.VMEM((units, 8, rows), jnp.float32),
        pltpu.VMEM((units, HEAD_SIZE, rows), jnp.float32),
        pltpu.SemaphoreType.DMA((GROUP,)),
    ]
    return pl.pallas_call(
        functools.partial(attend_kernel, first, width, rows, aliased),
        out_shape=out_shape,
        in_specs=in_specs,
        out_specs=[anywhere] + [vmem] * (len(out_shape) - 1),
        input_output_aliases={8: 0} if aliased else {},
        scratch_shapes=scratch,
        compiler_params=pltpu.CompilerParams(vmem_limit_bytes=VMEM_LIMIT),
        cost_estimate=pl.CostEstimate(
            flops=4 * units * rows * tokens * HEAD_SIZE,
            bytes_accessed=4 * tokens * HEAD_SIZE,
            transcendentals=units * rows * tokens,
        ),
    )(scal, order, *qs, *sources)


def on_device(
    hidden,
    w_query,
    key_weight,
    value_weight,
    q_gain,
    key_norm_gain,
    earlier_keys,
    earlier_values,
    counts,
    place,
):
    planes = lax.axis_size("ctx") // GROUP
    ctx = lax.axis_index("ctx")
    plane = ctx // GROUP
    pos = ctx % GROUP
    rows = hidden.shape[0]
    w_rows = w_query.shape[0]
    group_cols = w_query.shape[1] // GROUP
    widths = (group_cols // 2, group_cols - group_cols // 2)

    count = lax.dynamic_index_in_dim(counts, ctx // 2, 0, keepdims=False)
    order = lax.dynamic_index_in_dim(place, ctx // 2, 0, keepdims=False)
    scal = jnp.stack([plane, pos, count, lax.axis_index("tp")]).astype(jnp.int32)
    spots = pos ^ jnp.arange(GROUP, dtype=jnp.int32)
    spot_counts = counts[plane * 2 + spots // 2]
    token_position = (
        spot_counts[:, None] * BLOCK_TOKENS
        + (spots % 2)[:, None] * rows
        + jnp.arange(rows, dtype=jnp.int32)[None, :]
    )
    cosine, sine = rope_tables(token_position.reshape(GROUP * rows))
    cache_mine = jnp.concatenate(
        [
            jnp.transpose(cache.reshape(-1, BLOCK_TOKENS, HEAD_SIZE), (1, 0, 2)).reshape(
                BLOCK_TOKENS, cache.shape[0]
            )
            for cache in (earlier_keys, earlier_values)
        ],
        axis=1,
    )
    across = GROUP * (planes // 2)
    few = rows // 4

    own, *pieces = pick_columns(w_query, key_weight, value_weight)
    own_far = swap(own, across)
    got = [swap(piece, r) for r, piece in enumerate(pieces, 1)]
    own_near = near(own, planes)
    first, second = split_columns(got, widths)
    hidden, first, second, own_far, cosine, sine, scal, order, cache_mine = gate(
        (hidden, first, second, own_far, cosine, sine, scal, order, cache_mine),
        (*got, *own_near),
    )

    x_1, x_2 = swap(hidden, 1), swap(hidden, 2)
    first_far = swap(first, across)
    first_near = near(first, planes)
    own_w = own_near + near(own_far, planes)
    x_1, x_2, second, first_far = gate(
        (x_1, x_2, second, first_far), (*first_near, *own_w[planes // 2 + 1 :])
    )

    message = swap(jnp.concatenate([x_2[:few], cache_mine]), 1)
    x_3 = jnp.concatenate([message[:few], swap(x_1[few:], 2)])
    x_near = jnp.concatenate([hidden, x_1, x_2])
    core_near = swap_core(x_near)
    second_far = swap(second, across)
    rest_first = first_near + near(first_far, planes)
    parts = project_kv(scal, (x_near, core_near), own_w, group_cols, rows)
    x_3, second, second_far, *parts = gate(
        (x_3, second, second_far, *parts), rest_first[planes // 2 + 1 :]
    )

    xs = [x_near, x_3, core_near, swap_core(x_3)]
    rest_second = near(second, planes) + near(second_far, planes)

    parts += project_kv(scal, (x_3, xs[3]), own_w, group_cols, rows)
    parts = [parts[0]] + [swap(parts[r], r) for r in range(1, GROUP)]
    keys_mine, values_mine, new_mine = finish_kv(parts, cosine, sine, key_norm_gain[None, :])
    caches = (earlier_keys, earlier_values, message)
    news = (new_mine, swap(new_mine, 1))
    gain = q_gain[None, :]

    def queries(scal, rest_w, first, width):
        q = project(scal, xs, own_w, rest_w, cosine, sine, gain, first, width)
        return [q[0]] + [swap(q[r], r) for r in range(1, GROUP)]

    out_cols = w_query.shape[1]
    q_first = queries(
        scal, rest_first, 0, widths[0]
    )
    q_second = queries(after(scal, q_first[0], new_mine), rest_second, widths[0], widths[1])
    tokens = 2 * rows + place.shape[1] * BLOCK_TOKENS
    attended, all_keys, all_values = attend(
        after(scal, q_second[0]), order, q_first, (*caches, *news), 0, widths[0], out_cols, tokens
    )
    (attended,) = attend(
        scal,
        order,
        q_second,
        (all_keys, all_values, attended),
        widths[0],
        widths[1],
        out_cols,
        tokens,
    )
    return (attended, keys_mine, values_mine)


def solution(mesh):
    placed = (
        P("ctx", "tp"),
        P("ctx", "tp"),
        P("ctx", "tp"),
        P("ctx", "tp"),
        P(),
        P(),
        P("ctx", "tp"),
        P("ctx", "tp"),
        P(),
        P(),
    )
    return jax.shard_map(
        on_device,
        mesh=mesh,
        in_specs=placed,
        out_specs=(P("ctx", "tp"), P("ctx", "tp"), P("ctx", "tp")),
        check_vma=False,
    )
```

```python
import functools
import math

import jax
import jax.numpy as jnp
from jax import lax
from jax.experimental import pallas as pl
from jax.experimental.pallas import tpu as pltpu
from jax.sharding import PartitionSpec as P

HEAD_SIZE = 128
BLOCK_TOKENS = 128
GROUP = 4
KEY_CHUNK = 512
ONES = 16
VMEM_LIMIT = 16 * 1024 * 1024


def swap(value, mask):
    pairs = [(source, source ^ mask) for source in range(lax.axis_size("ctx"))]
    return lax.ppermute(value, "ctx", pairs)


def swap_core(value):
    return lax.ppermute(value, "tp", [(0, 1), (1, 0)])


def after(value, *others):
    return lax.optimization_barrier((value, *others))[0]


def near(source, planes):
    pieces = [source]
    bit = 1
    while bit < planes // 2:
        pieces = pieces + [swap(piece, GROUP * bit) for piece in pieces]
        bit *= 2
    return pieces


def gate(values, done):
    return lax.optimization_barrier((tuple(values), tuple(done)))[0]


def rope_tables(token_position):
    half = HEAD_SIZE // 2
    freq = jnp.exp(jnp.arange(half, dtype=jnp.float32) * (-2.0 / HEAD_SIZE) * math.log(1000000.0))
    angle = token_position.astype(jnp.float32)[..., None] * freq
    cosine, sine = jnp.cos(angle), jnp.sin(angle)
    return (
        jnp.concatenate([cosine, cosine], axis=-1),
        jnp.concatenate([-sine, sine], axis=-1),
    )


def half_slot(scal, planes, apart):
    there = scal[0] ^ apart
    other = (there // (planes // 2)) ^ scal[3]
    return other * (planes // 2) + there % (planes // 2)


def pick_columns_kernel(w_ref, key_ref, value_ref, own, *refs):
    *others, sems = refs
    pos = lax.axis_index("ctx") % GROUP
    cols = others[0].shape[1]

    def columns_for(r):
        return w_ref.at[:, pl.ds(pl.multiple_of((pos ^ r) * cols, cols), cols)]

    pairs = [
        (columns_for(0), own.at[:, pl.ds(0, cols)]),
        (key_ref, own.at[:, pl.ds(cols, HEAD_SIZE)]),
        (value_ref, own.at[:, pl.ds(cols + HEAD_SIZE, HEAD_SIZE)]),
    ]
    pairs += [(columns_for(1 + index), out) for index, out in enumerate(others)]
    copies = []
    for index, (src, dst) in enumerate(pairs):
        copy = pltpu.make_async_copy(src, dst, sems.at[index])
        copy.start()
        copies.append(copy)
    for copy in copies:
        copy.wait()


def pick_columns(w_query, key_weight, value_weight):
    rows = w_query.shape[0]
    cols = w_query.shape[1] // GROUP
    anywhere = pl.BlockSpec(memory_space=pl.ANY)
    widths = [cols + 2 * HEAD_SIZE] + [cols] * (GROUP - 1)
    return pl.pallas_call(
        pick_columns_kernel,
        out_shape=[jax.ShapeDtypeStruct((rows, width), jnp.bfloat16) for width in widths],
        in_specs=[anywhere] * 3,
        out_specs=[anywhere] * GROUP,
        scratch_shapes=[pltpu.SemaphoreType.DMA((GROUP + 2,))],
        compiler_params=pltpu.CompilerParams(vmem_limit_bytes=VMEM_LIMIT // 16),
    )(w_query, key_weight, value_weight)


def split_columns_kernel(widths, *refs):
    *got, first, second, sems = refs
    copies = []
    for index, piece in enumerate(got):
        begin = 0
        for part, out in enumerate((first, second)):
            cols = pl.ds(begin, widths[part])
            copy = pltpu.make_async_copy(
                piece.at[:, cols],
                out.at[:, pl.ds(index * widths[part], widths[part])],
                sems.at[index, part],
            )
            copy.start()
            copies.append(copy)
            begin += widths[part]
    for copy in copies:
        copy.wait()


def split_columns(got, widths):
    rows = got[0].shape[0]
    anywhere = pl.BlockSpec(memory_space=pl.ANY)
    return pl.pallas_call(
        functools.partial(split_columns_kernel, widths),
        out_shape=[
            jax.ShapeDtypeStruct((rows, len(got) * width), jnp.bfloat16) for width in widths
        ],
        in_specs=[anywhere] * len(got),
        out_specs=[anywhere] * 2,
        scratch_shapes=[pltpu.SemaphoreType.DMA((len(got), 2))],
        compiler_params=pltpu.CompilerParams(vmem_limit_bytes=VMEM_LIMIT // 16),
    )(*got)


def project_kernel(planes, first, width, *refs):
    scal, refs = refs[0], refs[1:]
    xs, refs = refs[:4], refs[4:]
    own_w, rest_w, refs = refs[:planes], refs[planes : 2 * planes], refs[2 * planes :]
    cosine, sine, gain, *q_out, w_all, w_sem = refs
    pos = scal[1]
    half_cols = xs[0].shape[1]
    w_rows = own_w[0].shape[0]

    copies = []
    for apart in range(planes):
        base = half_slot(scal, planes, apart) * GROUP
        for r in range(GROUP):
            if r == 0:
                src = own_w[apart].at[:, pl.ds(first, width)]
            else:
                src = rest_w[apart].at[:, pl.ds((r - 1) * width, width)]
            row = pl.multiple_of((base + (pos ^ r)) * w_rows, w_rows)
            copy = pltpu.make_async_copy(
                src, w_all.at[pl.ds(row, w_rows)], w_sem.at[apart, r]
            )
            copy.start()
            copies.append(copy)
    for copy in copies:
        copy.wait()

    rows = q_out[0].shape[0]
    for block in range(GROUP):
        part, begin = (0, block * rows) if block < GROUP - 1 else (1, 0)
        result = jnp.dot(
            xs[part][pl.ds(begin, rows), :],
            w_all[pl.ds(0, half_cols), :],
            preferred_element_type=jnp.float32,
        ) + jnp.dot(
            xs[2 + part][pl.ds(begin, rows), :],
            w_all[pl.ds(half_cols, half_cols), :],
            preferred_element_type=jnp.float32,
        )
        tokens = pl.ds(block * rows, rows)
        for head in range(width // HEAD_SIZE):
            values = result[:, head * HEAD_SIZE : (head + 1) * HEAD_SIZE]
            mean = jnp.mean(values * values, axis=-1, keepdims=True)
            scaled = values * lax.rsqrt(mean + 1e-06) * gain[...]
            turned = (
                scaled * cosine[tokens, :]
                + pltpu.roll(scaled, HEAD_SIZE // 2, 1) * sine[tokens, :]
            )
            q_out[block][:, pl.ds(head * HEAD_SIZE, HEAD_SIZE)] = turned.astype(jnp.bfloat16)


def project(scal, xs, own_w, rest_w, cosine, sine, gain, first, width):
    planes = len(own_w)
    rows, half_cols = xs[1].shape
    depth = 2 * half_cols
    anywhere = pl.BlockSpec(memory_space=pl.ANY)
    vmem = pl.BlockSpec(memory_space=pltpu.VMEM)
    return pl.pallas_call(
        functools.partial(project_kernel, planes, first, width),
        out_shape=[jax.ShapeDtypeStruct((rows, width), jnp.bfloat16)] * GROUP,
        in_specs=[pl.BlockSpec(memory_space=pltpu.SMEM)]
        + [vmem] * 4
        + [anywhere] * (2 * planes)
        + [vmem] * 3,
        out_specs=[vmem] * GROUP,
        scratch_shapes=[
            pltpu.VMEM((depth, width), jnp.bfloat16),
            pltpu.SemaphoreType.DMA((planes, GROUP)),
        ],
        compiler_params=pltpu.CompilerParams(vmem_limit_bytes=VMEM_LIMIT),
        cost_estimate=pl.CostEstimate(
            flops=2 * GROUP * rows * depth * width,
            bytes_accessed=2 * depth * (GROUP * rows + width),
            transcendentals=0,
        ),
    )(scal, *xs, *own_w, *rest_w, cosine, sine, gain)


def project_kv_kernel(planes, skip, *refs):
    scal, refs = refs[0], refs[1:]
    xs, own_w, refs = refs[:2], refs[2 : 2 + planes], refs[2 + planes :]
    *kv_out, x_all, w_all, x_sem, w_sem = refs
    pos = scal[1]
    w_rows = own_w[0].shape[0]
    _, depth, width = w_all.shape
    compact = depth == w_rows
    offset = pos * w_rows if compact else 0

    copies = []
    for apart in range(planes):
        slot = half_slot(scal, planes, apart)
        row = 0
        if not compact:
            w_all[slot] = jnp.zeros((depth, width), jnp.bfloat16)
            row = pl.multiple_of(pos * w_rows, w_rows)
        copy = pltpu.make_async_copy(
            own_w[apart].at[:, pl.ds(skip, width)],
            w_all.at[slot, pl.ds(row, w_rows)],
            w_sem.at[apart],
        )
        copy.start()
        copies.append(copy)
    for slot in range(planes):
        half, within = slot // (planes // 2), slot % (planes // 2)
        column = pl.multiple_of(within * GROUP * w_rows + offset, HEAD_SIZE)
        copy = pltpu.make_async_copy(
            xs[half].at[:, pl.ds(column, depth)], x_all.at[slot], x_sem.at[slot]
        )
        copy.start()
        copies.append(copy)
    for copy in copies:
        copy.wait()
    result = None
    for slot in range(planes):
        term = jnp.dot(x_all[slot], w_all[slot], preferred_element_type=jnp.float32)
        result = term if result is None else result + term
    rows = kv_out[0].shape[0]
    for block, out in enumerate(kv_out):
        out[...] = result[block * rows : (block + 1) * rows]


def project_kv(scal, xs, own_w, skip, rows):
    planes = len(own_w)
    tokens = xs[0].shape[0]
    w_rows = own_w[0].shape[0]
    width = own_w[0].shape[1] - skip
    depth = w_rows if w_rows % HEAD_SIZE == 0 else GROUP * w_rows
    anywhere = pl.BlockSpec(memory_space=pl.ANY)
    return pl.pallas_call(
        functools.partial(project_kv_kernel, planes, skip),
        out_shape=[jax.ShapeDtypeStruct((rows, width), jnp.float32)] * (tokens // rows),
        in_specs=[pl.BlockSpec(memory_space=pltpu.SMEM)] + [anywhere] * (2 + planes),
        out_specs=[pl.BlockSpec(memory_space=pltpu.VMEM)] * (tokens // rows),
        scratch_shapes=[
            pltpu.VMEM((planes, tokens, depth), jnp.bfloat16),
            pltpu.VMEM((planes, depth, width), jnp.bfloat16),
            pltpu.SemaphoreType.DMA((planes,)),
            pltpu.SemaphoreType.DMA((planes,)),
        ],
        compiler_params=pltpu.CompilerParams(vmem_limit_bytes=VMEM_LIMIT),
        cost_estimate=pl.CostEstimate(
            flops=2 * tokens * depth * planes * width,
            bytes_accessed=2 * depth * planes * (tokens + width),
            transcendentals=0,
        ),
    )(scal, *xs, *own_w)


def finish_kv_kernel(mine, *refs):
    *others, cosine, sine, gain, keys_out, values_out, both_out = refs
    summed = mine[...]
    for other in others:
        summed = summed + other[...]
    keys = summed[:, :HEAD_SIZE]
    mean = jnp.mean(keys * keys, axis=-1, keepdims=True)
    scaled = keys * lax.rsqrt(mean + 1e-06) * gain[...]
    own = pl.ds(0, keys.shape[0])
    turned = scaled * cosine[own, :] + pltpu.roll(scaled, HEAD_SIZE // 2, 1) * sine[own, :]
    keys_out[...] = turned.astype(jnp.bfloat16)
    values_out[...] = summed[:, HEAD_SIZE:].astype(jnp.bfloat16)
    both_out[0] = keys_out[...]
    turned_values = summed[:, HEAD_SIZE:].T.astype(jnp.bfloat16)
    for begin in range(0, keys.shape[0], HEAD_SIZE):
        both_out[1, pl.ds(begin, HEAD_SIZE), :] = turned_values[:, begin : begin + HEAD_SIZE]


def finish_kv(parts, cosine, sine, gain):
    rows = parts[0].shape[0]
    one = jax.ShapeDtypeStruct((rows, HEAD_SIZE), jnp.bfloat16)
    vmem = pl.BlockSpec(memory_space=pltpu.VMEM)
    return pl.pallas_call(
        finish_kv_kernel,
        out_shape=[one, one, jax.ShapeDtypeStruct((2, rows, HEAD_SIZE), jnp.bfloat16)],
        in_specs=[vmem] * (len(parts) + 3),
        out_specs=[vmem] * 3,
        compiler_params=pltpu.CompilerParams(vmem_limit_bytes=VMEM_LIMIT // 4),
    )(*parts, cosine, sine, gain)


def attend_kernel(first, width, rows, aliased, *refs):
    scal, order = refs[:2]
    qs = refs[2:6]
    if aliased:
        k_all, vt_all, _, out, *refs = refs[6:]
    else:
        keys_mine, values_mine, theirs, new_mine, new_theirs, out, k_all, vt_all, *refs = refs[6:]
        kv_sem, new_sem, *refs = refs
    q_all, o_all, tops, sums, out_sem = refs
    pos, count = scal[1], scal[2]
    side = pos % 2
    heads = width // HEAD_SIZE
    slots = order.shape[0]
    half_slots = slots // 2
    scale = HEAD_SIZE ** (-0.5) * math.log2(math.e)
    units = GROUP * heads
    lanes = rows

    lead = rows + side * rows

    def new_copies(new, row, index):
        copies = [
            pltpu.make_async_copy(
                new.at[0], k_all.at[pl.ds(row, rows)], new_sem.at[index, 0]
            )
        ]
        for begin in range(0, rows, HEAD_SIZE):
            copies.append(
                pltpu.make_async_copy(
                    new.at[1, pl.ds(begin, HEAD_SIZE)],
                    vt_all.at[pl.ds(0, HEAD_SIZE), pl.ds(row + begin, HEAD_SIZE)],
                    new_sem.at[index, 1 + begin // HEAD_SIZE],
                )
            )
        return copies

    def block_copies(j):
        slot = order[j]
        within = pl.multiple_of((slot % half_slots) * BLOCK_TOKENS, BLOCK_TOKENS)
        dst_row = pl.multiple_of(lead + j * BLOCK_TOKENS, BLOCK_TOKENS)
        near = (slot // half_slots) == side

        def pair(k_src, v_src):
            rows_at = pl.ds(dst_row, BLOCK_TOKENS)
            return (
                pltpu.make_async_copy(k_src, k_all.at[rows_at], kv_sem.at[0, j]),
                pltpu.make_async_copy(
                    v_src, vt_all.at[pl.ds(0, HEAD_SIZE), rows_at], kv_sem.at[1, j]
                ),
            )

        block = pl.ds(within, BLOCK_TOKENS)
        apart = half_slots * BLOCK_TOKENS
        beyond = pl.ds(pl.multiple_of(apart + within, BLOCK_TOKENS), BLOCK_TOKENS)
        there = pl.ds(theirs.shape[0] - BLOCK_TOKENS, BLOCK_TOKENS)
        return (
            near,
            pair(keys_mine.at[block], values_mine.at[:, block]),
            pair(theirs.at[there, block], theirs.at[there, beyond]),
        )

    def start_block(j, carry):
        near, mine, theirs = block_copies(j)

        @pl.when(near)
        def _():
            for copy in mine:
                copy.start()

        @pl.when(jnp.logical_not(near))
        def _():
            for copy in theirs:
                copy.start()

        return carry

    def wait_block(j, carry):
        _, mine, _ = block_copies(j)
        for copy in mine:
            copy.wait()
        return carry

    per_chunk = KEY_CHUNK // BLOCK_TOKENS
    blocks = count + side * (rows // BLOCK_TOKENS)
    full = blocks // per_chunk

    if not aliased:
        for copy in new_copies(new_mine, 0, 0):
            copy.start()

        @pl.when(side == 1)
        def _():
            for copy in new_copies(new_theirs, rows, 1):
                copy.start()

        lax.fori_loop(0, count, start_block, 0)
        vt_all[pl.ds(HEAD_SIZE, ONES), :] = jnp.ones((ONES, vt_all.shape[1]), jnp.bfloat16)

    for r in range(GROUP):
        for head in range(heads):
            q_all[r * heads + head] = qs[r][:, pl.ds(head * HEAD_SIZE, HEAD_SIZE)]

    def absorb(row, size, how, allowed=None):
        keys = k_all[pl.ds(row, size), :]
        values = vt_all[:, pl.ds(row, size)]

        def score(unit):
            return lax.dot_general(
                keys, q_all[unit], (((1,), (1,)), ((), ())), preferred_element_type=jnp.float32
            )

        ahead = score(0)
        for unit in range(units):
            s = ahead
            if unit + 1 < units:
                ahead = score(unit + 1)
            if allowed is not None:
                s = jnp.where(allowed, s, -1e30)
            top = before = None if how == "first" else tops[unit]
            if how != "same":
                top = jnp.max(jnp.max(s.reshape(size // 8, 8, lanes), axis=0), axis=0, keepdims=True)
                if how == "rising":
                    top = jnp.maximum(before, top)
                tops[unit] = top
            weight = jnp.exp2((s - top) * scale)
            mixed = jnp.dot(
                values, weight.astype(jnp.bfloat16), preferred_element_type=jnp.float32
            )
            if how == "first":
                sums[unit] = mixed
            elif how == "same":
                sums[unit] += mixed
            else:
                shrink = jnp.exp2((before - top) * scale)
                sums[unit] = sums[unit] * shrink + mixed

    def absorb_own():
        key = lax.broadcasted_iota(jnp.int32, (rows, lanes), 0)
        token = lax.broadcasted_iota(jnp.int32, (rows, lanes), 1)
        absorb(0, rows, "first", key <= token)

    def absorb_rest(how):
        def step(chunk, carry):
            row = pl.multiple_of(rows + chunk * KEY_CHUNK, BLOCK_TOKENS)
            absorb(row, KEY_CHUNK, how)
            return carry

        lax.fori_loop(0, full, step, 0)
        part = per_chunk // 2
        while part:
            size = part * BLOCK_TOKENS

            @pl.when((blocks // part) % 2 == 1)
            def _(part=part, size=size):
                row = pl.multiple_of(rows + (blocks // (2 * part)) * 2 * size, BLOCK_TOKENS)
                absorb(row, size, how)

            part //= 2

    if not aliased:
        for copy in new_copies(new_mine, 0, 0):
            copy.wait()
    absorb_own()
    if not aliased:

        @pl.when(side == 1)
        def _():
            for copy in new_copies(new_theirs, rows, 1):
                copy.wait()

        lax.fori_loop(0, count, wait_block, 0)

    absorb_rest("same")
    fits = jnp.max(sums[:, pl.ds(HEAD_SIZE, 8), :]) < 2.0**100

    @pl.when(jnp.logical_not(fits))
    def _():
        absorb_own()
        absorb_rest("rising")

    group_cols = out.shape[1] // GROUP
    copies = []
    for r in range(GROUP):
        for head in range(heads):
            unit = r * heads + head
            total = sums[unit, pl.ds(HEAD_SIZE, 1), :]
            result = (sums[unit, pl.ds(0, HEAD_SIZE), :] / total).T.astype(jnp.bfloat16)
            o_all[r, :, pl.ds(head * HEAD_SIZE, HEAD_SIZE)] = result
        column = pl.multiple_of((pos ^ r) * group_cols + first, HEAD_SIZE)
        copy = pltpu.make_async_copy(
            o_all.at[r], out.at[:, pl.ds(column, width)], out_sem.at[r]
        )
        copy.start()
        copies.append(copy)
    for copy in copies:
        copy.wait()


def attend(scal, order, qs, sources, first, width, out_cols, tokens):
    rows = qs[0].shape[0]
    slots = order.shape[0]
    heads = width // HEAD_SIZE
    units = GROUP * heads
    aliased = len(sources) == 3
    anywhere = pl.BlockSpec(memory_space=pl.ANY)
    vmem = pl.BlockSpec(memory_space=pltpu.VMEM)
    smem = pl.BlockSpec(memory_space=pltpu.SMEM)
    in_specs = [smem] * 2 + [vmem] * 4
    out_shape = [jax.ShapeDtypeStruct((rows, out_cols), jnp.bfloat16)]
    scratch = []
    if aliased:
        in_specs += [vmem, vmem, anywhere]
    else:
        in_specs += [anywhere] * len(sources)
        out_shape += [
            jax.ShapeDtypeStruct((tokens, HEAD_SIZE), jnp.bfloat16),
            jax.ShapeDtypeStruct((HEAD_SIZE + ONES, tokens), jnp.bfloat16),
        ]
        scratch += [
            pltpu.SemaphoreType.DMA((2, slots)),
            pltpu.SemaphoreType.DMA((2, 1 + rows // HEAD_SIZE)),
        ]
    scratch += [
        pltpu.VMEM((units, rows, HEAD_SIZE), jnp.bfloat16),
        pltpu.VMEM((GROUP, rows, width), jnp.bfloat16),
        pltpu.VMEM((units, 1, rows), jnp.float32),
        pltpu.VMEM((units, HEAD_SIZE + ONES, rows), jnp.float32),
        pltpu.SemaphoreType.DMA((GROUP,)),
    ]
    return pl.pallas_call(
        functools.partial(attend_kernel, first, width, rows, aliased),
        out_shape=out_shape,
        in_specs=in_specs,
        out_specs=[anywhere] + [vmem] * (len(out_shape) - 1),
        input_output_aliases={8: 0} if aliased else {},
        scratch_shapes=scratch,
        compiler_params=pltpu.CompilerParams(vmem_limit_bytes=VMEM_LIMIT),
        cost_estimate=pl.CostEstimate(
            flops=4 * units * rows * tokens * HEAD_SIZE,
            bytes_accessed=4 * tokens * HEAD_SIZE,
            transcendentals=units * rows * tokens,
        ),
    )(scal, order, *qs, *sources)


def on_device(
    hidden,
    w_query,
    key_weight,
    value_weight,
    q_gain,
    key_norm_gain,
    earlier_keys,
    earlier_values,
    counts,
    place,
):
    planes = lax.axis_size("ctx") // GROUP
    ctx = lax.axis_index("ctx")
    plane = ctx // GROUP
    pos = ctx % GROUP
    rows = hidden.shape[0]
    w_rows = w_query.shape[0]
    group_cols = w_query.shape[1] // GROUP
    widths = (group_cols // 2, group_cols - group_cols // 2)

    count = lax.dynamic_index_in_dim(counts, ctx // 2, 0, keepdims=False)
    order = lax.dynamic_index_in_dim(place, ctx // 2, 0, keepdims=False)
    scal = jnp.stack([plane, pos, count, lax.axis_index("tp")]).astype(jnp.int32)
    spots = pos ^ jnp.arange(GROUP, dtype=jnp.int32)
    spot_counts = counts[plane * 2 + spots // 2]
    token_position = (
        spot_counts[:, None] * BLOCK_TOKENS
        + (spots % 2)[:, None] * rows
        + jnp.arange(rows, dtype=jnp.int32)[None, :]
    )
    cosine, sine = rope_tables(token_position.reshape(GROUP * rows))
    key_blocks = earlier_keys.reshape(-1, BLOCK_TOKENS, HEAD_SIZE)
    key_blocks = jnp.transpose(key_blocks, (1, 0, 2)).reshape(BLOCK_TOKENS, -1)
    values_turned = earlier_values.T
    cache_mine = jnp.concatenate([key_blocks, values_turned], axis=1)
    across = GROUP * (planes // 2)
    few = rows // 4

    own, *pieces = pick_columns(w_query, key_weight, value_weight)
    own_far = swap(own, across)
    got = [swap(piece, r) for r, piece in enumerate(pieces, 1)]
    own_near = near(own, planes)
    first, second = split_columns(got, widths)
    hidden, first, second, own_far, cosine, sine, scal, order, cache_mine, values_turned = gate(
        (hidden, first, second, own_far, cosine, sine, scal, order, cache_mine, values_turned),
        (*got, *own_near),
    )

    x_1, x_2 = swap(hidden, 1), swap(hidden, 2)
    first_far = swap(first, across)
    first_near = near(first, planes)
    own_w = own_near + near(own_far, planes)
    x_1, x_2, second, first_far = gate(
        (x_1, x_2, second, first_far), (*first_near, *own_w[planes // 2 + 1 :])
    )

    message = swap(jnp.concatenate([x_2[:few], cache_mine]), 1)
    x_3 = jnp.concatenate([message[:few], swap(x_1[few:], 2)])
    x_near = jnp.concatenate([hidden, x_1, x_2])
    core_near = swap_core(x_near)
    second_far = swap(second, across)
    rest_first = first_near + near(first_far, planes)
    parts = project_kv(scal, (x_near, core_near), own_w, group_cols, rows)
    x_3, second, second_far, *parts = gate(
        (x_3, second, second_far, *parts), rest_first[planes // 2 + 1 :]
    )

    xs = [x_near, x_3, core_near, swap_core(x_3)]
    rest_second = near(second, planes) + near(second_far, planes)

    parts += project_kv(scal, (x_3, xs[3]), own_w, group_cols, rows)
    parts = [parts[0]] + [swap(parts[r], r) for r in range(1, GROUP)]
    keys_mine, values_mine, new_mine = finish_kv(parts, cosine, sine, key_norm_gain[None, :])
    caches = (earlier_keys, values_turned, message)
    news = (new_mine, swap(new_mine, 1))
    gain = q_gain[None, :]

    def queries(scal, rest_w, first, width):
        q = project(scal, xs, own_w, rest_w, cosine, sine, gain, first, width)
        return [q[0]] + [swap(q[r], r) for r in range(1, GROUP)]

    out_cols = w_query.shape[1]
    q_first = queries(
        scal, rest_first, 0, widths[0]
    )
    q_second = queries(after(scal, q_first[0], new_mine), rest_second, widths[0], widths[1])
    tokens = 2 * rows + place.shape[1] * BLOCK_TOKENS
    attended, all_keys, all_values = attend(
        after(scal, q_second[0]), order, q_first, (*caches, *news), 0, widths[0], out_cols, tokens
    )
    (attended,) = attend(
        scal,
        order,
        q_second,
        (all_keys, all_values, attended),
        widths[0],
        widths[1],
        out_cols,
        tokens,
    )
    return (attended, keys_mine, values_mine)


def solution(mesh):
    placed = (
        P("ctx", "tp"),
        P("ctx", "tp"),
        P("ctx", "tp"),
        P("ctx", "tp"),
        P(),
        P(),
        P("ctx", "tp"),
        P("ctx", "tp"),
        P(),
        P(),
    )
    return jax.shard_map(
        on_device,
        mesh=mesh,
        in_specs=placed,
        out_specs=(P("ctx", "tp"), P("ctx", "tp"), P("ctx", "tp")),
        check_vma=False,
    )
```

```python
import functools
import math

import jax
import jax.numpy as jnp
from jax import lax
from jax.experimental import pallas as pl
from jax.experimental.pallas import tpu as pltpu
from jax.sharding import PartitionSpec as P

HEAD_SIZE = 128
BLOCK_TOKENS = 128
GROUP = 4
KEY_CHUNK = 512
ONES = 16
UNROLL = 4
VMEM_LIMIT = 16 * 1024 * 1024


def swap(value, mask):
    pairs = [(source, source ^ mask) for source in range(lax.axis_size("ctx"))]
    return lax.ppermute(value, "ctx", pairs)


def swap_core(value):
    return lax.ppermute(value, "tp", [(0, 1), (1, 0)])


def after(value, *others):
    return lax.optimization_barrier((value, *others))[0]


def near(source, planes):
    pieces = [source]
    bit = 1
    while bit < planes // 2:
        pieces = pieces + [swap(piece, GROUP * bit) for piece in pieces]
        bit *= 2
    return pieces


def gate(values, done):
    return lax.optimization_barrier((tuple(values), tuple(done)))[0]


def rope_tables(token_position):
    half = HEAD_SIZE // 2
    freq = jnp.exp(jnp.arange(half, dtype=jnp.float32) * (-2.0 / HEAD_SIZE) * math.log(1000000.0))
    angle = token_position.astype(jnp.float32)[..., None] * freq
    cosine, sine = jnp.cos(angle), jnp.sin(angle)
    return (
        jnp.concatenate([cosine, cosine], axis=-1),
        jnp.concatenate([-sine, sine], axis=-1),
    )


def half_slot(scal, planes, apart):
    there = scal[0] ^ apart
    other = (there // (planes // 2)) ^ scal[3]
    return other * (planes // 2) + there % (planes // 2)


def pick_columns_kernel(w_ref, key_ref, value_ref, own, *refs):
    *others, sems = refs
    pos = lax.axis_index("ctx") % GROUP
    cols = others[0].shape[1]

    def columns_for(r):
        return w_ref.at[:, pl.ds(pl.multiple_of((pos ^ r) * cols, cols), cols)]

    pairs = [
        (columns_for(0), own.at[:, pl.ds(0, cols)]),
        (key_ref, own.at[:, pl.ds(cols, HEAD_SIZE)]),
        (value_ref, own.at[:, pl.ds(cols + HEAD_SIZE, HEAD_SIZE)]),
    ]
    pairs += [(columns_for(1 + index), out) for index, out in enumerate(others)]
    copies = []
    for index, (src, dst) in enumerate(pairs):
        copy = pltpu.make_async_copy(src, dst, sems.at[index])
        copy.start()
        copies.append(copy)
    for copy in copies:
        copy.wait()


def pick_columns(w_query, key_weight, value_weight):
    rows = w_query.shape[0]
    cols = w_query.shape[1] // GROUP
    anywhere = pl.BlockSpec(memory_space=pl.ANY)
    widths = [cols + 2 * HEAD_SIZE] + [cols] * (GROUP - 1)
    return pl.pallas_call(
        pick_columns_kernel,
        out_shape=[jax.ShapeDtypeStruct((rows, width), jnp.bfloat16) for width in widths],
        in_specs=[anywhere] * 3,
        out_specs=[pl.BlockSpec(memory_space=pltpu.VMEM)] * GROUP,
        scratch_shapes=[pltpu.SemaphoreType.DMA((GROUP + 2,))],
        compiler_params=pltpu.CompilerParams(vmem_limit_bytes=60 * 1024 * 1024),
    )(w_query, key_weight, value_weight)


def split_columns_kernel(widths, *refs):
    *got, first, second, sems = refs
    copies = []
    for index, piece in enumerate(got):
        begin = 0
        for part, out in enumerate((first, second)):
            cols = pl.ds(begin, widths[part])
            copy = pltpu.make_async_copy(
                piece.at[:, cols],
                out.at[:, pl.ds(index * widths[part], widths[part])],
                sems.at[index, part],
            )
            copy.start()
            copies.append(copy)
            begin += widths[part]
    for copy in copies:
        copy.wait()


def split_columns(got, widths):
    rows = got[0].shape[0]
    anywhere = pl.BlockSpec(memory_space=pl.ANY)
    return pl.pallas_call(
        functools.partial(split_columns_kernel, widths),
        out_shape=[
            jax.ShapeDtypeStruct((rows, len(got) * width), jnp.bfloat16) for width in widths
        ],
        in_specs=[anywhere] * len(got),
        out_specs=[anywhere] * 2,
        scratch_shapes=[pltpu.SemaphoreType.DMA((len(got), 2))],
        compiler_params=pltpu.CompilerParams(vmem_limit_bytes=VMEM_LIMIT // 16),
    )(*got)


def project_kernel(planes, first, width, *refs):
    scal, refs = refs[0], refs[1:]
    xs, refs = refs[:4], refs[4:]
    own_w, rest_w, refs = refs[:planes], refs[planes : 2 * planes], refs[2 * planes :]
    cosine, sine, gain, *q_out, w_all, w_sem = refs
    pos = scal[1]
    half_cols = xs[0].shape[1]
    w_rows = own_w[0].shape[0]

    copies = []
    for apart in range(planes):
        base = half_slot(scal, planes, apart) * GROUP
        for r in range(GROUP):
            if r == 0:
                src = own_w[apart].at[:, pl.ds(first, width)]
            else:
                src = rest_w[apart].at[:, pl.ds((r - 1) * width, width)]
            row = pl.multiple_of((base + (pos ^ r)) * w_rows, w_rows)
            copy = pltpu.make_async_copy(
                src, w_all.at[pl.ds(row, w_rows)], w_sem.at[apart, r]
            )
            copy.start()
            copies.append(copy)
    for copy in copies:
        copy.wait()

    rows = q_out[0].shape[0]
    for block in range(GROUP):
        part, begin = (0, block * rows) if block < GROUP - 1 else (1, 0)
        result = jnp.dot(
            xs[part][pl.ds(begin, rows), :],
            w_all[pl.ds(0, half_cols), :],
            preferred_element_type=jnp.float32,
        ) + jnp.dot(
            xs[2 + part][pl.ds(begin, rows), :],
            w_all[pl.ds(half_cols, half_cols), :],
            preferred_element_type=jnp.float32,
        )
        tokens = pl.ds(block * rows, rows)
        for head in range(width // HEAD_SIZE):
            values = result[:, head * HEAD_SIZE : (head + 1) * HEAD_SIZE]
            mean = jnp.mean(values * values, axis=-1, keepdims=True)
            scaled = values * lax.rsqrt(mean + 1e-06) * gain[...]
            turned = (
                scaled * cosine[tokens, :]
                + pltpu.roll(scaled, HEAD_SIZE // 2, 1) * sine[tokens, :]
            )
            q_out[block][:, pl.ds(head * HEAD_SIZE, HEAD_SIZE)] = turned.astype(jnp.bfloat16)


def project(scal, xs, own_w, rest_w, cosine, sine, gain, first, width):
    planes = len(own_w)
    rows, half_cols = xs[1].shape
    depth = 2 * half_cols
    anywhere = pl.BlockSpec(memory_space=pl.ANY)
    vmem = pl.BlockSpec(memory_space=pltpu.VMEM)
    return pl.pallas_call(
        functools.partial(project_kernel, planes, first, width),
        out_shape=[jax.ShapeDtypeStruct((rows, width), jnp.bfloat16)] * GROUP,
        in_specs=[pl.BlockSpec(memory_space=pltpu.SMEM)]
        + [vmem] * 4
        + [anywhere] * (2 * planes)
        + [vmem] * 3,
        out_specs=[vmem] * GROUP,
        scratch_shapes=[
            pltpu.VMEM((depth, width), jnp.bfloat16),
            pltpu.SemaphoreType.DMA((planes, GROUP)),
        ],
        compiler_params=pltpu.CompilerParams(vmem_limit_bytes=VMEM_LIMIT),
        cost_estimate=pl.CostEstimate(
            flops=2 * GROUP * rows * depth * width,
            bytes_accessed=2 * depth * (GROUP * rows + width),
            transcendentals=0,
        ),
    )(scal, *xs, *own_w, *rest_w, cosine, sine, gain)


def project_kv_kernel(planes, skip, *refs):
    scal, refs = refs[0], refs[1:]
    xs, own_w, refs = refs[:2], refs[2 : 2 + planes], refs[2 + planes :]
    *kv_out, x_all, w_all, x_sem, w_sem = refs
    pos = scal[1]
    w_rows = own_w[0].shape[0]
    _, depth, width = w_all.shape
    compact = depth == w_rows
    offset = pos * w_rows if compact else 0

    copies = []
    for apart in range(planes):
        slot = half_slot(scal, planes, apart)
        row = 0
        if not compact:
            w_all[slot] = jnp.zeros((depth, width), jnp.bfloat16)
            row = pl.multiple_of(pos * w_rows, w_rows)
        copy = pltpu.make_async_copy(
            own_w[apart].at[:, pl.ds(skip, width)],
            w_all.at[slot, pl.ds(row, w_rows)],
            w_sem.at[apart],
        )
        copy.start()
        copies.append(copy)
    for slot in range(planes):
        half, within = slot // (planes // 2), slot % (planes // 2)
        column = pl.multiple_of(within * GROUP * w_rows + offset, HEAD_SIZE)
        copy = pltpu.make_async_copy(
            xs[half].at[:, pl.ds(column, depth)], x_all.at[slot], x_sem.at[slot]
        )
        copy.start()
        copies.append(copy)
    for copy in copies:
        copy.wait()
    result = None
    for slot in range(planes):
        term = jnp.dot(x_all[slot], w_all[slot], preferred_element_type=jnp.float32)
        result = term if result is None else result + term
    rows = kv_out[0].shape[0]
    for block, out in enumerate(kv_out):
        out[...] = result[block * rows : (block + 1) * rows]


def project_kv(scal, xs, own_w, skip, rows):
    planes = len(own_w)
    tokens = xs[0].shape[0]
    w_rows = own_w[0].shape[0]
    width = own_w[0].shape[1] - skip
    depth = w_rows if w_rows % HEAD_SIZE == 0 else GROUP * w_rows
    anywhere = pl.BlockSpec(memory_space=pl.ANY)
    return pl.pallas_call(
        functools.partial(project_kv_kernel, planes, skip),
        out_shape=[jax.ShapeDtypeStruct((rows, width), jnp.float32)] * (tokens // rows),
        in_specs=[pl.BlockSpec(memory_space=pltpu.SMEM)] + [anywhere] * (2 + planes),
        out_specs=[pl.BlockSpec(memory_space=pltpu.VMEM)] * (tokens // rows),
        scratch_shapes=[
            pltpu.VMEM((planes, tokens, depth), jnp.bfloat16),
            pltpu.VMEM((planes, depth, width), jnp.bfloat16),
            pltpu.SemaphoreType.DMA((planes,)),
            pltpu.SemaphoreType.DMA((planes,)),
        ],
        compiler_params=pltpu.CompilerParams(vmem_limit_bytes=VMEM_LIMIT),
        cost_estimate=pl.CostEstimate(
            flops=2 * tokens * depth * planes * width,
            bytes_accessed=2 * depth * planes * (tokens + width),
            transcendentals=0,
        ),
    )(scal, *xs, *own_w)


def finish_kv_kernel(mine, *refs):
    *others, cosine, sine, gain, keys_out, values_out, both_out = refs
    summed = mine[...]
    for other in others:
        summed = summed + other[...]
    keys = summed[:, :HEAD_SIZE]
    mean = jnp.mean(keys * keys, axis=-1, keepdims=True)
    scaled = keys * lax.rsqrt(mean + 1e-06) * gain[...]
    own = pl.ds(0, keys.shape[0])
    turned = scaled * cosine[own, :] + pltpu.roll(scaled, HEAD_SIZE // 2, 1) * sine[own, :]
    keys_out[...] = turned.astype(jnp.bfloat16)
    values_out[...] = summed[:, HEAD_SIZE:].astype(jnp.bfloat16)
    both_out[0] = keys_out[...]
    turned_values = summed[:, HEAD_SIZE:].T.astype(jnp.bfloat16)
    for begin in range(0, keys.shape[0], HEAD_SIZE):
        both_out[1, pl.ds(begin, HEAD_SIZE), :] = turned_values[:, begin : begin + HEAD_SIZE]


def finish_kv(parts, cosine, sine, gain):
    rows = parts[0].shape[0]
    one = jax.ShapeDtypeStruct((rows, HEAD_SIZE), jnp.bfloat16)
    vmem = pl.BlockSpec(memory_space=pltpu.VMEM)
    return pl.pallas_call(
        finish_kv_kernel,
        out_shape=[one, one, jax.ShapeDtypeStruct((2, rows, HEAD_SIZE), jnp.bfloat16)],
        in_specs=[vmem] * (len(parts) + 3),
        out_specs=[vmem] * 3,
        compiler_params=pltpu.CompilerParams(vmem_limit_bytes=VMEM_LIMIT // 4),
    )(*parts, cosine, sine, gain)


def attend_kernel(first, width, rows, aliased, *refs):
    scal, order = refs[:2]
    qs = refs[2:6]
    if aliased:
        k_all, vt_all, _, out, *refs = refs[6:]
    else:
        keys_mine, values_mine, theirs, new_mine, new_theirs, out, k_all, vt_all, *refs = refs[6:]
        kv_sem, new_sem, *refs = refs
    q_all, o_all, tops, sums, out_sem = refs
    pos, count = scal[1], scal[2]
    side = pos % 2
    heads = width // HEAD_SIZE
    slots = order.shape[0]
    half_slots = slots // 2
    scale = HEAD_SIZE ** (-0.5) * math.log2(math.e)
    units = GROUP * heads
    lanes = rows

    lead = rows + side * rows

    def new_copies(new, row, index):
        copies = [
            pltpu.make_async_copy(
                new.at[0], k_all.at[pl.ds(row, rows)], new_sem.at[index, 0]
            )
        ]
        for begin in range(0, rows, HEAD_SIZE):
            copies.append(
                pltpu.make_async_copy(
                    new.at[1, pl.ds(begin, HEAD_SIZE)],
                    vt_all.at[pl.ds(0, HEAD_SIZE), pl.ds(row + begin, HEAD_SIZE)],
                    new_sem.at[index, 1 + begin // HEAD_SIZE],
                )
            )
        return copies

    def block_copies(j):
        slot = order[j]
        within = pl.multiple_of((slot % half_slots) * BLOCK_TOKENS, BLOCK_TOKENS)
        dst_row = pl.multiple_of(lead + j * BLOCK_TOKENS, BLOCK_TOKENS)
        near = (slot // half_slots) == side

        def pair(k_src, v_src):
            rows_at = pl.ds(dst_row, BLOCK_TOKENS)
            return (
                pltpu.make_async_copy(k_src, k_all.at[rows_at], kv_sem.at[0, j]),
                pltpu.make_async_copy(
                    v_src, vt_all.at[pl.ds(0, HEAD_SIZE), rows_at], kv_sem.at[1, j]
                ),
            )

        block = pl.ds(within, BLOCK_TOKENS)
        apart = half_slots * BLOCK_TOKENS
        beyond = pl.ds(pl.multiple_of(apart + within, BLOCK_TOKENS), BLOCK_TOKENS)
        there = pl.ds(theirs.shape[0] - BLOCK_TOKENS, BLOCK_TOKENS)
        return (
            near,
            pair(keys_mine.at[block], values_mine.at[:, block]),
            pair(theirs.at[there, block], theirs.at[there, beyond]),
        )

    def start_block(j, carry):
        near, mine, theirs = block_copies(j)

        @pl.when(near)
        def _():
            for copy in mine:
                copy.start()

        @pl.when(jnp.logical_not(near))
        def _():
            for copy in theirs:
                copy.start()

        return carry

    def wait_block(j, carry):
        _, mine, _ = block_copies(j)
        for copy in mine:
            copy.wait()
        return carry

    per_chunk = KEY_CHUNK // BLOCK_TOKENS
    blocks = count + side * (rows // BLOCK_TOKENS)
    full = blocks // per_chunk

    if not aliased:
        for copy in new_copies(new_mine, 0, 0):
            copy.start()

        @pl.when(side == 1)
        def _():
            for copy in new_copies(new_theirs, rows, 1):
                copy.start()

        lax.fori_loop(0, count, start_block, 0)
        vt_all[pl.ds(HEAD_SIZE, ONES), :] = jnp.ones((ONES, vt_all.shape[1]), jnp.bfloat16)

    for r in range(GROUP):
        for head in range(heads):
            q_all[r * heads + head] = qs[r][:, pl.ds(head * HEAD_SIZE, HEAD_SIZE)]

    def absorb(row, size, how, allowed=None):
        keys = k_all[pl.ds(row, size), :]
        values = vt_all[:, pl.ds(row, size)]

        def score(unit):
            return lax.dot_general(
                keys, q_all[unit], (((1,), (1,)), ((), ())), preferred_element_type=jnp.float32
            )

        def some(index, carry):
            begin = index * UNROLL
            ahead = score(begin)
            for step in range(UNROLL):
                unit = begin + step
                s = ahead
                if step + 1 < UNROLL:
                    ahead = score(unit + 1)
                if allowed is not None:
                    s = jnp.where(allowed, s, -1e30)
                top = before = None if how == "first" else tops[unit]
                if how != "same":
                    top = jnp.max(s.reshape(size // 8, 8, lanes), axis=0)
                    top = jnp.max(top, axis=0, keepdims=True)
                    if how == "rising":
                        top = jnp.maximum(before, top)
                    tops[unit] = top
                weight = jnp.exp2((s - top) * scale)
                mixed = jnp.dot(
                    values, weight.astype(jnp.bfloat16), preferred_element_type=jnp.float32
                )
                if how == "first":
                    sums[unit] = mixed
                elif how == "same":
                    sums[unit] += mixed
                else:
                    sums[unit] = sums[unit] * jnp.exp2((before - top) * scale) + mixed
            return carry

        lax.fori_loop(0, units // UNROLL, some, 0)

    def absorb_own():
        key = lax.broadcasted_iota(jnp.int32, (rows, lanes), 0)
        token = lax.broadcasted_iota(jnp.int32, (rows, lanes), 1)
        absorb(0, rows, "first", key <= token)

    def absorb_rest(how):
        def step(chunk, carry):
            row = pl.multiple_of(rows + chunk * KEY_CHUNK, BLOCK_TOKENS)
            absorb(row, KEY_CHUNK, how)
            return carry

        lax.fori_loop(0, full, step, 0)
        part = per_chunk // 2
        while part:
            size = part * BLOCK_TOKENS

            @pl.when((blocks // part) % 2 == 1)
            def _(part=part, size=size):
                row = pl.multiple_of(rows + (blocks // (2 * part)) * 2 * size, BLOCK_TOKENS)
                absorb(row, size, how)

            part //= 2

    if not aliased:
        for copy in new_copies(new_mine, 0, 0):
            copy.wait()
    absorb_own()
    if not aliased:

        @pl.when(side == 1)
        def _():
            for copy in new_copies(new_theirs, rows, 1):
                copy.wait()

        lax.fori_loop(0, count, wait_block, 0)

    absorb_rest("same")
    fits = jnp.max(sums[:, pl.ds(HEAD_SIZE, 8), :]) < 2.0**100

    @pl.when(jnp.logical_not(fits))
    def _():
        absorb_own()
        absorb_rest("rising")

    group_cols = out.shape[1] // GROUP
    copies = []
    for r in range(GROUP):
        for head in range(heads):
            unit = r * heads + head
            total = sums[unit, pl.ds(HEAD_SIZE, 1), :]
            result = (sums[unit, pl.ds(0, HEAD_SIZE), :] / total).T.astype(jnp.bfloat16)
            o_all[r, :, pl.ds(head * HEAD_SIZE, HEAD_SIZE)] = result
        column = pl.multiple_of((pos ^ r) * group_cols + first, HEAD_SIZE)
        copy = pltpu.make_async_copy(
            o_all.at[r], out.at[:, pl.ds(column, width)], out_sem.at[r]
        )
        copy.start()
        copies.append(copy)
    for copy in copies:
        copy.wait()


def attend(scal, order, qs, sources, first, width, out_cols, tokens):
    rows = qs[0].shape[0]
    slots = order.shape[0]
    heads = width // HEAD_SIZE
    units = GROUP * heads
    aliased = len(sources) == 3
    anywhere = pl.BlockSpec(memory_space=pl.ANY)
    vmem = pl.BlockSpec(memory_space=pltpu.VMEM)
    smem = pl.BlockSpec(memory_space=pltpu.SMEM)
    in_specs = [smem] * 2 + [vmem] * 4
    out_shape = [jax.ShapeDtypeStruct((rows, out_cols), jnp.bfloat16)]
    scratch = []
    if aliased:
        in_specs += [vmem, vmem, anywhere]
    else:
        in_specs += [anywhere] * len(sources)
        out_shape += [
            jax.ShapeDtypeStruct((tokens, HEAD_SIZE), jnp.bfloat16),
            jax.ShapeDtypeStruct((HEAD_SIZE + ONES, tokens), jnp.bfloat16),
        ]
        scratch += [
            pltpu.SemaphoreType.DMA((2, slots)),
            pltpu.SemaphoreType.DMA((2, 1 + rows // HEAD_SIZE)),
        ]
    scratch += [
        pltpu.VMEM((units, rows, HEAD_SIZE), jnp.bfloat16),
        pltpu.VMEM((GROUP, rows, width), jnp.bfloat16),
        pltpu.VMEM((units, 1, rows), jnp.float32),
        pltpu.VMEM((units, HEAD_SIZE + ONES, rows), jnp.float32),
        pltpu.SemaphoreType.DMA((GROUP,)),
    ]
    return pl.pallas_call(
        functools.partial(attend_kernel, first, width, rows, aliased),
        out_shape=out_shape,
        in_specs=in_specs,
        out_specs=[anywhere] + [vmem] * (len(out_shape) - 1),
        input_output_aliases={8: 0} if aliased else {},
        scratch_shapes=scratch,
        compiler_params=pltpu.CompilerParams(vmem_limit_bytes=VMEM_LIMIT),
        cost_estimate=pl.CostEstimate(
            flops=4 * units * rows * tokens * HEAD_SIZE,
            bytes_accessed=4 * tokens * HEAD_SIZE,
            transcendentals=units * rows * tokens,
        ),
    )(scal, order, *qs, *sources)


def on_device(
    hidden,
    w_query,
    key_weight,
    value_weight,
    q_gain,
    key_norm_gain,
    earlier_keys,
    earlier_values,
    counts,
    place,
):
    planes = lax.axis_size("ctx") // GROUP
    ctx = lax.axis_index("ctx")
    plane = ctx // GROUP
    pos = ctx % GROUP
    rows = hidden.shape[0]
    w_rows = w_query.shape[0]
    group_cols = w_query.shape[1] // GROUP
    widths = (group_cols // 2, group_cols - group_cols // 2)

    count = lax.dynamic_index_in_dim(counts, ctx // 2, 0, keepdims=False)
    order = lax.dynamic_index_in_dim(place, ctx // 2, 0, keepdims=False)
    scal = jnp.stack([plane, pos, count, lax.axis_index("tp")]).astype(jnp.int32)
    spots = pos ^ jnp.arange(GROUP, dtype=jnp.int32)
    spot_counts = counts[plane * 2 + spots // 2]
    token_position = (
        spot_counts[:, None] * BLOCK_TOKENS
        + (spots % 2)[:, None] * rows
        + jnp.arange(rows, dtype=jnp.int32)[None, :]
    )
    cosine, sine = rope_tables(token_position.reshape(GROUP * rows))
    key_blocks = earlier_keys.reshape(-1, BLOCK_TOKENS, HEAD_SIZE)
    key_blocks = jnp.transpose(key_blocks, (1, 0, 2)).reshape(BLOCK_TOKENS, -1)
    values_turned = earlier_values.T
    cache_mine = jnp.concatenate([key_blocks, values_turned], axis=1)
    across = GROUP * (planes // 2)
    few = rows // 4

    own, *pieces = pick_columns(w_query, key_weight, value_weight)
    own_far = swap(own, across)
    got = [swap(piece, r) for r, piece in enumerate(pieces, 1)]
    own_near = near(own, planes)
    first, second = split_columns(got, widths)
    hidden, first, second, own_far, cosine, sine, scal, order, cache_mine, values_turned = gate(
        (hidden, first, second, own_far, cosine, sine, scal, order, cache_mine, values_turned),
        (*got, *own_near),
    )

    x_1, x_2 = swap(hidden, 1), swap(hidden, 2)
    first_far = swap(first, across)
    first_near = near(first, planes)
    own_w = own_near + near(own_far, planes)
    x_1, x_2, second, first_far = gate(
        (x_1, x_2, second, first_far), (*first_near, *own_w[planes // 2 + 1 :])
    )

    message = swap(jnp.concatenate([x_2[:few], cache_mine]), 1)
    x_far = swap(x_1[few:], 2)
    x_near = jnp.concatenate([hidden, x_1, x_2])
    core_near = swap_core(x_near)
    second_far = swap(second, across)
    rest_first = first_near + near(first_far, planes)
    parts = project_kv(scal, (x_near, core_near), own_w, group_cols, rows)
    message, x_far, *parts = gate((message, x_far, *parts), ())
    x_3 = jnp.concatenate([message[:few], x_far])
    x_3, second, second_far, *parts = gate(
        (x_3, second, second_far, *parts), rest_first[planes // 2 + 1 :]
    )

    xs = [x_near, x_3, core_near, swap_core(x_3)]
    rest_second = near(second, planes) + near(second_far, planes)

    parts += project_kv(scal, (x_3, xs[3]), own_w, group_cols, rows)
    parts = [parts[0]] + [swap(parts[r], r) for r in range(1, GROUP)]
    keys_mine, values_mine, new_mine = finish_kv(parts, cosine, sine, key_norm_gain[None, :])
    caches = (earlier_keys, values_turned, message)
    news = (new_mine, swap(new_mine, 1))
    gain = q_gain[None, :]

    def queries(scal, rest_w, first, width):
        q = project(scal, xs, own_w, rest_w, cosine, sine, gain, first, width)
        return [q[0]] + [swap(q[r], r) for r in range(1, GROUP)]

    out_cols = w_query.shape[1]
    q_first = queries(
        scal, rest_first, 0, widths[0]
    )
    q_second = queries(after(scal, q_first[0], new_mine), rest_second, widths[0], widths[1])
    tokens = 2 * rows + place.shape[1] * BLOCK_TOKENS
    attended, all_keys, all_values = attend(
        after(scal, q_second[0]), order, q_first, (*caches, *news), 0, widths[0], out_cols, tokens
    )
    (attended,) = attend(
        scal,
        order,
        q_second,
        (all_keys, all_values, attended),
        widths[0],
        widths[1],
        out_cols,
        tokens,
    )
    return (attended, keys_mine, values_mine)


def solution(mesh):
    placed = (
        P("ctx", "tp"),
        P("ctx", "tp"),
        P("ctx", "tp"),
        P("ctx", "tp"),
        P(),
        P(),
        P("ctx", "tp"),
        P("ctx", "tp"),
        P(),
        P(),
    )
    return jax.shard_map(
        on_device,
        mesh=mesh,
        in_specs=placed,
        out_specs=(P("ctx", "tp"), P("ctx", "tp"), P("ctx", "tp")),
        check_vma=False,
    )
```

```python
import functools
import math

import jax
import jax.numpy as jnp
from jax import lax
from jax.experimental import pallas as pl
from jax.experimental.pallas import tpu as pltpu
from jax.sharding import PartitionSpec as P

HEAD_SIZE = 128
BLOCK_TOKENS = 128
GROUP = 4
KEY_CHUNK = 1024
ONES = 16
UNROLL = 8
VMEM_LIMIT = 16 * 1024 * 1024


def swap(value, mask):
    pairs = [(source, source ^ mask) for source in range(lax.axis_size("ctx"))]
    return lax.ppermute(value, "ctx", pairs)


def swap_core(value):
    return lax.ppermute(value, "tp", [(0, 1), (1, 0)])


def after(value, *others):
    return lax.optimization_barrier((value, *others))[0]


def near(source, planes):
    pieces = [source]
    bit = 1
    while bit < planes // 2:
        pieces = pieces + [swap(piece, GROUP * bit) for piece in pieces]
        bit *= 2
    return pieces


def gate(values, done):
    return lax.optimization_barrier((tuple(values), tuple(done)))[0]


def rope_tables(token_position):
    half = HEAD_SIZE // 2
    freq = jnp.exp(jnp.arange(half, dtype=jnp.float32) * (-2.0 / HEAD_SIZE) * math.log(1000000.0))
    angle = token_position.astype(jnp.float32)[..., None] * freq
    cosine, sine = jnp.cos(angle), jnp.sin(angle)
    return (
        jnp.concatenate([cosine, cosine], axis=-1),
        jnp.concatenate([-sine, sine], axis=-1),
    )


def half_slot(scal, planes, apart):
    there = scal[0] ^ apart
    other = (there // (planes // 2)) ^ scal[3]
    return other * (planes // 2) + there % (planes // 2)


def pick_columns_kernel(w_ref, key_ref, value_ref, own, *refs):
    *others, sems = refs
    pos = lax.axis_index("ctx") % GROUP
    cols = others[0].shape[1]

    def columns_for(r):
        return w_ref.at[:, pl.ds(pl.multiple_of((pos ^ r) * cols, cols), cols)]

    pairs = [
        (columns_for(0), own.at[:, pl.ds(0, cols)]),
        (key_ref, own.at[:, pl.ds(cols, HEAD_SIZE)]),
        (value_ref, own.at[:, pl.ds(cols + HEAD_SIZE, HEAD_SIZE)]),
    ]
    pairs += [(columns_for(1 + index), out) for index, out in enumerate(others)]
    copies = []
    for index, (src, dst) in enumerate(pairs):
        copy = pltpu.make_async_copy(src, dst, sems.at[index])
        copy.start()
        copies.append(copy)
    for copy in copies:
        copy.wait()


def pick_columns(w_query, key_weight, value_weight):
    rows = w_query.shape[0]
    cols = w_query.shape[1] // GROUP
    anywhere = pl.BlockSpec(memory_space=pl.ANY)
    widths = [cols + 2 * HEAD_SIZE] + [cols] * (GROUP - 1)
    return pl.pallas_call(
        pick_columns_kernel,
        out_shape=[jax.ShapeDtypeStruct((rows, width), jnp.bfloat16) for width in widths],
        in_specs=[anywhere] * 3,
        out_specs=[pl.BlockSpec(memory_space=pltpu.VMEM)] * GROUP,
        scratch_shapes=[pltpu.SemaphoreType.DMA((GROUP + 2,))],
        compiler_params=pltpu.CompilerParams(vmem_limit_bytes=60 * 1024 * 1024),
    )(w_query, key_weight, value_weight)


def split_columns_kernel(widths, *refs):
    *got, first, second, sems = refs
    copies = []
    for index, piece in enumerate(got):
        begin = 0
        for part, out in enumerate((first, second)):
            cols = pl.ds(begin, widths[part])
            copy = pltpu.make_async_copy(
                piece.at[:, cols],
                out.at[:, pl.ds(index * widths[part], widths[part])],
                sems.at[index, part],
            )
            copy.start()
            copies.append(copy)
            begin += widths[part]
    for copy in copies:
        copy.wait()


def split_columns(got, widths):
    rows = got[0].shape[0]
    anywhere = pl.BlockSpec(memory_space=pl.ANY)
    return pl.pallas_call(
        functools.partial(split_columns_kernel, widths),
        out_shape=[
            jax.ShapeDtypeStruct((rows, len(got) * width), jnp.bfloat16) for width in widths
        ],
        in_specs=[anywhere] * len(got),
        out_specs=[anywhere] * 2,
        scratch_shapes=[pltpu.SemaphoreType.DMA((len(got), 2))],
        compiler_params=pltpu.CompilerParams(vmem_limit_bytes=VMEM_LIMIT // 16),
    )(*got)


def project_kernel(planes, first, width, *refs):
    scal, refs = refs[0], refs[1:]
    xs, refs = refs[:4], refs[4:]
    own_w, rest_w, refs = refs[:planes], refs[planes : 2 * planes], refs[2 * planes :]
    cosine, sine, gain, *q_out, w_all, w_sem = refs
    pos = scal[1]
    half_cols = xs[0].shape[1]
    w_rows = own_w[0].shape[0]

    copies = []
    for apart in range(planes):
        base = half_slot(scal, planes, apart) * GROUP
        for r in range(GROUP):
            if r == 0:
                src = own_w[apart].at[:, pl.ds(first, width)]
            else:
                src = rest_w[apart].at[:, pl.ds((r - 1) * width, width)]
            row = pl.multiple_of((base + (pos ^ r)) * w_rows, w_rows)
            copy = pltpu.make_async_copy(
                src, w_all.at[pl.ds(row, w_rows)], w_sem.at[apart, r]
            )
            copy.start()
            copies.append(copy)
    for copy in copies:
        copy.wait()

    rows = q_out[0].shape[0]
    for block in range(GROUP):
        part, begin = (0, block * rows) if block < GROUP - 1 else (1, 0)
        result = jnp.dot(
            xs[part][pl.ds(begin, rows), :],
            w_all[pl.ds(0, half_cols), :],
            preferred_element_type=jnp.float32,
        ) + jnp.dot(
            xs[2 + part][pl.ds(begin, rows), :],
            w_all[pl.ds(half_cols, half_cols), :],
            preferred_element_type=jnp.float32,
        )
        tokens = pl.ds(block * rows, rows)
        for head in range(width // HEAD_SIZE):
            values = result[:, head * HEAD_SIZE : (head + 1) * HEAD_SIZE]
            mean = jnp.mean(values * values, axis=-1, keepdims=True)
            scaled = values * lax.rsqrt(mean + 1e-06) * gain[...]
            turned = (
                scaled * cosine[tokens, :]
                + pltpu.roll(scaled, HEAD_SIZE // 2, 1) * sine[tokens, :]
            )
            q_out[block][:, pl.ds(head * HEAD_SIZE, HEAD_SIZE)] = turned.astype(jnp.bfloat16)


def project(scal, xs, own_w, rest_w, cosine, sine, gain, first, width):
    planes = len(own_w)
    rows, half_cols = xs[1].shape
    depth = 2 * half_cols
    anywhere = pl.BlockSpec(memory_space=pl.ANY)
    vmem = pl.BlockSpec(memory_space=pltpu.VMEM)
    return pl.pallas_call(
        functools.partial(project_kernel, planes, first, width),
        out_shape=[jax.ShapeDtypeStruct((rows, width), jnp.bfloat16)] * GROUP,
        in_specs=[pl.BlockSpec(memory_space=pltpu.SMEM)]
        + [vmem] * 4
        + [anywhere] * (2 * planes)
        + [vmem] * 3,
        out_specs=[vmem] * GROUP,
        scratch_shapes=[
            pltpu.VMEM((depth, width), jnp.bfloat16),
            pltpu.SemaphoreType.DMA((planes, GROUP)),
        ],
        compiler_params=pltpu.CompilerParams(vmem_limit_bytes=VMEM_LIMIT),
        cost_estimate=pl.CostEstimate(
            flops=2 * GROUP * rows * depth * width,
            bytes_accessed=2 * depth * (GROUP * rows + width),
            transcendentals=0,
        ),
    )(scal, *xs, *own_w, *rest_w, cosine, sine, gain)


def project_kv_kernel(planes, skip, *refs):
    scal, refs = refs[0], refs[1:]
    xs, own_w, refs = refs[:2], refs[2 : 2 + planes], refs[2 + planes :]
    *kv_out, x_all, w_all, x_sem, w_sem = refs
    pos = scal[1]
    w_rows = own_w[0].shape[0]
    _, depth, width = w_all.shape
    compact = depth == w_rows
    offset = pos * w_rows if compact else 0

    copies = []
    for apart in range(planes):
        slot = half_slot(scal, planes, apart)
        row = 0
        if not compact:
            w_all[slot] = jnp.zeros((depth, width), jnp.bfloat16)
            row = pl.multiple_of(pos * w_rows, w_rows)
        copy = pltpu.make_async_copy(
            own_w[apart].at[:, pl.ds(skip, width)],
            w_all.at[slot, pl.ds(row, w_rows)],
            w_sem.at[apart],
        )
        copy.start()
        copies.append(copy)
    for slot in range(planes):
        half, within = slot // (planes // 2), slot % (planes // 2)
        column = pl.multiple_of(within * GROUP * w_rows + offset, HEAD_SIZE)
        copy = pltpu.make_async_copy(
            xs[half].at[:, pl.ds(column, depth)], x_all.at[slot], x_sem.at[slot]
        )
        copy.start()
        copies.append(copy)
    for copy in copies:
        copy.wait()
    result = None
    for slot in range(planes):
        term = jnp.dot(x_all[slot], w_all[slot], preferred_element_type=jnp.float32)
        result = term if result is None else result + term
    rows = kv_out[0].shape[0]
    for block, out in enumerate(kv_out):
        out[...] = result[block * rows : (block + 1) * rows]


def project_kv(scal, xs, own_w, skip, rows):
    planes = len(own_w)
    tokens = xs[0].shape[0]
    w_rows = own_w[0].shape[0]
    width = own_w[0].shape[1] - skip
    depth = w_rows if w_rows % HEAD_SIZE == 0 else GROUP * w_rows
    anywhere = pl.BlockSpec(memory_space=pl.ANY)
    return pl.pallas_call(
        functools.partial(project_kv_kernel, planes, skip),
        out_shape=[jax.ShapeDtypeStruct((rows, width), jnp.float32)] * (tokens // rows),
        in_specs=[pl.BlockSpec(memory_space=pltpu.SMEM)] + [anywhere] * (2 + planes),
        out_specs=[pl.BlockSpec(memory_space=pltpu.VMEM)] * (tokens // rows),
        scratch_shapes=[
            pltpu.VMEM((planes, tokens, depth), jnp.bfloat16),
            pltpu.VMEM((planes, depth, width), jnp.bfloat16),
            pltpu.SemaphoreType.DMA((planes,)),
            pltpu.SemaphoreType.DMA((planes,)),
        ],
        compiler_params=pltpu.CompilerParams(vmem_limit_bytes=VMEM_LIMIT),
        cost_estimate=pl.CostEstimate(
            flops=2 * tokens * depth * planes * width,
            bytes_accessed=2 * depth * planes * (tokens + width),
            transcendentals=0,
        ),
    )(scal, *xs, *own_w)


def finish_kv_kernel(mine, *refs):
    *others, cosine, sine, gain, keys_out, values_out, both_out = refs
    summed = mine[...]
    for other in others:
        summed = summed + other[...]
    keys = summed[:, :HEAD_SIZE]
    mean = jnp.mean(keys * keys, axis=-1, keepdims=True)
    scaled = keys * lax.rsqrt(mean + 1e-06) * gain[...]
    own = pl.ds(0, keys.shape[0])
    turned = scaled * cosine[own, :] + pltpu.roll(scaled, HEAD_SIZE // 2, 1) * sine[own, :]
    keys_out[...] = turned.astype(jnp.bfloat16)
    values_out[...] = summed[:, HEAD_SIZE:].astype(jnp.bfloat16)
    both_out[0] = keys_out[...]
    turned_values = summed[:, HEAD_SIZE:].T.astype(jnp.bfloat16)
    for begin in range(0, keys.shape[0], HEAD_SIZE):
        both_out[1, pl.ds(begin, HEAD_SIZE), :] = turned_values[:, begin : begin + HEAD_SIZE]


def finish_kv(parts, cosine, sine, gain):
    rows = parts[0].shape[0]
    one = jax.ShapeDtypeStruct((rows, HEAD_SIZE), jnp.bfloat16)
    vmem = pl.BlockSpec(memory_space=pltpu.VMEM)
    return pl.pallas_call(
        finish_kv_kernel,
        out_shape=[one, one, jax.ShapeDtypeStruct((2, rows, HEAD_SIZE), jnp.bfloat16)],
        in_specs=[vmem] * (len(parts) + 3),
        out_specs=[vmem] * 3,
        compiler_params=pltpu.CompilerParams(vmem_limit_bytes=VMEM_LIMIT // 4),
    )(*parts, cosine, sine, gain)


def attend_kernel(first, width, rows, aliased, *refs):
    scal, order = refs[:2]
    qs = refs[2:6]
    if aliased:
        k_all, vt_all, _, out, *refs = refs[6:]
    else:
        keys_mine, values_mine, theirs, new_mine, new_theirs, out, k_all, vt_all, *refs = refs[6:]
        kv_sem, new_sem, *refs = refs
    q_all, o_all, tops, sums, out_sem = refs
    pos, count = scal[1], scal[2]
    side = pos % 2
    heads = width // HEAD_SIZE
    slots = order.shape[0]
    half_slots = slots // 2
    scale = HEAD_SIZE ** (-0.5) * math.log2(math.e)
    units = GROUP * heads
    lanes = rows

    lead = rows + side * rows

    def new_copies(new, row, index):
        copies = [
            pltpu.make_async_copy(
                new.at[0], k_all.at[pl.ds(row, rows)], new_sem.at[index, 0]
            )
        ]
        for begin in range(0, rows, HEAD_SIZE):
            copies.append(
                pltpu.make_async_copy(
                    new.at[1, pl.ds(begin, HEAD_SIZE)],
                    vt_all.at[pl.ds(0, HEAD_SIZE), pl.ds(row + begin, HEAD_SIZE)],
                    new_sem.at[index, 1 + begin // HEAD_SIZE],
                )
            )
        return copies

    def block_copies(j):
        slot = order[j]
        within = pl.multiple_of((slot % half_slots) * BLOCK_TOKENS, BLOCK_TOKENS)
        dst_row = pl.multiple_of(lead + j * BLOCK_TOKENS, BLOCK_TOKENS)
        near = (slot // half_slots) == side

        def pair(k_src, v_src):
            rows_at = pl.ds(dst_row, BLOCK_TOKENS)
            return (
                pltpu.make_async_copy(k_src, k_all.at[rows_at], kv_sem.at[0, j]),
                pltpu.make_async_copy(
                    v_src, vt_all.at[pl.ds(0, HEAD_SIZE), rows_at], kv_sem.at[1, j]
                ),
            )

        block = pl.ds(within, BLOCK_TOKENS)
        apart = half_slots * BLOCK_TOKENS
        beyond = pl.ds(pl.multiple_of(apart + within, BLOCK_TOKENS), BLOCK_TOKENS)
        there = pl.ds(theirs.shape[0] - BLOCK_TOKENS, BLOCK_TOKENS)
        return (
            near,
            pair(keys_mine.at[block], values_mine.at[:, block]),
            pair(theirs.at[there, block], theirs.at[there, beyond]),
        )

    def start_block(j, carry):
        near, mine, theirs = block_copies(j)

        @pl.when(near)
        def _():
            for copy in mine:
                copy.start()

        @pl.when(jnp.logical_not(near))
        def _():
            for copy in theirs:
                copy.start()

        return carry

    def wait_block(j, carry):
        _, mine, _ = block_copies(j)
        for copy in mine:
            copy.wait()
        return carry

    per_chunk = KEY_CHUNK // BLOCK_TOKENS
    blocks = count + side * (rows // BLOCK_TOKENS)
    full = blocks // per_chunk

    if not aliased:
        for copy in new_copies(new_mine, 0, 0):
            copy.start()

        @pl.when(side == 1)
        def _():
            for copy in new_copies(new_theirs, rows, 1):
                copy.start()

        lax.fori_loop(0, count, start_block, 0)
        vt_all[pl.ds(HEAD_SIZE, ONES), :] = jnp.ones((ONES, vt_all.shape[1]), jnp.bfloat16)

    for r in range(GROUP):
        for head in range(heads):
            q_all[r * heads + head] = qs[r][:, pl.ds(head * HEAD_SIZE, HEAD_SIZE)]

    def absorb(row, size, how, allowed=None):
        keys = k_all[pl.ds(row, size), :]
        values = vt_all[:, pl.ds(row, size)]

        def score(unit):
            return lax.dot_general(
                keys, q_all[unit], (((1,), (1,)), ((), ())), preferred_element_type=jnp.float32
            )

        def some(index, carry):
            begin = index * UNROLL
            ahead = score(begin)
            for step in range(UNROLL):
                unit = begin + step
                s = ahead
                if step + 1 < UNROLL:
                    ahead = score(unit + 1)
                if allowed is not None:
                    s = jnp.where(allowed, s, -1e30)
                top = before = None if how == "first" else tops[unit]
                if how != "same":
                    top = jnp.max(s.reshape(size // 8, 8, lanes), axis=0)
                    top = jnp.max(top, axis=0, keepdims=True)
                    if how == "rising":
                        top = jnp.maximum(before, top)
                    tops[unit] = top
                weight = jnp.exp2((s - top) * scale)
                mixed = jnp.dot(
                    values, weight.astype(jnp.bfloat16), preferred_element_type=jnp.float32
                )
                if how == "first":
                    sums[unit] = mixed
                elif how == "same":
                    sums[unit] += mixed
                else:
                    sums[unit] = sums[unit] * jnp.exp2((before - top) * scale) + mixed
            return carry

        lax.fori_loop(0, units // UNROLL, some, 0)

    def absorb_own():
        key = lax.broadcasted_iota(jnp.int32, (rows, lanes), 0)
        token = lax.broadcasted_iota(jnp.int32, (rows, lanes), 1)
        absorb(0, rows, "first", key <= token)

    def absorb_rest(how):
        def step(chunk, carry):
            row = pl.multiple_of(rows + chunk * KEY_CHUNK, BLOCK_TOKENS)
            absorb(row, KEY_CHUNK, how)
            return carry

        lax.fori_loop(0, full, step, 0)
        part = per_chunk // 2
        while part:
            size = part * BLOCK_TOKENS

            @pl.when((blocks // part) % 2 == 1)
            def _(part=part, size=size):
                row = pl.multiple_of(rows + (blocks // (2 * part)) * 2 * size, BLOCK_TOKENS)
                absorb(row, size, how)

            part //= 2

    if not aliased:
        for copy in new_copies(new_mine, 0, 0):
            copy.wait()
    absorb_own()
    if not aliased:

        @pl.when(side == 1)
        def _():
            for copy in new_copies(new_theirs, rows, 1):
                copy.wait()

        lax.fori_loop(0, count, wait_block, 0)

    absorb_rest("same")
    fits = jnp.max(sums[:, pl.ds(HEAD_SIZE, 8), :]) < 2.0**100

    @pl.when(jnp.logical_not(fits))
    def _():
        absorb_own()
        absorb_rest("rising")

    group_cols = out.shape[1] // GROUP
    copies = []
    for r in range(GROUP):
        for head in range(heads):
            unit = r * heads + head
            total = sums[unit, pl.ds(HEAD_SIZE, 1), :]
            result = (sums[unit, pl.ds(0, HEAD_SIZE), :] / total).T.astype(jnp.bfloat16)
            o_all[r, :, pl.ds(head * HEAD_SIZE, HEAD_SIZE)] = result
        column = pl.multiple_of((pos ^ r) * group_cols + first, HEAD_SIZE)
        copy = pltpu.make_async_copy(
            o_all.at[r], out.at[:, pl.ds(column, width)], out_sem.at[r]
        )
        copy.start()
        copies.append(copy)
    for copy in copies:
        copy.wait()


def attend(scal, order, qs, sources, first, width, out_cols, tokens):
    rows = qs[0].shape[0]
    slots = order.shape[0]
    heads = width // HEAD_SIZE
    units = GROUP * heads
    aliased = len(sources) == 3
    anywhere = pl.BlockSpec(memory_space=pl.ANY)
    vmem = pl.BlockSpec(memory_space=pltpu.VMEM)
    smem = pl.BlockSpec(memory_space=pltpu.SMEM)
    in_specs = [smem] * 2 + [vmem] * 4
    out_shape = [jax.ShapeDtypeStruct((rows, out_cols), jnp.bfloat16)]
    scratch = []
    if aliased:
        in_specs += [vmem, vmem, anywhere]
    else:
        in_specs += [anywhere] * len(sources)
        out_shape += [
            jax.ShapeDtypeStruct((tokens, HEAD_SIZE), jnp.bfloat16),
            jax.ShapeDtypeStruct((HEAD_SIZE + ONES, tokens), jnp.bfloat16),
        ]
        scratch += [
            pltpu.SemaphoreType.DMA((2, slots)),
            pltpu.SemaphoreType.DMA((2, 1 + rows // HEAD_SIZE)),
        ]
    scratch += [
        pltpu.VMEM((units, rows, HEAD_SIZE), jnp.bfloat16),
        pltpu.VMEM((GROUP, rows, width), jnp.bfloat16),
        pltpu.VMEM((units, 1, rows), jnp.float32),
        pltpu.VMEM((units, HEAD_SIZE + ONES, rows), jnp.float32),
        pltpu.SemaphoreType.DMA((GROUP,)),
    ]
    return pl.pallas_call(
        functools.partial(attend_kernel, first, width, rows, aliased),
        out_shape=out_shape,
        in_specs=in_specs,
        out_specs=[anywhere] + [vmem] * (len(out_shape) - 1),
        input_output_aliases={8: 0} if aliased else {},
        scratch_shapes=scratch,
        compiler_params=pltpu.CompilerParams(vmem_limit_bytes=VMEM_LIMIT),
        cost_estimate=pl.CostEstimate(
            flops=4 * units * rows * tokens * HEAD_SIZE,
            bytes_accessed=4 * tokens * HEAD_SIZE,
            transcendentals=units * rows * tokens,
        ),
    )(scal, order, *qs, *sources)


def on_device(
    hidden,
    w_query,
    key_weight,
    value_weight,
    q_gain,
    key_norm_gain,
    earlier_keys,
    earlier_values,
    counts,
    place,
):
    planes = lax.axis_size("ctx") // GROUP
    ctx = lax.axis_index("ctx")
    plane = ctx // GROUP
    pos = ctx % GROUP
    rows = hidden.shape[0]
    w_rows = w_query.shape[0]
    group_cols = w_query.shape[1] // GROUP
    widths = (group_cols // 2, group_cols - group_cols // 2)

    count = lax.dynamic_index_in_dim(counts, ctx // 2, 0, keepdims=False)
    order = lax.dynamic_index_in_dim(place, ctx // 2, 0, keepdims=False)
    scal = jnp.stack([plane, pos, count, lax.axis_index("tp")]).astype(jnp.int32)
    spots = pos ^ jnp.arange(GROUP, dtype=jnp.int32)
    spot_counts = counts[plane * 2 + spots // 2]
    token_position = (
        spot_counts[:, None] * BLOCK_TOKENS
        + (spots % 2)[:, None] * rows
        + jnp.arange(rows, dtype=jnp.int32)[None, :]
    )
    cosine, sine = rope_tables(token_position.reshape(GROUP * rows))
    key_blocks = earlier_keys.reshape(-1, BLOCK_TOKENS, HEAD_SIZE)
    key_blocks = jnp.transpose(key_blocks, (1, 0, 2)).reshape(BLOCK_TOKENS, -1)
    values_turned = earlier_values.T
    cache_mine = jnp.concatenate([key_blocks, values_turned], axis=1)
    across = GROUP * (planes // 2)
    few = rows // 4

    own, *pieces = pick_columns(w_query, key_weight, value_weight)
    own_far = swap(own, across)
    got = [swap(piece, r) for r, piece in enumerate(pieces, 1)]
    own_near = near(own, planes)
    first, second = split_columns(got, widths)
    hidden, first, second, own_far, cosine, sine, scal, order, cache_mine, values_turned = gate(
        (hidden, first, second, own_far, cosine, sine, scal, order, cache_mine, values_turned),
        (*got, *own_near),
    )

    x_1, x_2 = swap(hidden, 1), swap(hidden, 2)
    first_far = swap(first, across)
    first_near = near(first, planes)
    own_w = own_near + near(own_far, planes)
    x_1, x_2, second, first_far = gate(
        (x_1, x_2, second, first_far), (*first_near, *own_w[planes // 2 + 1 :])
    )

    message = swap(jnp.concatenate([x_2[:few], cache_mine]), 1)
    x_far = swap(x_1[few:], 2)
    x_near = jnp.concatenate([hidden, x_1, x_2])
    core_near = swap_core(x_near)
    second_far = swap(second, across)
    rest_first = first_near + near(first_far, planes)
    parts = project_kv(scal, (x_near, core_near), own_w, group_cols, rows)
    message, x_far, *parts = gate((message, x_far, *parts), ())
    x_3 = jnp.concatenate([message[:few], x_far])
    x_3, second, second_far, *parts = gate(
        (x_3, second, second_far, *parts), rest_first[planes // 2 + 1 :]
    )

    xs = [x_near, x_3, core_near, swap_core(x_3)]
    rest_second = near(second, planes) + near(second_far, planes)

    parts += project_kv(scal, (x_3, xs[3]), own_w, group_cols, rows)
    parts = [parts[0]] + [swap(parts[r], r) for r in range(1, GROUP)]
    keys_mine, values_mine, new_mine = finish_kv(parts, cosine, sine, key_norm_gain[None, :])
    caches = (earlier_keys, values_turned, message)
    news = (new_mine, swap(new_mine, 1))
    gain = q_gain[None, :]

    def queries(scal, rest_w, first, width):
        q = project(scal, xs, own_w, rest_w, cosine, sine, gain, first, width)
        return [q[0]] + [swap(q[r], r) for r in range(1, GROUP)]

    out_cols = w_query.shape[1]
    q_first = queries(
        scal, rest_first, 0, widths[0]
    )
    q_second = queries(after(scal, q_first[0], new_mine), rest_second, widths[0], widths[1])
    tokens = 2 * rows + place.shape[1] * BLOCK_TOKENS
    attended, all_keys, all_values = attend(
        after(scal, q_second[0]), order, q_first, (*caches, *news), 0, widths[0], out_cols, tokens
    )
    (attended,) = attend(
        scal,
        order,
        q_second,
        (all_keys, all_values, attended),
        widths[0],
        widths[1],
        out_cols,
        tokens,
    )
    return (attended, keys_mine, values_mine)


def solution(mesh):
    placed = (
        P("ctx", "tp"),
        P("ctx", "tp"),
        P("ctx", "tp"),
        P("ctx", "tp"),
        P(),
        P(),
        P("ctx", "tp"),
        P("ctx", "tp"),
        P(),
        P(),
    )
    return jax.shard_map(
        on_device,
        mesh=mesh,
        in_specs=placed,
        out_specs=(P("ctx", "tp"), P("ctx", "tp"), P("ctx", "tp")),
        check_vma=False,
    )
```

```python
import functools
import math

import jax
import jax.numpy as jnp
from jax import lax
from jax.experimental import pallas as pl
from jax.experimental.pallas import tpu as pltpu
from jax.sharding import PartitionSpec as P

HEAD_SIZE = 128
BLOCK_TOKENS = 128
GROUP = 4
KEY_CHUNK = 1024
ONES = 16
UNROLL = 8
VMEM_LIMIT = 16 * 1024 * 1024


def swap(value, mask):
    pairs = [(source, source ^ mask) for source in range(lax.axis_size("ctx"))]
    return lax.ppermute(value, "ctx", pairs)


def swap_core(value):
    return lax.ppermute(value, "tp", [(0, 1), (1, 0)])


def after(value, *others):
    return lax.optimization_barrier((value, *others))[0]


def near(source, planes):
    pieces = [source]
    bit = 1
    while bit < planes // 2:
        pieces = pieces + [swap(piece, GROUP * bit) for piece in pieces]
        bit *= 2
    return pieces


def gate(values, done):
    return lax.optimization_barrier((tuple(values), tuple(done)))[0]


def rope_tables(token_position):
    half = HEAD_SIZE // 2
    freq = jnp.exp(jnp.arange(half, dtype=jnp.float32) * (-2.0 / HEAD_SIZE) * math.log(1000000.0))
    angle = token_position.astype(jnp.float32)[..., None] * freq
    cosine, sine = jnp.cos(angle), jnp.sin(angle)
    return (
        jnp.concatenate([cosine, cosine], axis=-1),
        jnp.concatenate([-sine, sine], axis=-1),
    )


def half_slot(scal, planes, apart):
    there = scal[0] ^ apart
    other = (there // (planes // 2)) ^ scal[3]
    return other * (planes // 2) + there % (planes // 2)


def pick_columns_kernel(w_ref, key_ref, value_ref, own, *refs):
    *others, sems = refs
    pos = lax.axis_index("ctx") % GROUP
    cols = others[0].shape[1]

    def columns_for(r):
        return w_ref.at[:, pl.ds(pl.multiple_of((pos ^ r) * cols, cols), cols)]

    pairs = [
        (columns_for(0), own.at[:, pl.ds(0, cols)]),
        (key_ref, own.at[:, pl.ds(cols, HEAD_SIZE)]),
        (value_ref, own.at[:, pl.ds(cols + HEAD_SIZE, HEAD_SIZE)]),
    ]
    pairs += [(columns_for(1 + index), out) for index, out in enumerate(others)]
    copies = []
    for index, (src, dst) in enumerate(pairs):
        copy = pltpu.make_async_copy(src, dst, sems.at[index])
        copy.start()
        copies.append(copy)
    for copy in copies:
        copy.wait()


def pick_columns(w_query, key_weight, value_weight):
    rows = w_query.shape[0]
    cols = w_query.shape[1] // GROUP
    anywhere = pl.BlockSpec(memory_space=pl.ANY)
    widths = [cols + 2 * HEAD_SIZE] + [cols] * (GROUP - 1)
    return pl.pallas_call(
        pick_columns_kernel,
        out_shape=[jax.ShapeDtypeStruct((rows, width), jnp.bfloat16) for width in widths],
        in_specs=[anywhere] * 3,
        out_specs=[pl.BlockSpec(memory_space=pltpu.VMEM)] * GROUP,
        scratch_shapes=[pltpu.SemaphoreType.DMA((GROUP + 2,))],
        compiler_params=pltpu.CompilerParams(vmem_limit_bytes=60 * 1024 * 1024),
    )(w_query, key_weight, value_weight)


def split_columns_kernel(widths, *refs):
    *got, first, second, sems = refs
    copies = []
    for index, piece in enumerate(got):
        begin = 0
        for part, out in enumerate((first, second)):
            cols = pl.ds(begin, widths[part])
            copy = pltpu.make_async_copy(
                piece.at[:, cols],
                out.at[:, pl.ds(index * widths[part], widths[part])],
                sems.at[index, part],
            )
            copy.start()
            copies.append(copy)
            begin += widths[part]
    for copy in copies:
        copy.wait()


def split_columns(got, widths):
    rows = got[0].shape[0]
    anywhere = pl.BlockSpec(memory_space=pl.ANY)
    return pl.pallas_call(
        functools.partial(split_columns_kernel, widths),
        out_shape=[
            jax.ShapeDtypeStruct((rows, len(got) * width), jnp.bfloat16) for width in widths
        ],
        in_specs=[anywhere] * len(got),
        out_specs=[anywhere] * 2,
        scratch_shapes=[pltpu.SemaphoreType.DMA((len(got), 2))],
        compiler_params=pltpu.CompilerParams(vmem_limit_bytes=VMEM_LIMIT // 16),
    )(*got)


def project_kernel(planes, first, width, steps, begun, ends, *refs):
    scal, refs = refs[0], refs[1:]
    xs, refs = refs[:4], refs[4:]
    own_w, rest_w, refs = refs[:planes], refs[planes : 2 * planes], refs[2 * planes :]
    so_far, refs = (refs[:GROUP], refs[GROUP:]) if begun else (None, refs)
    cosine, sine, gain, refs = (*refs[:3], refs[3:]) if ends else (None, None, None, refs)
    *outs, w_all, w_sem = refs
    plane, pos, core = scal[0], scal[1], scal[3]
    w_rows = own_w[0].shape[0]
    half = planes // 2
    depth = GROUP * w_rows

    copies = []
    for index, step in enumerate(steps):
        for apart in (step, half + step):
            other = ((plane ^ apart) // half) ^ core
            for r in range(GROUP):
                if r == 0:
                    src = own_w[apart].at[:, pl.ds(first, width)]
                else:
                    src = rest_w[apart].at[:, pl.ds((r - 1) * width, width)]
                row = pl.multiple_of((pos ^ r) * w_rows, w_rows)
                copy = pltpu.make_async_copy(
                    src, w_all.at[index, other, pl.ds(row, w_rows)], w_sem.at[apart, r]
                )
                copy.start()
                copies.append(copy)
    for copy in copies:
        copy.wait()

    rows = outs[0].shape[0]
    for block in range(GROUP):
        part, begin = (0, block * rows) if block < GROUP - 1 else (1, 0)
        result = so_far[block][...] if begun else None
        for index, step in enumerate(steps):
            column = pl.multiple_of(((plane % half) ^ step) * depth, depth)
            for other in range(2):
                term = jnp.dot(
                    xs[2 * other + part][pl.ds(begin, rows), pl.ds(column, depth)],
                    w_all[index, other],
                    preferred_element_type=jnp.float32,
                )
                result = term if result is None else result + term
        if not ends:
            outs[block][...] = result
            continue
        tokens = pl.ds(block * rows, rows)
        for head in range(width // HEAD_SIZE):
            values = result[:, head * HEAD_SIZE : (head + 1) * HEAD_SIZE]
            mean = jnp.mean(values * values, axis=-1, keepdims=True)
            scaled = values * lax.rsqrt(mean + 1e-06) * gain[...]
            turned = (
                scaled * cosine[tokens, :]
                + pltpu.roll(scaled, HEAD_SIZE // 2, 1) * sine[tokens, :]
            )
            outs[block][:, pl.ds(head * HEAD_SIZE, HEAD_SIZE)] = turned.astype(jnp.bfloat16)


def project(scal, xs, own_w, rest_w, first, width, steps, so_far, finish):
    planes = len(own_w)
    rows = xs[1].shape[0]
    depth = GROUP * own_w[0].shape[0]
    out_type = jnp.float32 if finish is None else jnp.bfloat16
    extra = [*(so_far or ()), *(finish or ())]
    anywhere = pl.BlockSpec(memory_space=pl.ANY)
    vmem = pl.BlockSpec(memory_space=pltpu.VMEM)
    return pl.pallas_call(
        functools.partial(
            project_kernel, planes, first, width, steps, so_far is not None, finish is not None
        ),
        out_shape=[jax.ShapeDtypeStruct((rows, width), out_type)] * GROUP,
        in_specs=[pl.BlockSpec(memory_space=pltpu.SMEM)]
        + [vmem] * 4
        + [anywhere] * (2 * planes)
        + [vmem] * len(extra),
        out_specs=[vmem] * GROUP,
        scratch_shapes=[
            pltpu.VMEM((len(steps), 2, depth, width), jnp.bfloat16),
            pltpu.SemaphoreType.DMA((planes, GROUP)),
        ],
        compiler_params=pltpu.CompilerParams(vmem_limit_bytes=VMEM_LIMIT),
        cost_estimate=pl.CostEstimate(
            flops=4 * len(steps) * GROUP * rows * depth * width,
            bytes_accessed=4 * len(steps) * depth * (GROUP * rows + width),
            transcendentals=0,
        ),
    )(scal, *xs, *own_w, *rest_w, *extra)


def project_kv_kernel(planes, skip, *refs):
    scal, refs = refs[0], refs[1:]
    xs, own_w, refs = refs[:2], refs[2 : 2 + planes], refs[2 + planes :]
    *kv_out, x_all, w_all, x_sem, w_sem = refs
    pos = scal[1]
    w_rows = own_w[0].shape[0]
    _, depth, width = w_all.shape
    compact = depth == w_rows
    offset = pos * w_rows if compact else 0

    copies = []
    for apart in range(planes):
        slot = half_slot(scal, planes, apart)
        row = 0
        if not compact:
            w_all[slot] = jnp.zeros((depth, width), jnp.bfloat16)
            row = pl.multiple_of(pos * w_rows, w_rows)
        copy = pltpu.make_async_copy(
            own_w[apart].at[:, pl.ds(skip, width)],
            w_all.at[slot, pl.ds(row, w_rows)],
            w_sem.at[apart],
        )
        copy.start()
        copies.append(copy)
    for slot in range(planes):
        half, within = slot // (planes // 2), slot % (planes // 2)
        column = pl.multiple_of(within * GROUP * w_rows + offset, HEAD_SIZE)
        copy = pltpu.make_async_copy(
            xs[half].at[:, pl.ds(column, depth)], x_all.at[slot], x_sem.at[slot]
        )
        copy.start()
        copies.append(copy)
    for copy in copies:
        copy.wait()
    result = None
    for slot in range(planes):
        term = jnp.dot(x_all[slot], w_all[slot], preferred_element_type=jnp.float32)
        result = term if result is None else result + term
    rows = kv_out[0].shape[0]
    for block, out in enumerate(kv_out):
        out[...] = result[block * rows : (block + 1) * rows]


def project_kv(scal, xs, own_w, skip, rows):
    planes = len(own_w)
    tokens = xs[0].shape[0]
    w_rows = own_w[0].shape[0]
    width = own_w[0].shape[1] - skip
    depth = w_rows if w_rows % HEAD_SIZE == 0 else GROUP * w_rows
    anywhere = pl.BlockSpec(memory_space=pl.ANY)
    return pl.pallas_call(
        functools.partial(project_kv_kernel, planes, skip),
        out_shape=[jax.ShapeDtypeStruct((rows, width), jnp.float32)] * (tokens // rows),
        in_specs=[pl.BlockSpec(memory_space=pltpu.SMEM)] + [anywhere] * (2 + planes),
        out_specs=[pl.BlockSpec(memory_space=pltpu.VMEM)] * (tokens // rows),
        scratch_shapes=[
            pltpu.VMEM((planes, tokens, depth), jnp.bfloat16),
            pltpu.VMEM((planes, depth, width), jnp.bfloat16),
            pltpu.SemaphoreType.DMA((planes,)),
            pltpu.SemaphoreType.DMA((planes,)),
        ],
        compiler_params=pltpu.CompilerParams(vmem_limit_bytes=VMEM_LIMIT),
        cost_estimate=pl.CostEstimate(
            flops=2 * tokens * depth * planes * width,
            bytes_accessed=2 * depth * planes * (tokens + width),
            transcendentals=0,
        ),
    )(scal, *xs, *own_w)


def finish_kv_kernel(mine, *refs):
    *others, cosine, sine, gain, keys_out, values_out, both_out = refs
    summed = mine[...]
    for other in others:
        summed = summed + other[...]
    keys = summed[:, :HEAD_SIZE]
    mean = jnp.mean(keys * keys, axis=-1, keepdims=True)
    scaled = keys * lax.rsqrt(mean + 1e-06) * gain[...]
    own = pl.ds(0, keys.shape[0])
    turned = scaled * cosine[own, :] + pltpu.roll(scaled, HEAD_SIZE // 2, 1) * sine[own, :]
    keys_out[...] = turned.astype(jnp.bfloat16)
    values_out[...] = summed[:, HEAD_SIZE:].astype(jnp.bfloat16)
    both_out[0] = keys_out[...]
    turned_values = summed[:, HEAD_SIZE:].T.astype(jnp.bfloat16)
    for begin in range(0, keys.shape[0], HEAD_SIZE):
        both_out[1, pl.ds(begin, HEAD_SIZE), :] = turned_values[:, begin : begin + HEAD_SIZE]


def finish_kv(parts, cosine, sine, gain):
    rows = parts[0].shape[0]
    one = jax.ShapeDtypeStruct((rows, HEAD_SIZE), jnp.bfloat16)
    vmem = pl.BlockSpec(memory_space=pltpu.VMEM)
    return pl.pallas_call(
        finish_kv_kernel,
        out_shape=[one, one, jax.ShapeDtypeStruct((2, rows, HEAD_SIZE), jnp.bfloat16)],
        in_specs=[vmem] * (len(parts) + 3),
        out_specs=[vmem] * 3,
        compiler_params=pltpu.CompilerParams(vmem_limit_bytes=VMEM_LIMIT // 4),
    )(*parts, cosine, sine, gain)


def attend_kernel(first, width, rows, aliased, *refs):
    scal, order = refs[:2]
    qs = refs[2:6]
    if aliased:
        k_all, vt_all, _, out, *refs = refs[6:]
    else:
        keys_mine, values_mine, theirs, new_mine, new_theirs, out, k_all, vt_all, *refs = refs[6:]
        kv_sem, new_sem, *refs = refs
    q_all, o_all, tops, sums, out_sem = refs
    pos, count = scal[1], scal[2]
    side = pos % 2
    heads = width // HEAD_SIZE
    slots = order.shape[0]
    half_slots = slots // 2
    scale = HEAD_SIZE ** (-0.5) * math.log2(math.e)
    units = GROUP * heads
    lanes = rows

    lead = rows + side * rows

    def new_copies(new, row, index):
        copies = [
            pltpu.make_async_copy(
                new.at[0], k_all.at[pl.ds(row, rows)], new_sem.at[index, 0]
            )
        ]
        for begin in range(0, rows, HEAD_SIZE):
            copies.append(
                pltpu.make_async_copy(
                    new.at[1, pl.ds(begin, HEAD_SIZE)],
                    vt_all.at[pl.ds(0, HEAD_SIZE), pl.ds(row + begin, HEAD_SIZE)],
                    new_sem.at[index, 1 + begin // HEAD_SIZE],
                )
            )
        return copies

    def block_copies(j):
        slot = order[j]
        within = pl.multiple_of((slot % half_slots) * BLOCK_TOKENS, BLOCK_TOKENS)
        dst_row = pl.multiple_of(lead + j * BLOCK_TOKENS, BLOCK_TOKENS)
        near = (slot // half_slots) == side

        def pair(k_src, v_src):
            rows_at = pl.ds(dst_row, BLOCK_TOKENS)
            return (
                pltpu.make_async_copy(k_src, k_all.at[rows_at], kv_sem.at[0, j]),
                pltpu.make_async_copy(
                    v_src, vt_all.at[pl.ds(0, HEAD_SIZE), rows_at], kv_sem.at[1, j]
                ),
            )

        block = pl.ds(within, BLOCK_TOKENS)
        apart = half_slots * BLOCK_TOKENS
        beyond = pl.ds(pl.multiple_of(apart + within, BLOCK_TOKENS), BLOCK_TOKENS)
        there = pl.ds(theirs.shape[0] - BLOCK_TOKENS, BLOCK_TOKENS)
        return (
            near,
            pair(keys_mine.at[block], values_mine.at[:, block]),
            pair(theirs.at[there, block], theirs.at[there, beyond]),
        )

    def start_block(j, carry):
        near, mine, theirs = block_copies(j)

        @pl.when(near)
        def _():
            for copy in mine:
                copy.start()

        @pl.when(jnp.logical_not(near))
        def _():
            for copy in theirs:
                copy.start()

        return carry

    def wait_block(j, carry):
        _, mine, _ = block_copies(j)
        for copy in mine:
            copy.wait()
        return carry

    per_chunk = KEY_CHUNK // BLOCK_TOKENS
    blocks = count + side * (rows // BLOCK_TOKENS)
    full = blocks // per_chunk

    if not aliased:
        for copy in new_copies(new_mine, 0, 0):
            copy.start()

        @pl.when(side == 1)
        def _():
            for copy in new_copies(new_theirs, rows, 1):
                copy.start()

        lax.fori_loop(0, count, start_block, 0)
        vt_all[pl.ds(HEAD_SIZE, ONES), :] = jnp.ones((ONES, vt_all.shape[1]), jnp.bfloat16)

    for r in range(GROUP):
        for head in range(heads):
            q_all[r * heads + head] = qs[r][:, pl.ds(head * HEAD_SIZE, HEAD_SIZE)]

    def absorb(row, size, how, allowed=None):
        keys = k_all[pl.ds(row, size), :]
        values = vt_all[:, pl.ds(row, size)]

        def score(unit):
            return lax.dot_general(
                keys, q_all[unit], (((1,), (1,)), ((), ())), preferred_element_type=jnp.float32
            )

        def some(index, carry):
            begin = index * UNROLL
            ahead = score(begin)
            for step in range(UNROLL):
                unit = begin + step
                s = ahead
                if step + 1 < UNROLL:
                    ahead = score(unit + 1)
                if allowed is not None:
                    s = jnp.where(allowed, s, -1e30)
                top = before = None if how == "first" else tops[unit]
                if how != "same":
                    top = jnp.max(s.reshape(size // 8, 8, lanes), axis=0)
                    top = jnp.max(top, axis=0, keepdims=True)
                    if how == "rising":
                        top = jnp.maximum(before, top)
                    tops[unit] = top
                weight = jnp.exp2((s - top) * scale)
                mixed = jnp.dot(
                    values, weight.astype(jnp.bfloat16), preferred_element_type=jnp.float32
                )
                if how == "first":
                    sums[unit] = mixed
                elif how == "same":
                    sums[unit] += mixed
                else:
                    sums[unit] = sums[unit] * jnp.exp2((before - top) * scale) + mixed
            return carry

        lax.fori_loop(0, units // UNROLL, some, 0)

    def absorb_own():
        key = lax.broadcasted_iota(jnp.int32, (rows, lanes), 0)
        token = lax.broadcasted_iota(jnp.int32, (rows, lanes), 1)
        absorb(0, rows, "first", key <= token)

    def absorb_rest(how):
        def step(chunk, carry):
            row = pl.multiple_of(rows + chunk * KEY_CHUNK, BLOCK_TOKENS)
            absorb(row, KEY_CHUNK, how)
            return carry

        lax.fori_loop(0, full, step, 0)
        part = per_chunk // 2
        while part:
            size = part * BLOCK_TOKENS

            @pl.when((blocks // part) % 2 == 1)
            def _(part=part, size=size):
                row = pl.multiple_of(rows + (blocks // (2 * part)) * 2 * size, BLOCK_TOKENS)
                absorb(row, size, how)

            part //= 2

    if not aliased:
        for copy in new_copies(new_mine, 0, 0):
            copy.wait()
    absorb_own()
    if not aliased:

        @pl.when(side == 1)
        def _():
            for copy in new_copies(new_theirs, rows, 1):
                copy.wait()

        lax.fori_loop(0, count, wait_block, 0)

    absorb_rest("same")
    fits = jnp.max(sums[:, pl.ds(HEAD_SIZE, 8), :]) < 2.0**100

    @pl.when(jnp.logical_not(fits))
    def _():
        absorb_own()
        absorb_rest("rising")

    group_cols = out.shape[1] // GROUP
    copies = []
    for r in range(GROUP):
        for head in range(heads):
            unit = r * heads + head
            total = sums[unit, pl.ds(HEAD_SIZE, 1), :]
            result = (sums[unit, pl.ds(0, HEAD_SIZE), :] / total).T.astype(jnp.bfloat16)
            o_all[r, :, pl.ds(head * HEAD_SIZE, HEAD_SIZE)] = result
        column = pl.multiple_of((pos ^ r) * group_cols + first, HEAD_SIZE)
        copy = pltpu.make_async_copy(
            o_all.at[r], out.at[:, pl.ds(column, width)], out_sem.at[r]
        )
        copy.start()
        copies.append(copy)
    for copy in copies:
        copy.wait()


def attend(scal, order, qs, sources, first, width, out_cols, tokens):
    rows = qs[0].shape[0]
    slots = order.shape[0]
    heads = width // HEAD_SIZE
    units = GROUP * heads
    aliased = len(sources) == 3
    anywhere = pl.BlockSpec(memory_space=pl.ANY)
    vmem = pl.BlockSpec(memory_space=pltpu.VMEM)
    smem = pl.BlockSpec(memory_space=pltpu.SMEM)
    in_specs = [smem] * 2 + [vmem] * 4
    out_shape = [jax.ShapeDtypeStruct((rows, out_cols), jnp.bfloat16)]
    scratch = []
    if aliased:
        in_specs += [vmem, vmem, anywhere]
    else:
        in_specs += [anywhere] * len(sources)
        out_shape += [
            jax.ShapeDtypeStruct((tokens, HEAD_SIZE), jnp.bfloat16),
            jax.ShapeDtypeStruct((HEAD_SIZE + ONES, tokens), jnp.bfloat16),
        ]
        scratch += [
            pltpu.SemaphoreType.DMA((2, slots)),
            pltpu.SemaphoreType.DMA((2, 1 + rows // HEAD_SIZE)),
        ]
    scratch += [
        pltpu.VMEM((units, rows, HEAD_SIZE), jnp.bfloat16),
        pltpu.VMEM((GROUP, rows, width), jnp.bfloat16),
        pltpu.VMEM((units, 1, rows), jnp.float32),
        pltpu.VMEM((units, HEAD_SIZE + ONES, rows), jnp.float32),
        pltpu.SemaphoreType.DMA((GROUP,)),
    ]
    return pl.pallas_call(
        functools.partial(attend_kernel, first, width, rows, aliased),
        out_shape=out_shape,
        in_specs=in_specs,
        out_specs=[anywhere] + [vmem] * (len(out_shape) - 1),
        input_output_aliases={8: 0} if aliased else {},
        scratch_shapes=scratch,
        compiler_params=pltpu.CompilerParams(vmem_limit_bytes=VMEM_LIMIT),
        cost_estimate=pl.CostEstimate(
            flops=4 * units * rows * tokens * HEAD_SIZE,
            bytes_accessed=4 * tokens * HEAD_SIZE,
            transcendentals=units * rows * tokens,
        ),
    )(scal, order, *qs, *sources)


def on_device(
    hidden,
    w_query,
    key_weight,
    value_weight,
    q_gain,
    key_norm_gain,
    earlier_keys,
    earlier_values,
    counts,
    place,
):
    planes = lax.axis_size("ctx") // GROUP
    ctx = lax.axis_index("ctx")
    plane = ctx // GROUP
    pos = ctx % GROUP
    rows = hidden.shape[0]
    w_rows = w_query.shape[0]
    group_cols = w_query.shape[1] // GROUP
    widths = (group_cols // 2, group_cols - group_cols // 2)

    count = lax.dynamic_index_in_dim(counts, ctx // 2, 0, keepdims=False)
    order = lax.dynamic_index_in_dim(place, ctx // 2, 0, keepdims=False)
    scal = jnp.stack([plane, pos, count, lax.axis_index("tp")]).astype(jnp.int32)
    spots = pos ^ jnp.arange(GROUP, dtype=jnp.int32)
    spot_counts = counts[plane * 2 + spots // 2]
    token_position = (
        spot_counts[:, None] * BLOCK_TOKENS
        + (spots % 2)[:, None] * rows
        + jnp.arange(rows, dtype=jnp.int32)[None, :]
    )
    cosine, sine = rope_tables(token_position.reshape(GROUP * rows))
    key_blocks = earlier_keys.reshape(-1, BLOCK_TOKENS, HEAD_SIZE)
    key_blocks = jnp.transpose(key_blocks, (1, 0, 2)).reshape(BLOCK_TOKENS, -1)
    values_turned = earlier_values.T
    cache_mine = jnp.concatenate([key_blocks, values_turned], axis=1)
    across = GROUP * (planes // 2)
    few = rows // 4

    own, *pieces = pick_columns(w_query, key_weight, value_weight)
    own_far = swap(own, across)
    got = [swap(piece, r) for r, piece in enumerate(pieces, 1)]
    own_near = near(own, planes)
    first, second = split_columns(got, widths)
    hidden, first, second, own_far, cosine, sine, scal, order, cache_mine, values_turned = gate(
        (hidden, first, second, own_far, cosine, sine, scal, order, cache_mine, values_turned),
        own_near,
    )

    x_1, x_2 = swap(hidden, 1), swap(hidden, 2)
    first_far = swap(first, across)
    first_near = near(first, planes)
    own_w = own_near + near(own_far, planes)
    x_1, x_2, second, first_far = gate(
        (x_1, x_2, second, first_far), (*first_near, *own_w[planes // 2 + 1 :])
    )

    message = swap(jnp.concatenate([x_2[:few], cache_mine]), 1)
    x_far = swap(x_1[few:], 2)
    x_near = jnp.concatenate([hidden, x_1, x_2])
    core_near = swap_core(x_near)
    second_far = swap(second, across)
    rest_first = first_near + near(first_far, planes)
    parts = project_kv(scal, (x_near, core_near), own_w, group_cols, rows)
    message, x_far, *parts = gate((message, x_far, *parts), ())
    x_3 = jnp.concatenate([message[:few], x_far])
    x_3, second, second_far, *parts = gate(
        (x_3, second, second_far, *parts), rest_first[planes // 2 + 1 :]
    )

    xs = [x_near, x_3, core_near, swap_core(x_3)]
    rest_second = near(second, planes) + near(second_far, planes)

    parts += project_kv(scal, (x_3, xs[3]), own_w, group_cols, rows)
    parts = [parts[0]] + [swap(parts[r], r) for r in range(1, GROUP)]
    gain = q_gain[None, :]

    finish = (cosine, sine, gain)
    steps = tuple(range(planes // 2))

    def to_owners(q):
        return [q[0]] + [swap(q[r], r) for r in range(1, GROUP)]

    out_cols = w_query.shape[1]
    q_first = to_owners(
        project(scal, xs, own_w, rest_first, 0, widths[0], steps, None, finish)
    )
    here = list(rest_second)
    for apart in range(planes):
        if apart % (planes // 2):
            here[apart] = rest_second[0]
    begun = project(
        after(scal, q_first[0]), xs, own_w, here, widths[0], widths[1], steps[:1], None, None
    )
    parts[0] = after(parts[0], begun[0])
    keys_mine, values_mine, new_mine = finish_kv(parts, cosine, sine, key_norm_gain[None, :])
    caches = (earlier_keys, values_turned, message)
    news = (new_mine, swap(new_mine, 1))
    q_second = to_owners(
        project(
            after(scal, begun[0], new_mine),
            xs,
            own_w,
            rest_second,
            widths[0],
            widths[1],
            steps[1:],
            begun,
            finish,
        )
    )
    tokens = 2 * rows + place.shape[1] * BLOCK_TOKENS
    attended, all_keys, all_values = attend(
        after(scal, q_second[0]), order, q_first, (*caches, *news), 0, widths[0], out_cols, tokens
    )
    (attended,) = attend(
        scal,
        order,
        q_second,
        (all_keys, all_values, attended),
        widths[0],
        widths[1],
        out_cols,
        tokens,
    )
    return (attended, keys_mine, values_mine)


def solution(mesh):
    placed = (
        P("ctx", "tp"),
        P("ctx", "tp"),
        P("ctx", "tp"),
        P("ctx", "tp"),
        P(),
        P(),
        P("ctx", "tp"),
        P("ctx", "tp"),
        P(),
        P(),
    )
    return jax.shard_map(
        on_device,
        mesh=mesh,
        in_specs=placed,
        out_specs=(P("ctx", "tp"), P("ctx", "tp"), P("ctx", "tp")),
        check_vma=False,
    )
```

```python
import functools
import math

import jax
import jax.numpy as jnp
from jax import lax
from jax.experimental import pallas as pl
from jax.experimental.pallas import tpu as pltpu
from jax.sharding import PartitionSpec as P

HEAD_SIZE = 128
BLOCK_TOKENS = 128
GROUP = 4
KEY_CHUNK = 1024
ONES = 16
UNROLL = 8
VMEM_LIMIT = 16 * 1024 * 1024


def swap(value, mask):
    pairs = [(source, source ^ mask) for source in range(lax.axis_size("ctx"))]
    return lax.ppermute(value, "ctx", pairs)


def swap_core(value):
    return lax.ppermute(value, "tp", [(0, 1), (1, 0)])


def after(value, *others):
    return lax.optimization_barrier((value, *others))[0]


def near(source, planes):
    pieces = [source]
    bit = 1
    while bit < planes // 2:
        pieces = pieces + [swap(piece, GROUP * bit) for piece in pieces]
        bit *= 2
    return pieces


def gate(values, done):
    return lax.optimization_barrier((tuple(values), tuple(done)))[0]


def rope_tables(token_position):
    half = HEAD_SIZE // 2
    freq = jnp.exp(jnp.arange(half, dtype=jnp.float32) * (-2.0 / HEAD_SIZE) * math.log(1000000.0))
    angle = token_position.astype(jnp.float32)[..., None] * freq
    cosine, sine = jnp.cos(angle), jnp.sin(angle)
    return (
        jnp.concatenate([cosine, cosine], axis=-1),
        jnp.concatenate([-sine, sine], axis=-1),
    )


def half_slot(scal, planes, apart):
    there = scal[0] ^ apart
    other = (there // (planes // 2)) ^ scal[3]
    return other * (planes // 2) + there % (planes // 2)


def pick_columns_kernel(apart, count, *refs):
    w_ref, extra, outs, sems = refs[0], refs[1 : 1 + count], refs[1 + count : -1], refs[-1]
    pos = lax.axis_index("ctx") % GROUP
    cols = w_ref.shape[1] // GROUP
    pairs = []
    for r, out in zip(apart, outs):
        begin = pl.multiple_of((pos ^ r) * cols, cols)
        pairs.append((w_ref.at[:, pl.ds(begin, cols)], out.at[:, pl.ds(0, cols)]))
    for index, src in enumerate(extra):
        pairs.append((src, outs[0].at[:, pl.ds(cols + index * HEAD_SIZE, HEAD_SIZE)]))
    copies = []
    for index, (src, dst) in enumerate(pairs):
        copy = pltpu.make_async_copy(src, dst, sems.at[index])
        copy.start()
        copies.append(copy)
    for copy in copies:
        copy.wait()


def pick_columns(apart, w_query, *extra):
    rows = w_query.shape[0]
    widths = [w_query.shape[1] // GROUP] * len(apart)
    widths[0] += len(extra) * HEAD_SIZE
    return pl.pallas_call(
        functools.partial(pick_columns_kernel, apart, len(extra)),
        out_shape=[jax.ShapeDtypeStruct((rows, width), jnp.bfloat16) for width in widths],
        in_specs=[pl.BlockSpec(memory_space=pl.ANY)] * (1 + len(extra)),
        out_specs=[pl.BlockSpec(memory_space=pltpu.VMEM)] * len(apart),
        scratch_shapes=[pltpu.SemaphoreType.DMA((len(apart) + len(extra),))],
        compiler_params=pltpu.CompilerParams(vmem_limit_bytes=60 * 1024 * 1024),
    )(w_query, *extra)


def split_columns_kernel(widths, *refs):
    *got, first, second, sems = refs
    copies = []
    for index, piece in enumerate(got):
        begin = 0
        for part, out in enumerate((first, second)):
            cols = pl.ds(begin, widths[part])
            copy = pltpu.make_async_copy(
                piece.at[:, cols],
                out.at[:, pl.ds(index * widths[part], widths[part])],
                sems.at[index, part],
            )
            copy.start()
            copies.append(copy)
            begin += widths[part]
    for copy in copies:
        copy.wait()


def split_columns(got, widths):
    rows = got[0].shape[0]
    anywhere = pl.BlockSpec(memory_space=pl.ANY)
    return pl.pallas_call(
        functools.partial(split_columns_kernel, widths),
        out_shape=[
            jax.ShapeDtypeStruct((rows, len(got) * width), jnp.bfloat16) for width in widths
        ],
        in_specs=[anywhere] * len(got),
        out_specs=[anywhere] * 2,
        scratch_shapes=[pltpu.SemaphoreType.DMA((len(got), 2))],
        compiler_params=pltpu.CompilerParams(vmem_limit_bytes=VMEM_LIMIT // 16),
    )(*got)


def project_kernel(planes, first, width, steps, begun, ends, *refs):
    scal, refs = refs[0], refs[1:]
    xs, refs = refs[:4], refs[4:]
    own_w, rest_w, refs = refs[:planes], refs[planes : 2 * planes], refs[2 * planes :]
    so_far, refs = (refs[:GROUP], refs[GROUP:]) if begun else (None, refs)
    cosine, sine, gain, refs = (*refs[:3], refs[3:]) if ends else (None, None, None, refs)
    *outs, w_all, w_sem = refs
    plane, pos, core = scal[0], scal[1], scal[3]
    w_rows = own_w[0].shape[0]
    half = planes // 2
    depth = GROUP * w_rows

    copies = []
    for index, step in enumerate(steps):
        for apart in (step, half + step):
            other = ((plane ^ apart) // half) ^ core
            for r in range(GROUP):
                if r == 0:
                    src = own_w[apart].at[:, pl.ds(first, width)]
                else:
                    src = rest_w[apart].at[:, pl.ds((r - 1) * width, width)]
                row = pl.multiple_of((pos ^ r) * w_rows, w_rows)
                copy = pltpu.make_async_copy(
                    src, w_all.at[index, other, pl.ds(row, w_rows)], w_sem.at[apart, r]
                )
                copy.start()
                copies.append(copy)
    for copy in copies:
        copy.wait()

    rows = outs[0].shape[0]
    for block in range(GROUP):
        part, begin = (0, block * rows) if block < GROUP - 1 else (1, 0)
        result = so_far[block][...] if begun else None
        for index, step in enumerate(steps):
            column = pl.multiple_of(((plane % half) ^ step) * depth, depth)
            for other in range(2):
                term = jnp.dot(
                    xs[2 * other + part][pl.ds(begin, rows), pl.ds(column, depth)],
                    w_all[index, other],
                    preferred_element_type=jnp.float32,
                )
                result = term if result is None else result + term
        if not ends:
            outs[block][...] = result
            continue
        tokens = pl.ds(block * rows, rows)
        for head in range(width // HEAD_SIZE):
            values = result[:, head * HEAD_SIZE : (head + 1) * HEAD_SIZE]
            mean = jnp.mean(values * values, axis=-1, keepdims=True)
            scaled = values * lax.rsqrt(mean + 1e-06) * gain[...]
            turned = (
                scaled * cosine[tokens, :]
                + pltpu.roll(scaled, HEAD_SIZE // 2, 1) * sine[tokens, :]
            )
            outs[block][:, pl.ds(head * HEAD_SIZE, HEAD_SIZE)] = turned.astype(jnp.bfloat16)


def project(scal, xs, own_w, rest_w, first, width, steps, so_far, finish):
    planes = len(own_w)
    rows = xs[1].shape[0]
    depth = GROUP * own_w[0].shape[0]
    out_type = jnp.float32 if finish is None else jnp.bfloat16
    extra = [*(so_far or ()), *(finish or ())]
    anywhere = pl.BlockSpec(memory_space=pl.ANY)
    vmem = pl.BlockSpec(memory_space=pltpu.VMEM)
    return pl.pallas_call(
        functools.partial(
            project_kernel, planes, first, width, steps, so_far is not None, finish is not None
        ),
        out_shape=[jax.ShapeDtypeStruct((rows, width), out_type)] * GROUP,
        in_specs=[pl.BlockSpec(memory_space=pltpu.SMEM)]
        + [vmem] * 4
        + [anywhere] * (2 * planes)
        + [vmem] * len(extra),
        out_specs=[vmem] * GROUP,
        scratch_shapes=[
            pltpu.VMEM((len(steps), 2, depth, width), jnp.bfloat16),
            pltpu.SemaphoreType.DMA((planes, GROUP)),
        ],
        compiler_params=pltpu.CompilerParams(vmem_limit_bytes=VMEM_LIMIT),
        cost_estimate=pl.CostEstimate(
            flops=4 * len(steps) * GROUP * rows * depth * width,
            bytes_accessed=4 * len(steps) * depth * (GROUP * rows + width),
            transcendentals=0,
        ),
    )(scal, *xs, *own_w, *rest_w, *extra)


def project_kv_kernel(planes, skip, *refs):
    scal, refs = refs[0], refs[1:]
    xs, own_w, refs = refs[:2], refs[2 : 2 + planes], refs[2 + planes :]
    *kv_out, x_all, w_all, x_sem, w_sem = refs
    pos = scal[1]
    w_rows = own_w[0].shape[0]
    _, depth, width = w_all.shape
    compact = depth == w_rows
    offset = pos * w_rows if compact else 0

    copies = []
    for apart in range(planes):
        slot = half_slot(scal, planes, apart)
        row = 0
        if not compact:
            w_all[slot] = jnp.zeros((depth, width), jnp.bfloat16)
            row = pl.multiple_of(pos * w_rows, w_rows)
        copy = pltpu.make_async_copy(
            own_w[apart].at[:, pl.ds(skip, width)],
            w_all.at[slot, pl.ds(row, w_rows)],
            w_sem.at[apart],
        )
        copy.start()
        copies.append(copy)
    for slot in range(planes):
        half, within = slot // (planes // 2), slot % (planes // 2)
        column = pl.multiple_of(within * GROUP * w_rows + offset, HEAD_SIZE)
        copy = pltpu.make_async_copy(
            xs[half].at[:, pl.ds(column, depth)], x_all.at[slot], x_sem.at[slot]
        )
        copy.start()
        copies.append(copy)
    for copy in copies:
        copy.wait()
    result = None
    for slot in range(planes):
        term = jnp.dot(x_all[slot], w_all[slot], preferred_element_type=jnp.float32)
        result = term if result is None else result + term
    rows = kv_out[0].shape[0]
    for block, out in enumerate(kv_out):
        part = result[block * rows : (block + 1) * rows]
        if out.dtype == jnp.float32:
            out[...] = part
            continue
        keys = part[:, :HEAD_SIZE]
        high = keys.astype(jnp.bfloat16)
        low = (keys - high.astype(jnp.float32)).astype(jnp.bfloat16)
        out[:, pl.ds(0, HEAD_SIZE)] = high
        out[:, pl.ds(HEAD_SIZE, HEAD_SIZE)] = low
        out[:, pl.ds(2 * HEAD_SIZE, HEAD_SIZE)] = part[:, HEAD_SIZE:].astype(jnp.bfloat16)


def project_kv(scal, xs, own_w, skip, rows, with_own):
    planes = len(own_w)
    tokens = xs[0].shape[0]
    w_rows = own_w[0].shape[0]
    width = own_w[0].shape[1] - skip
    depth = w_rows if w_rows % HEAD_SIZE == 0 else GROUP * w_rows
    sent = jax.ShapeDtypeStruct((rows, 3 * HEAD_SIZE), jnp.bfloat16)
    out_shape = [sent] * (tokens // rows)
    if with_own:
        out_shape[0] = jax.ShapeDtypeStruct((rows, width), jnp.float32)
    anywhere = pl.BlockSpec(memory_space=pl.ANY)
    return pl.pallas_call(
        functools.partial(project_kv_kernel, planes, skip),
        out_shape=out_shape,
        in_specs=[pl.BlockSpec(memory_space=pltpu.SMEM)] + [anywhere] * (2 + planes),
        out_specs=[pl.BlockSpec(memory_space=pltpu.VMEM)] * (tokens // rows),
        scratch_shapes=[
            pltpu.VMEM((planes, tokens, depth), jnp.bfloat16),
            pltpu.VMEM((planes, depth, width), jnp.bfloat16),
            pltpu.SemaphoreType.DMA((planes,)),
            pltpu.SemaphoreType.DMA((planes,)),
        ],
        compiler_params=pltpu.CompilerParams(vmem_limit_bytes=VMEM_LIMIT),
        cost_estimate=pl.CostEstimate(
            flops=2 * tokens * depth * planes * width,
            bytes_accessed=2 * depth * planes * (tokens + width),
            transcendentals=0,
        ),
    )(scal, *xs, *own_w)


def finish_kv_kernel(mine, *refs):
    *others, cosine, sine, gain, keys_out, values_out, both_out = refs
    keys, values = mine[:, :HEAD_SIZE], mine[:, HEAD_SIZE:]
    for other in others:
        high, low, part = (
            other[:, pl.ds(index * HEAD_SIZE, HEAD_SIZE)].astype(jnp.float32) for index in range(3)
        )
        keys = keys + (high + low)
        values = values + part
    mean = jnp.mean(keys * keys, axis=-1, keepdims=True)
    scaled = keys * lax.rsqrt(mean + 1e-06) * gain[...]
    own = pl.ds(0, keys.shape[0])
    turned = scaled * cosine[own, :] + pltpu.roll(scaled, HEAD_SIZE // 2, 1) * sine[own, :]
    keys_out[...] = turned.astype(jnp.bfloat16)
    values_out[...] = values.astype(jnp.bfloat16)
    both_out[0] = keys_out[...]
    turned_values = values.T.astype(jnp.bfloat16)
    for begin in range(0, keys.shape[0], HEAD_SIZE):
        both_out[1, pl.ds(begin, HEAD_SIZE), :] = turned_values[:, begin : begin + HEAD_SIZE]


def finish_kv(parts, cosine, sine, gain):
    rows = parts[0].shape[0]
    one = jax.ShapeDtypeStruct((rows, HEAD_SIZE), jnp.bfloat16)
    vmem = pl.BlockSpec(memory_space=pltpu.VMEM)
    return pl.pallas_call(
        finish_kv_kernel,
        out_shape=[one, one, jax.ShapeDtypeStruct((2, rows, HEAD_SIZE), jnp.bfloat16)],
        in_specs=[vmem] * (len(parts) + 3),
        out_specs=[vmem] * 3,
        compiler_params=pltpu.CompilerParams(vmem_limit_bytes=VMEM_LIMIT // 4),
    )(*parts, cosine, sine, gain)


def attend_kernel(first, width, rows, aliased, *refs):
    scal, order = refs[:2]
    qs = refs[2:6]
    if aliased:
        k_all, vt_all, _, out, *refs = refs[6:]
    else:
        keys_mine, values_mine, theirs, new_mine, new_theirs, out, k_all, vt_all, *refs = refs[6:]
        kv_sem, new_sem, *refs = refs
    q_all, o_all, tops, sums, out_sem = refs
    pos, count = scal[1], scal[2]
    side = pos % 2
    heads = width // HEAD_SIZE
    slots = order.shape[0]
    half_slots = slots // 2
    scale = HEAD_SIZE ** (-0.5) * math.log2(math.e)
    units = GROUP * heads
    lanes = rows

    lead = rows + side * rows

    def new_copies(new, row, index):
        copies = [
            pltpu.make_async_copy(
                new.at[0], k_all.at[pl.ds(row, rows)], new_sem.at[index, 0]
            )
        ]
        for begin in range(0, rows, HEAD_SIZE):
            copies.append(
                pltpu.make_async_copy(
                    new.at[1, pl.ds(begin, HEAD_SIZE)],
                    vt_all.at[pl.ds(0, HEAD_SIZE), pl.ds(row + begin, HEAD_SIZE)],
                    new_sem.at[index, 1 + begin // HEAD_SIZE],
                )
            )
        return copies

    def block_copies(j):
        slot = order[j]
        within = pl.multiple_of((slot % half_slots) * BLOCK_TOKENS, BLOCK_TOKENS)
        dst_row = pl.multiple_of(lead + j * BLOCK_TOKENS, BLOCK_TOKENS)
        near = (slot // half_slots) == side

        def pair(k_src, v_src):
            rows_at = pl.ds(dst_row, BLOCK_TOKENS)
            return (
                pltpu.make_async_copy(k_src, k_all.at[rows_at], kv_sem.at[0, j]),
                pltpu.make_async_copy(
                    v_src, vt_all.at[pl.ds(0, HEAD_SIZE), rows_at], kv_sem.at[1, j]
                ),
            )

        block = pl.ds(within, BLOCK_TOKENS)
        apart = half_slots * BLOCK_TOKENS
        beyond = pl.ds(pl.multiple_of(apart + within, BLOCK_TOKENS), BLOCK_TOKENS)
        there = pl.ds(theirs.shape[0] - BLOCK_TOKENS, BLOCK_TOKENS)
        return (
            near,
            pair(keys_mine.at[block], values_mine.at[:, block]),
            pair(theirs.at[there, block], theirs.at[there, beyond]),
        )

    def start_block(j, carry):
        near, mine, theirs = block_copies(j)

        @pl.when(near)
        def _():
            for copy in mine:
                copy.start()

        @pl.when(jnp.logical_not(near))
        def _():
            for copy in theirs:
                copy.start()

        return carry

    def wait_block(j, carry):
        _, mine, _ = block_copies(j)
        for copy in mine:
            copy.wait()
        return carry

    per_chunk = KEY_CHUNK // BLOCK_TOKENS
    blocks = count + side * (rows // BLOCK_TOKENS)
    full = blocks // per_chunk

    if not aliased:
        for copy in new_copies(new_mine, 0, 0):
            copy.start()

        @pl.when(side == 1)
        def _():
            for copy in new_copies(new_theirs, rows, 1):
                copy.start()

        lax.fori_loop(0, count, start_block, 0)
        vt_all[pl.ds(HEAD_SIZE, ONES), :] = jnp.ones((ONES, vt_all.shape[1]), jnp.bfloat16)

    for r in range(GROUP):
        for head in range(heads):
            q_all[r * heads + head] = qs[r][:, pl.ds(head * HEAD_SIZE, HEAD_SIZE)]

    def absorb(row, size, how, allowed=None):
        keys = k_all[pl.ds(row, size), :]
        values = vt_all[:, pl.ds(row, size)]

        def score(unit):
            return lax.dot_general(
                keys, q_all[unit], (((1,), (1,)), ((), ())), preferred_element_type=jnp.float32
            )

        def some(index, carry):
            begin = index * UNROLL
            ahead = score(begin)
            for step in range(UNROLL):
                unit = begin + step
                s = ahead
                if step + 1 < UNROLL:
                    ahead = score(unit + 1)
                if allowed is not None:
                    s = jnp.where(allowed, s, -1e30)
                top = before = None if how == "first" else tops[unit]
                if how != "same":
                    top = jnp.max(s.reshape(size // 8, 8, lanes), axis=0)
                    top = jnp.max(top, axis=0, keepdims=True)
                    if how == "rising":
                        top = jnp.maximum(before, top)
                    tops[unit] = top
                weight = jnp.exp2((s - top) * scale)
                mixed = jnp.dot(
                    values, weight.astype(jnp.bfloat16), preferred_element_type=jnp.float32
                )
                if how == "first":
                    sums[unit] = mixed
                elif how == "same":
                    sums[unit] += mixed
                else:
                    sums[unit] = sums[unit] * jnp.exp2((before - top) * scale) + mixed
            return carry

        lax.fori_loop(0, units // UNROLL, some, 0)

    def absorb_own():
        key = lax.broadcasted_iota(jnp.int32, (rows, lanes), 0)
        token = lax.broadcasted_iota(jnp.int32, (rows, lanes), 1)
        absorb(0, rows, "first", key <= token)

    def absorb_rest(how):
        def step(chunk, carry):
            row = pl.multiple_of(rows + chunk * KEY_CHUNK, BLOCK_TOKENS)
            absorb(row, KEY_CHUNK, how)
            return carry

        lax.fori_loop(0, full, step, 0)
        part = per_chunk // 2
        while part:
            size = part * BLOCK_TOKENS

            @pl.when((blocks // part) % 2 == 1)
            def _(part=part, size=size):
                row = pl.multiple_of(rows + (blocks // (2 * part)) * 2 * size, BLOCK_TOKENS)
                absorb(row, size, how)

            part //= 2

    if not aliased:
        for copy in new_copies(new_mine, 0, 0):
            copy.wait()
    absorb_own()
    if not aliased:

        @pl.when(side == 1)
        def _():
            for copy in new_copies(new_theirs, rows, 1):
                copy.wait()

        lax.fori_loop(0, count, wait_block, 0)

    absorb_rest("same")
    fits = jnp.max(sums[:, pl.ds(HEAD_SIZE, 8), :]) < 2.0**100

    @pl.when(jnp.logical_not(fits))
    def _():
        absorb_own()
        absorb_rest("rising")

    group_cols = out.shape[1] // GROUP
    copies = []
    for r in range(GROUP):
        for head in range(heads):
            unit = r * heads + head
            total = sums[unit, pl.ds(HEAD_SIZE, 1), :]
            result = (sums[unit, pl.ds(0, HEAD_SIZE), :] / total).T.astype(jnp.bfloat16)
            o_all[r, :, pl.ds(head * HEAD_SIZE, HEAD_SIZE)] = result
        column = pl.multiple_of((pos ^ r) * group_cols + first, HEAD_SIZE)
        copy = pltpu.make_async_copy(
            o_all.at[r], out.at[:, pl.ds(column, width)], out_sem.at[r]
        )
        copy.start()
        copies.append(copy)
    for copy in copies:
        copy.wait()


def attend(scal, order, qs, sources, first, width, out_cols, tokens):
    rows = qs[0].shape[0]
    slots = order.shape[0]
    heads = width // HEAD_SIZE
    units = GROUP * heads
    aliased = len(sources) == 3
    anywhere = pl.BlockSpec(memory_space=pl.ANY)
    vmem = pl.BlockSpec(memory_space=pltpu.VMEM)
    smem = pl.BlockSpec(memory_space=pltpu.SMEM)
    in_specs = [smem] * 2 + [vmem] * 4
    out_shape = [jax.ShapeDtypeStruct((rows, out_cols), jnp.bfloat16)]
    scratch = []
    if aliased:
        in_specs += [vmem, vmem, anywhere]
    else:
        in_specs += [anywhere] * len(sources)
        out_shape += [
            jax.ShapeDtypeStruct((tokens, HEAD_SIZE), jnp.bfloat16),
            jax.ShapeDtypeStruct((HEAD_SIZE + ONES, tokens), jnp.bfloat16),
        ]
        scratch += [
            pltpu.SemaphoreType.DMA((2, slots)),
            pltpu.SemaphoreType.DMA((2, 1 + rows // HEAD_SIZE)),
        ]
    scratch += [
        pltpu.VMEM((units, rows, HEAD_SIZE), jnp.bfloat16),
        pltpu.VMEM((GROUP, rows, width), jnp.bfloat16),
        pltpu.VMEM((units, 1, rows), jnp.float32),
        pltpu.VMEM((units, HEAD_SIZE + ONES, rows), jnp.float32),
        pltpu.SemaphoreType.DMA((GROUP,)),
    ]
    return pl.pallas_call(
        functools.partial(attend_kernel, first, width, rows, aliased),
        out_shape=out_shape,
        in_specs=in_specs,
        out_specs=[anywhere] + [vmem] * (len(out_shape) - 1),
        input_output_aliases={8: 0} if aliased else {},
        scratch_shapes=scratch,
        compiler_params=pltpu.CompilerParams(vmem_limit_bytes=VMEM_LIMIT),
        cost_estimate=pl.CostEstimate(
            flops=4 * units * rows * tokens * HEAD_SIZE,
            bytes_accessed=4 * tokens * HEAD_SIZE,
            transcendentals=units * rows * tokens,
        ),
    )(scal, order, *qs, *sources)


def on_device(
    hidden,
    w_query,
    key_weight,
    value_weight,
    q_gain,
    key_norm_gain,
    earlier_keys,
    earlier_values,
    counts,
    place,
):
    planes = lax.axis_size("ctx") // GROUP
    ctx = lax.axis_index("ctx")
    plane = ctx // GROUP
    pos = ctx % GROUP
    rows = hidden.shape[0]
    w_rows = w_query.shape[0]
    group_cols = w_query.shape[1] // GROUP
    widths = (group_cols // 2, group_cols - group_cols // 2)

    count = lax.dynamic_index_in_dim(counts, ctx // 2, 0, keepdims=False)
    order = lax.dynamic_index_in_dim(place, ctx // 2, 0, keepdims=False)
    scal = jnp.stack([plane, pos, count, lax.axis_index("tp")]).astype(jnp.int32)
    spots = pos ^ jnp.arange(GROUP, dtype=jnp.int32)
    spot_counts = counts[plane * 2 + spots // 2]
    token_position = (
        spot_counts[:, None] * BLOCK_TOKENS
        + (spots % 2)[:, None] * rows
        + jnp.arange(rows, dtype=jnp.int32)[None, :]
    )
    cosine, sine = rope_tables(token_position.reshape(GROUP * rows))
    key_blocks = earlier_keys.reshape(-1, BLOCK_TOKENS, HEAD_SIZE)
    key_blocks = jnp.transpose(key_blocks, (1, 0, 2)).reshape(BLOCK_TOKENS, -1)
    values_turned = earlier_values.T
    cache_mine = jnp.concatenate([key_blocks, values_turned], axis=1)
    across = GROUP * (planes // 2)
    few = rows // 4

    (own,) = pick_columns((0,), w_query, key_weight, value_weight)
    pieces = pick_columns(tuple(range(1, GROUP)), w_query)
    own_far = swap(own, across)
    got = [swap(piece, r) for r, piece in enumerate(pieces, 1)]
    own_near = near(own, planes)
    first, second = split_columns(got, widths)
    hidden, first, second, own_far, cosine, sine, scal, order, cache_mine, values_turned = gate(
        (hidden, first, second, own_far, cosine, sine, scal, order, cache_mine, values_turned),
        own_near,
    )

    x_1, x_2 = swap(hidden, 1), swap(hidden, 2)
    first_far = swap(first, across)
    first_near = near(first, planes)
    own_w = own_near + near(own_far, planes)
    x_1, x_2, second, first_far = gate(
        (x_1, x_2, second, first_far), (*first_near, *own_w[planes // 2 + 1 :])
    )

    message = swap(jnp.concatenate([x_2[:few], cache_mine]), 1)
    x_far = swap(x_1[few:], 2)
    x_near = jnp.concatenate([hidden, x_1, x_2])
    core_near = swap_core(x_near)
    second_far = swap(second, across)
    rest_first = first_near + near(first_far, planes)
    parts = project_kv(scal, (x_near, core_near), own_w, group_cols, rows, True)
    message, x_far, *parts = gate((message, x_far, *parts), ())
    x_3 = jnp.concatenate([message[:few], x_far])
    x_3, second, second_far, *parts = gate(
        (x_3, second, second_far, *parts), rest_first[planes // 2 + 1 :]
    )

    xs = [x_near, x_3, core_near, swap_core(x_3)]
    rest_second = near(second, planes) + near(second_far, planes)

    parts += project_kv(scal, (x_3, xs[3]), own_w, group_cols, rows, False)
    parts = [parts[0]] + [swap(parts[r], r) for r in range(1, GROUP)]
    gain = q_gain[None, :]

    finish = (cosine, sine, gain)
    steps = tuple(range(planes // 2))

    def to_owners(q):
        return [q[0]] + [swap(q[r], r) for r in range(1, GROUP)]

    out_cols = w_query.shape[1]
    q_first = to_owners(
        project(scal, xs, own_w, rest_first, 0, widths[0], steps, None, finish)
    )
    here = list(rest_second)
    for apart in range(planes):
        if apart % (planes // 2):
            here[apart] = rest_second[0]
    begun = project(
        after(scal, q_first[0]), xs, own_w, here, widths[0], widths[1], steps[:1], None, None
    )
    parts[0] = after(parts[0], begun[0])
    keys_mine, values_mine, new_mine = finish_kv(parts, cosine, sine, key_norm_gain[None, :])
    caches = (earlier_keys, values_turned, message)
    news = (new_mine, swap(new_mine, 1))
    q_second = to_owners(
        project(
            after(scal, begun[0], new_mine),
            xs,
            own_w,
            rest_second,
            widths[0],
            widths[1],
            steps[1:],
            begun,
            finish,
        )
    )
    tokens = 2 * rows + place.shape[1] * BLOCK_TOKENS
    attended, all_keys, all_values = attend(
        after(scal, q_second[0]), order, q_first, (*caches, *news), 0, widths[0], out_cols, tokens
    )
    (attended,) = attend(
        scal,
        order,
        q_second,
        (all_keys, all_values, attended),
        widths[0],
        widths[1],
        out_cols,
        tokens,
    )
    return (attended, keys_mine, values_mine)


def solution(mesh):
    placed = (
        P("ctx", "tp"),
        P("ctx", "tp"),
        P("ctx", "tp"),
        P("ctx", "tp"),
        P(),
        P(),
        P("ctx", "tp"),
        P("ctx", "tp"),
        P(),
        P(),
    )
    return jax.shard_map(
        on_device,
        mesh=mesh,
        in_specs=placed,
        out_specs=(P("ctx", "tp"), P("ctx", "tp"), P("ctx", "tp")),
        check_vma=False,
    )
```

```python
import functools
import math

import jax
import jax.numpy as jnp
from jax import lax
from jax.experimental import pallas as pl
from jax.experimental.pallas import tpu as pltpu
from jax.sharding import PartitionSpec as P

HEAD_SIZE = 128
BLOCK_TOKENS = 128
GROUP = 4
KEY_CHUNK = 2048
ONES = 16
UNROLL = 8
VMEM_LIMIT = 16 * 1024 * 1024


def swap(value, mask):
    pairs = [(source, source ^ mask) for source in range(lax.axis_size("ctx"))]
    return lax.ppermute(value, "ctx", pairs)


def swap_core(value):
    return lax.ppermute(value, "tp", [(0, 1), (1, 0)])


def after(value, *others):
    return lax.optimization_barrier((value, *others))[0]


def near(source, planes):
    pieces = [source]
    bit = 1
    while bit < planes // 2:
        pieces = pieces + [swap(piece, GROUP * bit) for piece in pieces]
        bit *= 2
    return pieces


def gate(values, done):
    return lax.optimization_barrier((tuple(values), tuple(done)))[0]


def rope_tables(token_position):
    half = HEAD_SIZE // 2
    freq = jnp.exp(jnp.arange(half, dtype=jnp.float32) * (-2.0 / HEAD_SIZE) * math.log(1000000.0))
    angle = token_position.astype(jnp.float32)[..., None] * freq
    cosine, sine = jnp.cos(angle), jnp.sin(angle)
    return (
        jnp.concatenate([cosine, cosine], axis=-1),
        jnp.concatenate([-sine, sine], axis=-1),
    )


def half_slot(scal, planes, apart):
    there = scal[0] ^ apart
    other = (there // (planes // 2)) ^ scal[3]
    return other * (planes // 2) + there % (planes // 2)


def pick_columns_kernel(apart, count, *refs):
    w_ref, extra, outs, sems = refs[0], refs[1 : 1 + count], refs[1 + count : -1], refs[-1]
    pos = lax.axis_index("ctx") % GROUP
    cols = w_ref.shape[1] // GROUP
    pairs = []
    for r, out in zip(apart, outs):
        begin = pl.multiple_of((pos ^ r) * cols, cols)
        pairs.append((w_ref.at[:, pl.ds(begin, cols)], out.at[:, pl.ds(0, cols)]))
    for index, src in enumerate(extra):
        pairs.append((src, outs[0].at[:, pl.ds(cols + index * HEAD_SIZE, HEAD_SIZE)]))
    copies = []
    for index, (src, dst) in enumerate(pairs):
        copy = pltpu.make_async_copy(src, dst, sems.at[index])
        copy.start()
        copies.append(copy)
    for copy in copies:
        copy.wait()


def pick_columns(apart, w_query, *extra):
    rows = w_query.shape[0]
    widths = [w_query.shape[1] // GROUP] * len(apart)
    widths[0] += len(extra) * HEAD_SIZE
    return pl.pallas_call(
        functools.partial(pick_columns_kernel, apart, len(extra)),
        out_shape=[jax.ShapeDtypeStruct((rows, width), jnp.bfloat16) for width in widths],
        in_specs=[pl.BlockSpec(memory_space=pl.ANY)] * (1 + len(extra)),
        out_specs=[pl.BlockSpec(memory_space=pltpu.VMEM)] * len(apart),
        scratch_shapes=[pltpu.SemaphoreType.DMA((len(apart) + len(extra),))],
        compiler_params=pltpu.CompilerParams(vmem_limit_bytes=60 * 1024 * 1024),
    )(w_query, *extra)


def split_columns_kernel(widths, *refs):
    *got, first, second, sems = refs
    copies = []
    for index, piece in enumerate(got):
        begin = 0
        for part, out in enumerate((first, second)):
            cols = pl.ds(begin, widths[part])
            copy = pltpu.make_async_copy(
                piece.at[:, cols],
                out.at[:, pl.ds(index * widths[part], widths[part])],
                sems.at[index, part],
            )
            copy.start()
            copies.append(copy)
            begin += widths[part]
    for copy in copies:
        copy.wait()


def split_columns(got, widths):
    rows = got[0].shape[0]
    anywhere = pl.BlockSpec(memory_space=pl.ANY)
    return pl.pallas_call(
        functools.partial(split_columns_kernel, widths),
        out_shape=[
            jax.ShapeDtypeStruct((rows, len(got) * width), jnp.bfloat16) for width in widths
        ],
        in_specs=[anywhere] * len(got),
        out_specs=[anywhere] * 2,
        scratch_shapes=[pltpu.SemaphoreType.DMA((len(got), 2))],
        compiler_params=pltpu.CompilerParams(vmem_limit_bytes=VMEM_LIMIT // 16),
    )(*got)


def project_kernel(planes, first, width, steps, begun, ends, *refs):
    scal, refs = refs[0], refs[1:]
    xs, refs = refs[:4], refs[4:]
    own_w, rest_w, refs = refs[:planes], refs[planes : 2 * planes], refs[2 * planes :]
    so_far, refs = (refs[:GROUP], refs[GROUP:]) if begun else (None, refs)
    cosine, sine, gain, refs = (*refs[:3], refs[3:]) if ends else (None, None, None, refs)
    *outs, w_all, w_sem = refs
    plane, pos, core = scal[0], scal[1], scal[3]
    w_rows = own_w[0].shape[0]
    half = planes // 2
    depth = GROUP * w_rows

    copies = []
    for index, step in enumerate(steps):
        for apart in (step, half + step):
            other = ((plane ^ apart) // half) ^ core
            for r in range(GROUP):
                if r == 0:
                    src = own_w[apart].at[:, pl.ds(first, width)]
                else:
                    src = rest_w[apart].at[:, pl.ds((r - 1) * width, width)]
                row = pl.multiple_of((pos ^ r) * w_rows, w_rows)
                copy = pltpu.make_async_copy(
                    src, w_all.at[index, other, pl.ds(row, w_rows)], w_sem.at[apart, r]
                )
                copy.start()
                copies.append(copy)
    for copy in copies:
        copy.wait()

    rows = outs[0].shape[0]
    for block in range(GROUP):
        part, begin = (0, block * rows) if block < GROUP - 1 else (1, 0)
        result = so_far[block][...] if begun else None
        for index, step in enumerate(steps):
            column = pl.multiple_of(((plane % half) ^ step) * depth, depth)
            for other in range(2):
                term = jnp.dot(
                    xs[2 * other + part][pl.ds(begin, rows), pl.ds(column, depth)],
                    w_all[index, other],
                    preferred_element_type=jnp.float32,
                )
                result = term if result is None else result + term
        if not ends:
            outs[block][...] = result
            continue
        tokens = pl.ds(block * rows, rows)
        for head in range(width // HEAD_SIZE):
            values = result[:, head * HEAD_SIZE : (head + 1) * HEAD_SIZE]
            mean = jnp.mean(values * values, axis=-1, keepdims=True)
            scaled = values * lax.rsqrt(mean + 1e-06) * gain[...]
            turned = (
                scaled * cosine[tokens, :]
                + pltpu.roll(scaled, HEAD_SIZE // 2, 1) * sine[tokens, :]
            )
            outs[block][:, pl.ds(head * HEAD_SIZE, HEAD_SIZE)] = turned.astype(jnp.bfloat16)


def project(scal, xs, own_w, rest_w, first, width, steps, so_far, finish):
    planes = len(own_w)
    rows = xs[1].shape[0]
    depth = GROUP * own_w[0].shape[0]
    out_type = jnp.float32 if finish is None else jnp.bfloat16
    extra = [*(so_far or ()), *(finish or ())]
    anywhere = pl.BlockSpec(memory_space=pl.ANY)
    vmem = pl.BlockSpec(memory_space=pltpu.VMEM)
    return pl.pallas_call(
        functools.partial(
            project_kernel, planes, first, width, steps, so_far is not None, finish is not None
        ),
        out_shape=[jax.ShapeDtypeStruct((rows, width), out_type)] * GROUP,
        in_specs=[pl.BlockSpec(memory_space=pltpu.SMEM)]
        + [vmem] * 4
        + [anywhere] * (2 * planes)
        + [vmem] * len(extra),
        out_specs=[vmem] * GROUP,
        scratch_shapes=[
            pltpu.VMEM((len(steps), 2, depth, width), jnp.bfloat16),
            pltpu.SemaphoreType.DMA((planes, GROUP)),
        ],
        compiler_params=pltpu.CompilerParams(vmem_limit_bytes=VMEM_LIMIT),
        cost_estimate=pl.CostEstimate(
            flops=4 * len(steps) * GROUP * rows * depth * width,
            bytes_accessed=4 * len(steps) * depth * (GROUP * rows + width),
            transcendentals=0,
        ),
    )(scal, *xs, *own_w, *rest_w, *extra)


def project_kv_kernel(planes, skip, *refs):
    scal, refs = refs[0], refs[1:]
    xs, own_w, refs = refs[:2], refs[2 : 2 + planes], refs[2 + planes :]
    *kv_out, x_all, w_all, x_sem, w_sem = refs
    pos = scal[1]
    w_rows = own_w[0].shape[0]
    _, depth, width = w_all.shape
    compact = depth == w_rows
    offset = pos * w_rows if compact else 0

    copies = []
    for apart in range(planes):
        slot = half_slot(scal, planes, apart)
        row = 0
        if not compact:
            w_all[slot] = jnp.zeros((depth, width), jnp.bfloat16)
            row = pl.multiple_of(pos * w_rows, w_rows)
        copy = pltpu.make_async_copy(
            own_w[apart].at[:, pl.ds(skip, width)],
            w_all.at[slot, pl.ds(row, w_rows)],
            w_sem.at[apart],
        )
        copy.start()
        copies.append(copy)
    for slot in range(planes):
        half, within = slot // (planes // 2), slot % (planes // 2)
        column = pl.multiple_of(within * GROUP * w_rows + offset, HEAD_SIZE)
        copy = pltpu.make_async_copy(
            xs[half].at[:, pl.ds(column, depth)], x_all.at[slot], x_sem.at[slot]
        )
        copy.start()
        copies.append(copy)
    for copy in copies:
        copy.wait()
    result = None
    for slot in range(planes):
        term = jnp.dot(x_all[slot], w_all[slot], preferred_element_type=jnp.float32)
        result = term if result is None else result + term
    rows = kv_out[0].shape[0]
    for block, out in enumerate(kv_out):
        part = result[block * rows : (block + 1) * rows]
        if out.dtype == jnp.float32:
            out[...] = part
            continue
        keys = part[:, :HEAD_SIZE]
        high = keys.astype(jnp.bfloat16)
        low = (keys - high.astype(jnp.float32)).astype(jnp.bfloat16)
        out[:, pl.ds(0, HEAD_SIZE)] = high
        out[:, pl.ds(HEAD_SIZE, HEAD_SIZE)] = low
        out[:, pl.ds(2 * HEAD_SIZE, HEAD_SIZE)] = part[:, HEAD_SIZE:].astype(jnp.bfloat16)


def project_kv(scal, xs, own_w, skip, rows, with_own):
    planes = len(own_w)
    tokens = xs[0].shape[0]
    w_rows = own_w[0].shape[0]
    width = own_w[0].shape[1] - skip
    depth = w_rows if w_rows % HEAD_SIZE == 0 else GROUP * w_rows
    sent = jax.ShapeDtypeStruct((rows, 3 * HEAD_SIZE), jnp.bfloat16)
    out_shape = [sent] * (tokens // rows)
    if with_own:
        out_shape[0] = jax.ShapeDtypeStruct((rows, width), jnp.float32)
    anywhere = pl.BlockSpec(memory_space=pl.ANY)
    return pl.pallas_call(
        functools.partial(project_kv_kernel, planes, skip),
        out_shape=out_shape,
        in_specs=[pl.BlockSpec(memory_space=pltpu.SMEM)] + [anywhere] * (2 + planes),
        out_specs=[pl.BlockSpec(memory_space=pltpu.VMEM)] * (tokens // rows),
        scratch_shapes=[
            pltpu.VMEM((planes, tokens, depth), jnp.bfloat16),
            pltpu.VMEM((planes, depth, width), jnp.bfloat16),
            pltpu.SemaphoreType.DMA((planes,)),
            pltpu.SemaphoreType.DMA((planes,)),
        ],
        compiler_params=pltpu.CompilerParams(vmem_limit_bytes=VMEM_LIMIT),
        cost_estimate=pl.CostEstimate(
            flops=2 * tokens * depth * planes * width,
            bytes_accessed=2 * depth * planes * (tokens + width),
            transcendentals=0,
        ),
    )(scal, *xs, *own_w)


def finish_kv_kernel(mine, *refs):
    *others, cosine, sine, gain, keys_out, values_out, both_out = refs
    keys, values = mine[:, :HEAD_SIZE], mine[:, HEAD_SIZE:]
    for other in others:
        high, low, part = (
            other[:, pl.ds(index * HEAD_SIZE, HEAD_SIZE)].astype(jnp.float32) for index in range(3)
        )
        keys = keys + (high + low)
        values = values + part
    mean = jnp.mean(keys * keys, axis=-1, keepdims=True)
    scaled = keys * lax.rsqrt(mean + 1e-06) * gain[...]
    own = pl.ds(0, keys.shape[0])
    turned = scaled * cosine[own, :] + pltpu.roll(scaled, HEAD_SIZE // 2, 1) * sine[own, :]
    keys_out[...] = turned.astype(jnp.bfloat16)
    values_out[...] = values.astype(jnp.bfloat16)
    both_out[0] = keys_out[...]
    turned_values = values.T.astype(jnp.bfloat16)
    for begin in range(0, keys.shape[0], HEAD_SIZE):
        both_out[1, pl.ds(begin, HEAD_SIZE), :] = turned_values[:, begin : begin + HEAD_SIZE]


def finish_kv(parts, cosine, sine, gain):
    rows = parts[0].shape[0]
    one = jax.ShapeDtypeStruct((rows, HEAD_SIZE), jnp.bfloat16)
    vmem = pl.BlockSpec(memory_space=pltpu.VMEM)
    return pl.pallas_call(
        finish_kv_kernel,
        out_shape=[one, one, jax.ShapeDtypeStruct((2, rows, HEAD_SIZE), jnp.bfloat16)],
        in_specs=[vmem] * (len(parts) + 3),
        out_specs=[vmem] * 3,
        compiler_params=pltpu.CompilerParams(vmem_limit_bytes=VMEM_LIMIT // 4),
    )(*parts, cosine, sine, gain)


def attend_kernel(first, width, rows, aliased, *refs):
    scal, order = refs[:2]
    qs = refs[2:6]
    if aliased:
        k_all, vt_all, _, out, *refs = refs[6:]
    else:
        keys_mine, values_mine, theirs, new_mine, new_theirs, out, k_all, vt_all, *refs = refs[6:]
        kv_sem, new_sem, *refs = refs
    q_all, o_all, tops, sums, out_sem = refs
    pos, count = scal[1], scal[2]
    side = pos % 2
    heads = width // HEAD_SIZE
    slots = order.shape[0]
    half_slots = slots // 2
    scale = HEAD_SIZE ** (-0.5) * math.log2(math.e)
    units = GROUP * heads
    lanes = rows

    lead = rows + side * rows

    def new_copies(new, row, index):
        copies = [
            pltpu.make_async_copy(
                new.at[0], k_all.at[pl.ds(row, rows)], new_sem.at[index, 0]
            )
        ]
        for begin in range(0, rows, HEAD_SIZE):
            copies.append(
                pltpu.make_async_copy(
                    new.at[1, pl.ds(begin, HEAD_SIZE)],
                    vt_all.at[pl.ds(0, HEAD_SIZE), pl.ds(row + begin, HEAD_SIZE)],
                    new_sem.at[index, 1 + begin // HEAD_SIZE],
                )
            )
        return copies

    def block_copies(j):
        slot = order[j]
        within = pl.multiple_of((slot % half_slots) * BLOCK_TOKENS, BLOCK_TOKENS)
        dst_row = pl.multiple_of(lead + j * BLOCK_TOKENS, BLOCK_TOKENS)
        near = (slot // half_slots) == side

        def pair(k_src, v_src):
            rows_at = pl.ds(dst_row, BLOCK_TOKENS)
            return (
                pltpu.make_async_copy(k_src, k_all.at[rows_at], kv_sem.at[0, j]),
                pltpu.make_async_copy(
                    v_src, vt_all.at[pl.ds(0, HEAD_SIZE), rows_at], kv_sem.at[1, j]
                ),
            )

        block = pl.ds(within, BLOCK_TOKENS)
        apart = half_slots * BLOCK_TOKENS
        beyond = pl.ds(pl.multiple_of(apart + within, BLOCK_TOKENS), BLOCK_TOKENS)
        there = pl.ds(theirs.shape[0] - BLOCK_TOKENS, BLOCK_TOKENS)
        return (
            near,
            pair(keys_mine.at[block], values_mine.at[:, block]),
            pair(theirs.at[there, block], theirs.at[there, beyond]),
        )

    def start_block(j, carry):
        near, mine, theirs = block_copies(j)

        @pl.when(near)
        def _():
            for copy in mine:
                copy.start()

        @pl.when(jnp.logical_not(near))
        def _():
            for copy in theirs:
                copy.start()

        return carry

    def wait_block(j, carry):
        _, mine, _ = block_copies(j)
        for copy in mine:
            copy.wait()
        return carry

    per_chunk = KEY_CHUNK // BLOCK_TOKENS
    blocks = count + side * (rows // BLOCK_TOKENS)
    full = blocks // per_chunk

    if not aliased:
        for copy in new_copies(new_mine, 0, 0):
            copy.start()

        @pl.when(side == 1)
        def _():
            for copy in new_copies(new_theirs, rows, 1):
                copy.start()

        lax.fori_loop(0, count, start_block, 0)
        vt_all[pl.ds(HEAD_SIZE, ONES), :] = jnp.ones((ONES, vt_all.shape[1]), jnp.bfloat16)

    for r in range(GROUP):
        for head in range(heads):
            q_all[r * heads + head] = qs[r][:, pl.ds(head * HEAD_SIZE, HEAD_SIZE)]

    def absorb(row, size, how, allowed=None):
        keys = k_all[pl.ds(row, size), :]
        values = vt_all[:, pl.ds(row, size)]

        def score(unit):
            return lax.dot_general(
                keys, q_all[unit], (((1,), (1,)), ((), ())), preferred_element_type=jnp.float32
            )

        def some(index, carry):
            begin = index * UNROLL
            ahead = score(begin)
            for step in range(UNROLL):
                unit = begin + step
                s = ahead
                if step + 1 < UNROLL:
                    ahead = score(unit + 1)
                if allowed is not None:
                    s = jnp.where(allowed, s, -1e30)
                top = before = None if how == "first" else tops[unit]
                if how != "same":
                    top = jnp.max(s.reshape(size // 8, 8, lanes), axis=0)
                    top = jnp.max(top, axis=0, keepdims=True)
                    if how == "rising":
                        top = jnp.maximum(before, top)
                    tops[unit] = top
                weight = jnp.exp2((s - top) * scale)
                mixed = jnp.dot(
                    values, weight.astype(jnp.bfloat16), preferred_element_type=jnp.float32
                )
                if how == "first":
                    sums[unit] = mixed
                elif how == "same":
                    sums[unit] += mixed
                else:
                    sums[unit] = sums[unit] * jnp.exp2((before - top) * scale) + mixed
            return carry

        lax.fori_loop(0, units // UNROLL, some, 0)

    def absorb_own():
        key = lax.broadcasted_iota(jnp.int32, (rows, lanes), 0)
        token = lax.broadcasted_iota(jnp.int32, (rows, lanes), 1)
        absorb(0, rows, "first", key <= token)

    def absorb_rest(how):
        def step(chunk, carry):
            row = pl.multiple_of(rows + chunk * KEY_CHUNK, BLOCK_TOKENS)
            absorb(row, KEY_CHUNK, how)
            return carry

        lax.fori_loop(0, full, step, 0)
        part = per_chunk // 2
        while part:
            size = part * BLOCK_TOKENS

            @pl.when((blocks // part) % 2 == 1)
            def _(part=part, size=size):
                row = pl.multiple_of(rows + (blocks // (2 * part)) * 2 * size, BLOCK_TOKENS)
                absorb(row, size, how)

            part //= 2

    if not aliased:
        for copy in new_copies(new_mine, 0, 0):
            copy.wait()
    absorb_own()
    if not aliased:

        @pl.when(side == 1)
        def _():
            for copy in new_copies(new_theirs, rows, 1):
                copy.wait()

        lax.fori_loop(0, count, wait_block, 0)

    absorb_rest("same")
    fits = jnp.max(sums[:, pl.ds(HEAD_SIZE, 8), :]) < 2.0**100

    @pl.when(jnp.logical_not(fits))
    def _():
        absorb_own()
        absorb_rest("rising")

    group_cols = out.shape[1] // GROUP
    copies = []
    for r in range(GROUP):
        for head in range(heads):
            unit = r * heads + head
            total = sums[unit, pl.ds(HEAD_SIZE, 1), :]
            result = (sums[unit, pl.ds(0, HEAD_SIZE), :] / total).T.astype(jnp.bfloat16)
            o_all[r, :, pl.ds(head * HEAD_SIZE, HEAD_SIZE)] = result
        column = pl.multiple_of((pos ^ r) * group_cols + first, HEAD_SIZE)
        copy = pltpu.make_async_copy(
            o_all.at[r], out.at[:, pl.ds(column, width)], out_sem.at[r]
        )
        copy.start()
        copies.append(copy)
    for copy in copies:
        copy.wait()


def attend(scal, order, qs, sources, first, width, out_cols, tokens):
    rows = qs[0].shape[0]
    slots = order.shape[0]
    heads = width // HEAD_SIZE
    units = GROUP * heads
    aliased = len(sources) == 3
    anywhere = pl.BlockSpec(memory_space=pl.ANY)
    vmem = pl.BlockSpec(memory_space=pltpu.VMEM)
    smem = pl.BlockSpec(memory_space=pltpu.SMEM)
    in_specs = [smem] * 2 + [vmem] * 4
    out_shape = [jax.ShapeDtypeStruct((rows, out_cols), jnp.bfloat16)]
    scratch = []
    if aliased:
        in_specs += [vmem, vmem, anywhere]
    else:
        in_specs += [anywhere] * len(sources)
        out_shape += [
            jax.ShapeDtypeStruct((tokens, HEAD_SIZE), jnp.bfloat16),
            jax.ShapeDtypeStruct((HEAD_SIZE + ONES, tokens), jnp.bfloat16),
        ]
        scratch += [
            pltpu.SemaphoreType.DMA((2, slots)),
            pltpu.SemaphoreType.DMA((2, 1 + rows // HEAD_SIZE)),
        ]
    scratch += [
        pltpu.VMEM((units, rows, HEAD_SIZE), jnp.bfloat16),
        pltpu.VMEM((GROUP, rows, width), jnp.bfloat16),
        pltpu.VMEM((units, 1, rows), jnp.float32),
        pltpu.VMEM((units, HEAD_SIZE + ONES, rows), jnp.float32),
        pltpu.SemaphoreType.DMA((GROUP,)),
    ]
    return pl.pallas_call(
        functools.partial(attend_kernel, first, width, rows, aliased),
        out_shape=out_shape,
        in_specs=in_specs,
        out_specs=[anywhere] + [vmem] * (len(out_shape) - 1),
        input_output_aliases={8: 0} if aliased else {},
        scratch_shapes=scratch,
        compiler_params=pltpu.CompilerParams(vmem_limit_bytes=VMEM_LIMIT),
        cost_estimate=pl.CostEstimate(
            flops=4 * units * rows * tokens * HEAD_SIZE,
            bytes_accessed=4 * tokens * HEAD_SIZE,
            transcendentals=units * rows * tokens,
        ),
    )(scal, order, *qs, *sources)


def on_device(
    hidden,
    w_query,
    key_weight,
    value_weight,
    q_gain,
    key_norm_gain,
    earlier_keys,
    earlier_values,
    counts,
    place,
):
    planes = lax.axis_size("ctx") // GROUP
    ctx = lax.axis_index("ctx")
    plane = ctx // GROUP
    pos = ctx % GROUP
    rows = hidden.shape[0]
    w_rows = w_query.shape[0]
    group_cols = w_query.shape[1] // GROUP
    widths = (group_cols // 2, group_cols - group_cols // 2)

    count = lax.dynamic_index_in_dim(counts, ctx // 2, 0, keepdims=False)
    order = lax.dynamic_index_in_dim(place, ctx // 2, 0, keepdims=False)
    scal = jnp.stack([plane, pos, count, lax.axis_index("tp")]).astype(jnp.int32)
    spots = pos ^ jnp.arange(GROUP, dtype=jnp.int32)
    spot_counts = counts[plane * 2 + spots // 2]
    token_position = (
        spot_counts[:, None] * BLOCK_TOKENS
        + (spots % 2)[:, None] * rows
        + jnp.arange(rows, dtype=jnp.int32)[None, :]
    )
    cosine, sine = rope_tables(token_position.reshape(GROUP * rows))
    key_blocks = earlier_keys.reshape(-1, BLOCK_TOKENS, HEAD_SIZE)
    key_blocks = jnp.transpose(key_blocks, (1, 0, 2)).reshape(BLOCK_TOKENS, -1)
    values_turned = earlier_values.T
    cache_mine = jnp.concatenate([key_blocks, values_turned], axis=1)
    across = GROUP * (planes // 2)
    few = rows // 4

    (own,) = pick_columns((0,), w_query, key_weight, value_weight)
    pieces = pick_columns(tuple(range(1, GROUP)), w_query)
    own_far = swap(own, across)
    got = [swap(piece, r) for r, piece in enumerate(pieces, 1)]
    own_near = near(own, planes)
    first, second = split_columns(got, widths)
    hidden, first, second, own_far, cosine, sine, scal, order, cache_mine, values_turned = gate(
        (hidden, first, second, own_far, cosine, sine, scal, order, cache_mine, values_turned),
        own_near,
    )

    x_1, x_2 = swap(hidden, 1), swap(hidden, 2)
    first_far = swap(first, across)
    first_near = near(first, planes)
    own_w = own_near + near(own_far, planes)
    x_1, x_2, second, first_far = gate(
        (x_1, x_2, second, first_far), (*first_near, *own_w[planes // 2 + 1 :])
    )

    message = swap(jnp.concatenate([x_2[:few], cache_mine]), 1)
    x_far = swap(x_1[few:], 2)
    x_near = jnp.concatenate([hidden, x_1, x_2])
    core_near = swap_core(x_near)
    second_far = swap(second, across)
    rest_first = first_near + near(first_far, planes)
    parts = project_kv(scal, (x_near, core_near), own_w, group_cols, rows, True)
    message, x_far, *parts = gate((message, x_far, *parts), ())
    x_3 = jnp.concatenate([message[:few], x_far])
    x_3, second, second_far, *parts = gate(
        (x_3, second, second_far, *parts), rest_first[planes // 2 + 1 :]
    )

    xs = [x_near, x_3, core_near, swap_core(x_3)]
    rest_second = near(second, planes) + near(second_far, planes)

    parts += project_kv(scal, (x_3, xs[3]), own_w, group_cols, rows, False)
    parts = [parts[0]] + [swap(parts[r], r) for r in range(1, GROUP)]
    gain = q_gain[None, :]

    finish = (cosine, sine, gain)
    steps = tuple(range(planes // 2))

    def to_owners(q):
        return [q[0]] + [swap(q[r], r) for r in range(1, GROUP)]

    out_cols = w_query.shape[1]
    q_first = to_owners(
        project(scal, xs, own_w, rest_first, 0, widths[0], steps, None, finish)
    )
    here = list(rest_second)
    for apart in range(planes):
        if apart % (planes // 2):
            here[apart] = rest_second[0]
    begun = project(
        after(scal, q_first[0]), xs, own_w, here, widths[0], widths[1], steps[:1], None, None
    )
    parts[0] = after(parts[0], begun[0])
    keys_mine, values_mine, new_mine = finish_kv(parts, cosine, sine, key_norm_gain[None, :])
    caches = (earlier_keys, values_turned, message)
    news = (new_mine, swap(new_mine, 1))
    q_second = to_owners(
        project(
            after(scal, begun[0], new_mine),
            xs,
            own_w,
            rest_second,
            widths[0],
            widths[1],
            steps[1:],
            begun,
            finish,
        )
    )
    tokens = 2 * rows + place.shape[1] * BLOCK_TOKENS
    attended, all_keys, all_values = attend(
        after(scal, q_second[0]), order, q_first, (*caches, *news), 0, widths[0], out_cols, tokens
    )
    (attended,) = attend(
        scal,
        order,
        q_second,
        (all_keys, all_values, attended),
        widths[0],
        widths[1],
        out_cols,
        tokens,
    )
    return (attended, keys_mine, values_mine)


def solution(mesh):
    placed = (
        P("ctx", "tp"),
        P("ctx", "tp"),
        P("ctx", "tp"),
        P("ctx", "tp"),
        P(),
        P(),
        P("ctx", "tp"),
        P("ctx", "tp"),
        P(),
        P(),
    )
    return jax.shard_map(
        on_device,
        mesh=mesh,
        in_specs=placed,
        out_specs=(P("ctx", "tp"), P("ctx", "tp"), P("ctx", "tp")),
        check_vma=False,
    )
```
